32 devices in a mesh: section: 2 (over core), dp: 4 (over y, x), head: 4 (over z).
Axes of the slice: x: 2, y: 2, z: 4, core: 2. Of those that a mesh axis runs over, the one named last changes fastest.
Arguments:
- hidden_in: bfloat16 [8, 2048, 1024], P('dp', 'head'), may hold values from -6 to 6
- lengths: int32 [8, 16], P('dp'), may hold values from 0 to 2048, as said below
- w_query: bfloat16 [2, 1024, 1024], P('section', None, 'head'), may hold values from -0.1875 to 0.1875
- w_key: bfloat16 [2, 1024, 1024], P('section', None, 'head'), may hold values from -0.1875 to 0.1875
- w_value: bfloat16 [2, 1024, 1024], P('section', None, 'head'), may hold values from -0.1875 to 0.1875
- w_out: bfloat16 [2, 1024, 1024], P('section', 'head'), may hold values from -3 to 3
- w_gate: bfloat16 [2, 1024, 2816], P('section', None, 'head'), may hold values from -0.1875 to 0.1875
- w_up: bfloat16 [2, 1024, 2816], P('section', None, 'head'), may hold values from -0.1875 to 0.1875
- w_down: bfloat16 [2, 2816, 1024], P('section', 'head'), may hold values from -0.109375 to 0.109375
- attn_gain: float32 [2, 1024], P('section'), may hold values from 0.5 to 1.5
- ffn_gain: float32 [2, 1024], P('section'), may hold values from 0.5 to 1.5
- cotangent: float32 [8, 2048, 1024], P('dp', 'head'), may hold values from -6 to 6
Outputs:
- layer_outputs: bfloat16 [2, 8, 2048, 1024], P('section', 'dp', 'head')
- input_grads: float32 [2, 8, 2048, 1024], P('section', 'dp', 'head')
- grad_query: float32 [2, 1024, 1024], P('section', None, 'head')
- grad_key: float32 [2, 1024, 1024], P('section', None, 'head')
- grad_value: float32 [2, 1024, 1024], P('section', None, 'head')
- grad_out: float32 [2, 1024, 1024], P('section', 'head')
- grad_gate: float32 [2, 1024, 2816], P('section', None, 'head')
- grad_up: float32 [2, 1024, 2816], P('section', None, 'head')
- grad_down: float32 [2, 2816, 1024], P('section', 'head')
- grad_attn_gain: float32 [2, 1024], P('section')
- grad_ffn_gain: float32 [2, 1024], P('section')
The draws below stay inside these ranges and needn't reach their ends.
Inputs may be any that keep to these rules, and one draw needn't show every extreme that they name: Each row lists the lengths of its sequences in slot order, then zeros; every nonzero length is 128 or more; rounded up to multiples of 128, a row's lengths fill exactly 2048 slots.
All inputs are finite; a program needn't handle non-finite values.
Results may differ from the reference program's by a relative error of at most 0.038.
Values may be sent and summed in bfloat16 or wider, within the bound.
No kernel may reach another device: no remote copies, remote signals or barrier semaphores. Data moves between devices by JAX's collectives and lax.ppermute only.
A program may use at most 512 MiB of HBM per device.

```python
import jax
import jax.numpy as jnp
from jax import lax

D = 1024
HD = 64
FF = 2816
SLOTS = 2048
PAD = 128
ROWS = 8


def draw_lengths(key, part):
    key = jax.random.fold_in(key, 7)
    blocks = SLOTS // PAD
    cut_key, long_key, row_key, place_key, trim_key = jax.random.split(key, 5)
    index = jnp.arange(blocks, dtype=jnp.int32)
    rows = jnp.arange(ROWS, dtype=jnp.int32)
    whole_row = jax.random.randint(row_key, (), 0, ROWS, dtype=jnp.int32)
    longest = jax.random.randint(long_key, (ROWS,), blocks // 2, blocks + 1, dtype=jnp.int32)
    longest = jnp.where(rows == whole_row, blocks, longest)
    first = jax.random.randint(place_key, (ROWS,), 0, blocks - longest + 1, dtype=jnp.int32)
    cuts = jax.random.randint(cut_key, (ROWS, blocks), 0, 20, dtype=jnp.int32) < 7
    inner = (index[None, :] > first[:, None]) & (index[None, :] < (first + longest)[:, None])
    flags = cuts & ~inner | (index[None, :] == first[:, None]) | (index[None, :] == (first + longest)[:, None]) | (index[None, :] == 0)
    doc_of_block = (jnp.cumsum(flags.astype(jnp.int32), axis=1) - 1).astype(jnp.int32)
    counts = jnp.sum((doc_of_block[:, :, None] == index[None, None, :]).astype(jnp.int32), axis=1)
    trim = jax.random.randint(trim_key, (ROWS, blocks), 0, PAD, dtype=jnp.int32)
    trim = jnp.where(rows[:, None] == whole_row, 0, trim)
    return jnp.where(counts > 1, counts * PAD - trim, counts * PAD).astype(jnp.int32)


def steps_of(rng, shape, cuts, low, top_value):
    def one(dim, shards_of):
        draws = jax.random.uniform(jax.random.fold_in(jax.random.fold_in(rng, 6), dim), (shards_of,), jnp.float32, low / len(cuts), top_value / len(cuts))
        return jnp.repeat(jnp.exp(draws), shape[dim] // shards_of).reshape((-1,) + (1,) * (len(shape) - dim - 1))

    factor_of = one(*cuts[0])
    for cut in cuts[1:]:
        factor_of = factor_of * one(*cut)
    return factor_of


def gaussian(stream_key, dims, width, bound, pieces=(), kind=jnp.bfloat16):
    array = jax.random.normal(stream_key, dims, jnp.float32) * width
    if len(pieces) > 0:
        array = steps_of(stream_key, dims, pieces, -0.22, 0.18) * array
    return jnp.clip(array, min=-bound, max=bound).astype(kind)


def setup_inputs(seed: int = 0) -> dict:
    streams_of = jax.random.split(jax.random.key(seed), 13)
    return {
        "hidden_in": gaussian(streams_of[0], (ROWS, SLOTS, D), 1.0, 6.0, ((0, 4), (1, 4))),
        "lengths": draw_lengths(jax.random.fold_in(streams_of[12], 71), 0),
        "w_query": gaussian(streams_of[2], (2, D, D), D ** -0.5, 0.1875, ((0, 2), (2, 4))),
        "w_key": gaussian(streams_of[3], (2, D, D), D ** -0.5, 0.1875, ((0, 2), (2, 4))),
        "w_value": gaussian(streams_of[4], (2, D, D), D ** -0.5, 0.1875, ((0, 2), (2, 4))),
        "w_out": gaussian(streams_of[5], (2, D, D), (max(4, D // 256)) ** -0.5, 3.0, ((0, 2), (1, 4))),
        "w_gate": gaussian(streams_of[6], (2, D, FF), D ** -0.5, 0.1875, ((0, 2), (2, 4))),
        "w_up": gaussian(streams_of[7], (2, D, FF), D ** -0.5, 0.1875, ((0, 2), (2, 4))),
        "w_down": gaussian(streams_of[8], (2, FF, D), FF ** -0.5, 0.109375, ((0, 2), (1, 4))),
        "attn_gain": jnp.clip(1.0 + 0.1 * jax.random.normal(streams_of[9], (2, D), jnp.float32), 0.5, 1.5),
        "ffn_gain": jnp.clip(1.0 + 0.1 * jax.random.normal(streams_of[10], (2, D), jnp.float32), 0.5, 1.5),
        "cotangent": gaussian(streams_of[11], (ROWS, SLOTS, D), 1.0, 6.0, ((0, 4), (1, 4)), jnp.float32),
    }


EPSILON = 1e-05
MASKED = -1e+30

@jax.custom_vjp
def low(v):
    return lax.optimization_barrier(v.astype(jnp.bfloat16)).astype(jnp.float32)

@jax.custom_vjp
def low_back(v):
    return v

def low_keep(v):
    return (low(v), None)

def low_pass(kept, grad):
    return (grad,)

def back_keep(v):
    return (v, None)

def back_low(kept, grad):
    return (low(grad),)
low.defvjp(low_keep, low_pass)
low_back.defvjp(back_keep, back_low)

def product(left, right):
    return jnp.dot(left, right, precision=lax.Precision.HIGHEST)

def rms_norm(rows, gain):
    inverse = lax.rsqrt(lax.optimization_barrier(jnp.mean(rows * rows, axis=-1, keepdims=True)) + EPSILON)
    return rows * inverse * gain

def slot_tables(length_row):
    padded = (length_row + PAD - 1) // PAD * PAD
    starts = (jnp.cumsum(padded) - padded).astype(jnp.int32)
    slots = jnp.arange(SLOTS, dtype=jnp.int32)
    docs = jnp.arange(length_row.shape[0], dtype=jnp.int32)
    inside = (slots[:, None] >= starts[None, :]) & (slots[:, None] < (starts + padded)[None, :])
    segment = lax.optimization_barrier(jnp.sum(jnp.where(inside, docs[None, :], 0), axis=1)).astype(jnp.int32)
    begin = lax.optimization_barrier(jnp.sum(jnp.where(inside, starts[None, :], 0), axis=1)).astype(jnp.int32)
    live = lax.optimization_barrier(jnp.sum(jnp.where(inside & (slots[:, None] < (starts + length_row)[None, :]), 1, 0), axis=1)) > 0
    freq = 10000.0 ** (-2.0 * jnp.arange(HD // 2, dtype=jnp.float32) / HD)
    angle = (slots - begin).astype(jnp.float32)[:, None] * freq[None, :]
    cosine = jnp.concatenate([jnp.cos(angle), jnp.cos(angle)], axis=1)
    sine = jnp.concatenate([jnp.sin(angle), jnp.sin(angle)], axis=1)
    return (segment, live, cosine, sine)

def rotary(rows, cosine, sine):
    shaped = rows.reshape(rows.shape[0], -1, HD)
    half = HD // 2
    turned = jnp.concatenate([-shaped[..., half:], shaped[..., :half]], axis=2)
    return (shaped * cosine[:, None, :] + turned * sine[:, None, :]).reshape(rows.shape)

def attention(queries, keyset, values, segment, live):
    total = queries.shape[0]
    block = min(512, total)
    heads = queries.shape[1] // HD
    query_blocks = queries.reshape(total // block, block, heads, HD)
    key_heads = keyset.reshape(total, heads, HD)
    value_heads = values.reshape(total, heads, HD)
    starts = (jnp.arange(total // block) * block).astype(jnp.int32)
    positions = jnp.arange(total, dtype=jnp.int32)

    def block_out(pair):
        query_block, start = pair
        rows = start + jnp.arange(block, dtype=jnp.int32)
        scores = jnp.einsum('qhd,khd->hqk', query_block, key_heads, precision=lax.Precision.HIGHEST) * HD ** (-0.5)
        scores = low_back(scores)
        own_segment = lax.dynamic_slice_in_dim(segment, start, block)
        allowed = (own_segment[:, None] == segment[None, :]) & (positions[None, :] <= rows[:, None]) & live[None, :]
        scores = jnp.where(allowed[None], scores, MASKED)
        probs = low(jax.nn.softmax(scores, axis=2))
        return jnp.einsum('hqk,khd->qhd', probs, value_heads, precision=lax.Precision.HIGHEST)
    return lax.map(jax.checkpoint(block_out), (query_blocks, starts)).reshape(total, heads * HD)

def layer(rows, first_values, weights, tables):
    w_query, w_key, w_value, w_out, w_gate, w_up, w_down, attn_gain, ffn_gain = weights
    segment, live, cosine, sine = tables
    normed = low(rms_norm(rows, attn_gain))
    queries = low(rotary(low_back(product(normed, w_query)), cosine, sine))
    keyset = low(rotary(low_back(product(normed, w_key)), cosine, sine))
    own_values = low_back(low(product(normed, w_value)))
    if first_values is None:
        mixed = own_values
    else:
        mixed = low(0.5 * own_values + 0.5 * low_back(first_values))
    attended = low_back(low(attention(queries, keyset, mixed, segment, live)))
    middle = rows + low_back(product(attended, w_out))
    ffn_normed = low(rms_norm(middle, ffn_gain))
    gate_rows = low_back(product(ffn_normed, w_gate))
    up_rows = low_back(product(ffn_normed, w_up))
    activation = low(jax.nn.silu(gate_rows) * up_rows)
    return (middle + low_back(product(activation, w_down)), own_values)

def reference(hidden_in, lengths, w_query, w_key, w_value, w_out, w_gate, w_up, w_down, attn_gain, ffn_gain, cotangent):
    weights = tuple((item.astype(jnp.float32) for item in (w_query, w_key, w_value, w_out, w_gate, w_up, w_down, attn_gain, ffn_gain)))

    def row_step(totals, inputs):
        row_in, row_cot, row_len = inputs
        tables = slot_tables(row_len)

        def forward(rows, probe, params):
            lower = tuple((item[0] for item in params))
            upper = tuple((item[1] for item in params))
            first_out, first_values = layer(rows, None, lower, tables)
            carried = low_back(low(first_out) + probe)
            second_out, unused = layer(carried, first_values, upper, tables)
            return (carried, second_out)
        (carried, second_out), pullback = jax.vjp(forward, row_in, jnp.zeros_like(row_in), weights)
        row_grad, carried_grad, param_grads = pullback((jnp.zeros_like(carried), row_cot))
        totals = tuple((a + b for a, b in zip(totals, param_grads)))
        return (totals, (carried, second_out, row_grad, carried_grad))
    start = tuple((jnp.zeros_like(item) for item in weights))
    totals, outputs = lax.scan(row_step, start, (hidden_in.astype(jnp.float32), cotangent.astype(jnp.float32), lengths))
    first_all, second_all, grad_first, grad_second = outputs
    layer_outputs = jnp.stack([first_all, second_all]).astype(jnp.bfloat16)
    input_grads = jnp.stack([grad_first, grad_second])
    return (layer_outputs, input_grads, totals[0], totals[1], totals[2], totals[3], totals[4], totals[5], totals[6], totals[7], totals[8])
```

```python
import functools

import jax
import jax.numpy as jnp
from jax import lax
from jax.experimental import pallas as pl
from jax.experimental.pallas import tpu as pltpu
from jax.sharding import PartitionSpec as P

D = 1024
HD = 64
SLOTS = 2048
PAD = 128

EPSILON = 1e-05
MASKED = -1e30
SCALE = HD ** (-0.5)
VMEM_LIMIT = 56 * 1024 * 1024

F32 = jnp.float32
BF16 = jnp.bfloat16


def dot_nn(a, b):
    return lax.dot_general(a, b, (((1,), (0,)), ((), ())), preferred_element_type=F32)


def dot_nt(a, b):
    return lax.dot_general(a, b, (((1,), (1,)), ((), ())), preferred_element_type=F32)


def dot_tn(a, b):
    return lax.dot_general(a, b, (((0,), (0,)), ((), ())), preferred_element_type=F32)


def slot_tables(length_row):
    padded = (length_row + PAD - 1) // PAD * PAD
    starts = jnp.cumsum(padded) - padded
    slots = jnp.arange(SLOTS, dtype=jnp.int32)
    inside = (slots[:, None] >= starts[None, :]) & (slots[:, None] < (starts + padded)[None, :])
    begin = jnp.sum(jnp.where(inside, starts[None, :], 0), axis=1).astype(jnp.int32)
    end = jnp.sum(jnp.where(inside, (starts + length_row)[None, :], 0), axis=1).astype(jnp.int32)
    last = jnp.minimum(slots, end - 1)
    freq = 10000.0 ** (-2.0 * jnp.arange(HD // 2, dtype=F32) / HD)
    angle = (slots - begin).astype(F32)[:, None] * freq[None, :]
    cosine = jnp.concatenate([jnp.cos(angle), jnp.cos(angle)], axis=1)
    sine = jnp.concatenate([-jnp.sin(angle), jnp.sin(angle)], axis=1)
    return begin, last, cosine, sine


def tile_tables(begin, tile):
    count = SLOTS // tile
    index = jnp.arange(count, dtype=jnp.int32)
    low = begin[::tile]
    high = begin[tile - 1 :: tile]
    first = low // tile
    free = jnp.minimum((high + tile - 1) // tile, index)
    later = index[None, :] > index[:, None]
    free_end = index + 1 + jnp.sum(
        jnp.where(later & (high[None, :] <= index[:, None] * tile), 1, 0), axis=1
    )
    seen_end = index + 1 + jnp.sum(
        jnp.where(later & (low[None, :] < (index[:, None] + 1) * tile), 1, 0), axis=1
    )
    return jnp.stack([first, free, free_end.astype(jnp.int32), seen_end.astype(jnp.int32)])


def lane_in_head(shape):
    return lax.broadcasted_iota(jnp.int32, shape, 1) % HD


def turn(rows, cosine, sine):
    width = rows.shape[1]
    low = lane_in_head(rows.shape) < HD // 2
    if width == HD:
        swapped = jnp.concatenate([rows[:, HD // 2 :], rows[:, : HD // 2]], axis=1)
    else:
        swapped = jnp.where(
            low,
            pltpu.roll(rows, width - HD // 2, 1),
            pltpu.roll(rows, HD // 2, 1),
        )
    return rows * cosine + swapped * sine


def qkv_kernel(width, x_ref, w_ref, cos_ref, sin_ref, first_ref, q_ref, k_ref, v_ref, m_ref):
    product = dot_nn(x_ref[...], w_ref[...])
    repeat = width // cos_ref.shape[1]
    cosine = jnp.concatenate([cos_ref[...]] * repeat, axis=1)
    sine = jnp.concatenate([sin_ref[...]] * repeat, axis=1)
    q_ref[...] = (turn(product[:, :width], cosine, sine).astype(BF16).astype(F32) * SCALE).astype(BF16)
    k_ref[...] = turn(product[:, width : 2 * width], cosine, sine).astype(BF16)
    own = product[:, 2 * width :].astype(BF16)
    v_ref[...] = own
    if first_ref is not None:
        m_ref[...] = (0.5 * own.astype(F32) + 0.5 * first_ref[...].astype(F32)).astype(BF16)


def project(gathered, w_qkv, cosine, sine, first_values):
    width = w_qkv.shape[1] // 3
    tile = min(256, SLOTS)
    table = cosine.shape[1]
    row = lambda cols: pl.BlockSpec((tile, cols), lambda i: (i, 0))
    shape = jax.ShapeDtypeStruct((SLOTS, width), BF16)
    if first_values is None:
        kernel = lambda x, w, c, s, q, k, v: qkv_kernel(width, x, w, c, s, None, q, k, v, None)
        extra, specs, outs = (), [], 3
    else:
        kernel = functools.partial(qkv_kernel, width)
        extra, specs, outs = (first_values,), [row(width)], 4
    result = pl.pallas_call(
        kernel,
        grid=(SLOTS // tile,),
        in_specs=[
            row(D),
            pl.BlockSpec((D, 3 * width), lambda i: (0, 0)),
            row(table),
            row(table),
        ]
        + specs,
        out_specs=[row(width)] * outs,
        out_shape=[shape] * outs,
        compiler_params=pltpu.CompilerParams(vmem_limit_bytes=VMEM_LIMIT),
        cost_estimate=pl.CostEstimate(
            flops=2 * SLOTS * D * 3 * width, bytes_accessed=SLOTS * D * 4, transcendentals=0
        ),
        name="project",
    )(gathered, w_qkv, cosine, sine, *extra)
    return result if first_values is not None else (*result, result[2])


def allowed_scores(scores, start, low, high, tile):
    keys = start + lax.broadcasted_iota(jnp.int32, scores.shape, 0)
    return jnp.where((keys >= low) & (keys <= high), scores, MASKED)


def head_mask(rows, width, head):
    lanes = lax.broadcasted_iota(jnp.int32, (rows, width), 1)
    return (lanes >= head * HD) & (lanes < (head + 1) * HD)


def attend_kernel(tile, heads, meta, q_ref, k_ref, vt_ref, low_ref, high_ref, o_ref, lse_ref, acc, peak, mass):
    width = heads * HD
    index = pl.program_id(0)
    q = q_ref[...]
    low = low_ref[...]
    high = high_ref[...]
    queries = [jnp.where(head_mask(tile, width, hh), q, jnp.zeros_like(q)) for hh in range(heads)]
    acc[...] = jnp.zeros_like(acc)
    peak[...] = jnp.full_like(peak, MASKED)
    mass[...] = jnp.zeros_like(mass)

    def step(kt, masked):
        start = pl.multiple_of(kt * tile, tile)
        keys = k_ref[pl.ds(start, tile), :]
        for hh in range(heads):
            scores = dot_nt(keys, queries[hh])
            if masked:
                scores = allowed_scores(scores, start, low, high, tile)
            before = peak[hh : hh + 1, :]
            top = jnp.maximum(before, jnp.max(scores, axis=0, keepdims=True))
            weights = jnp.exp(scores - top)
            shrink = jnp.exp(before - top)
            peak[hh : hh + 1, :] = top
            mass[hh : hh + 1, :] = mass[hh : hh + 1, :] * shrink + jnp.sum(
                weights, axis=0, keepdims=True
            )
            rows = slice(hh * HD, (hh + 1) * HD)
            values = vt_ref[rows, pl.ds(start, tile)]
            acc[rows, :] = acc[rows, :] * shrink + dot_nn(values, weights.astype(BF16))

    step(index, True)

    def masked_step(kt, carry):
        step(kt, True)
        return carry

    def free_step(kt, carry):
        step(kt, False)
        return carry

    lax.fori_loop(meta[0, index], meta[1, index], masked_step, 0)
    lax.fori_loop(meta[1, index], index, free_step, 0)
    for hh in range(heads):
        rows = slice(hh * HD, (hh + 1) * HD)
        acc[rows, :] = acc[rows, :] / mass[hh : hh + 1, :]
    o_ref[...] = acc[...].T.astype(BF16)
    lse_ref[...] = peak[...] + jnp.log(mass[...])


def attend(queries, keys, mixed, low, high, meta, tile):
    width = queries.shape[1]
    heads = width // HD
    whole = lambda shape: pl.BlockSpec(shape, lambda i, meta: (0, 0))
    return pl.pallas_call(
        functools.partial(attend_kernel, tile, heads),
        grid_spec=pltpu.PrefetchScalarGridSpec(
            num_scalar_prefetch=1,
            grid=(SLOTS // tile,),
            in_specs=[
                pl.BlockSpec((tile, width), lambda i, meta: (i, 0)),
                whole((SLOTS, width)),
                whole((width, SLOTS)),
                pl.BlockSpec((1, tile), lambda i, meta: (0, i)),
                pl.BlockSpec((1, tile), lambda i, meta: (0, i)),
            ],
            out_specs=[
                pl.BlockSpec((tile, width), lambda i, meta: (i, 0)),
                pl.BlockSpec((heads, tile), lambda i, meta: (0, i)),
            ],
            scratch_shapes=[
                pltpu.VMEM((width, tile), F32),
                pltpu.VMEM((heads, tile), F32),
                pltpu.VMEM((heads, tile), F32),
            ],
        ),
        out_shape=[
            jax.ShapeDtypeStruct((SLOTS, width), BF16),
            jax.ShapeDtypeStruct((heads, SLOTS), F32),
        ],
        compiler_params=pltpu.CompilerParams(vmem_limit_bytes=VMEM_LIMIT),
        cost_estimate=pl.CostEstimate(
            flops=8 * SLOTS * SLOTS * width, bytes_accessed=SLOTS * width * 8, transcendentals=0
        ),
        name="attend",
    )(meta, queries, keys, mixed.T, low, high)


def attend_back_kernel(
    tile, heads, share, meta, q_ref, k_ref, kt_ref, v_ref, do_ref, lse_ref, delta_ref, low_ref, high_ref,
    cos_ref, sin_ref, cost_ref, sint_ref, carry_ref, dq_ref, dk_ref, dv_ref, dqt, dk, dv
):
    width = heads * HD
    index = pl.program_id(0)
    count = pl.num_programs(0)

    @pl.when(index == 0)
    def _():
        dqt[...] = jnp.zeros_like(dqt)

    dk[...] = jnp.zeros_like(dk)
    dv[...] = jnp.zeros_like(dv)
    keys = k_ref[...]
    values = v_ref[...]
    key_start = index * tile
    masks = [head_mask(tile, width, hh) for hh in range(heads)]
    transposed = [kt_ref[hh * HD : (hh + 1) * HD, :] for hh in range(heads)]

    def step(qt, masked):
        start = pl.multiple_of(qt * tile, tile)
        here = pl.ds(start, tile)
        q = q_ref[here, :]
        do = do_ref[here, :]
        low = low_ref[:, here]
        high = high_ref[:, here]
        for hh in range(heads):
            q_h = jnp.where(masks[hh], q, jnp.zeros_like(q))
            do_h = jnp.where(masks[hh], do, jnp.zeros_like(do))
            scores = dot_nt(keys, q_h)
            prob_grad = dot_nt(values, do_h)
            if masked:
                scores = allowed_scores(scores, key_start, low, high, tile)
            probs = jnp.exp(scores - lse_ref[hh : hh + 1, here])
            score_grad = (probs * (prob_grad - delta_ref[hh : hh + 1, here])).astype(BF16)
            dv[...] += dot_nn(probs.astype(BF16), do_h)
            dk[...] += dot_nn(score_grad, q_h)
            rows = slice(hh * HD, (hh + 1) * HD)
            dqt[rows, here] += dot_nn(transposed[hh], score_grad)

    step(index, True)

    def masked_step(qt, carry):
        step(qt, True)
        return carry

    def free_step(qt, carry):
        step(qt, False)
        return carry

    lax.fori_loop(index + 1, meta[2, index], free_step, 0)
    lax.fori_loop(meta[2, index], meta[3, index], masked_step, 0)
    repeat = width // cos_ref.shape[1]
    cosine = jnp.concatenate([cos_ref[...]] * repeat, axis=1)
    sine = jnp.concatenate([sin_ref[...]] * repeat, axis=1)
    dk_ref[...] = turn(dk[...], cosine, -sine).astype(BF16)
    if carry_ref is None:
        dv_ref[...] = (share * dv[...]).astype(BF16)
    else:
        dv_ref[...] = (share * dv[...] + carry_ref[...].astype(F32)).astype(BF16)

    @pl.when(index == count - 1)
    def _():
        half = HD // 2

        def finish(qt, carry):
            here = pl.ds(pl.multiple_of(qt * tile, tile), tile)
            cosine_t = cost_ref[:, here] * SCALE
            sine_t = sint_ref[:, here] * SCALE
            parts = []
            for hh in range(heads):
                u1 = dqt[hh * HD : hh * HD + half, here]
                u2 = dqt[hh * HD + half : (hh + 1) * HD, here]
                parts.append(u1 * cosine_t + u2 * sine_t)
                parts.append(u2 * cosine_t - u1 * sine_t)
            dq_ref[here, :] = jnp.concatenate(parts, axis=0).T.astype(BF16)
            return carry

        lax.fori_loop(0, count, finish, 0)


def attend_back(queries, keys, mixed, out_grad, sums, delta, low, high, meta, cosine, sine, half_tables, share, carry, tile):
    width = queries.shape[1]
    heads = width // HD
    whole = lambda shape: pl.BlockSpec(shape, lambda i, meta: (0, 0))
    rows = lambda cols: pl.BlockSpec((tile, cols), lambda i, meta: (i, 0))
    table = cosine.shape[1]
    base = functools.partial(attend_back_kernel, tile, heads, share)
    if carry is None:
        kernel = lambda *refs: base(*refs[:14], None, *refs[14:])
        extra, specs = (), []
    else:
        kernel = base
        extra, specs = (carry,), [rows(width)]
    return pl.pallas_call(
        kernel,
        grid_spec=pltpu.PrefetchScalarGridSpec(
            num_scalar_prefetch=1,
            grid=(SLOTS // tile,),
            in_specs=[
                whole((SLOTS, width)),
                rows(width),
                pl.BlockSpec((width, tile), lambda i, meta: (0, i)),
                rows(width),
                whole((SLOTS, width)),
                whole((heads, SLOTS)),
                whole((heads, SLOTS)),
                whole((1, SLOTS)),
                whole((1, SLOTS)),
                rows(table),
                rows(table),
                whole((HD // 2, SLOTS)),
                whole((HD // 2, SLOTS)),
            ]
            + specs,
            out_specs=[whole((SLOTS, width)), rows(width), rows(width)],
            scratch_shapes=[
                pltpu.VMEM((width, SLOTS), F32),
                pltpu.VMEM((tile, width), F32),
                pltpu.VMEM((tile, width), F32),
            ],
        ),
        out_shape=[jax.ShapeDtypeStruct((SLOTS, width), BF16)] * 3,
        compiler_params=pltpu.CompilerParams(vmem_limit_bytes=VMEM_LIMIT),
        cost_estimate=pl.CostEstimate(
            flops=20 * SLOTS * SLOTS * width, bytes_accessed=SLOTS * width * 14, transcendentals=0
        ),
        name="attend_back",
    )(meta, queries, keys, keys.T, mixed, out_grad, sums, delta, low, high, cosine, sine, *half_tables, *extra)


class Place:
    def __init__(self):
        self.size = lax.axis_size("head")
        self.half = self.size // 2
        self.data = lax.axis_size("dp")
        self.core = lax.axis_index("section")
        self.dp = lax.axis_index("dp")
        self.head = lax.axis_index("head")
        self.row = self.head // self.half
        self.seat = self.head % self.half
        self.region = (self.row + self.core) % 2

    def swap(self, x):
        return lax.ppermute(x, "section", [(0, 1), (1, 0)])

    def to_core(self, x, core):
        return lax.ppermute(x, "section", [(1 - core, core)])

    def across(self, x, core):
        size, half = self.size, self.half
        pairs = [(size + h, core * size + (h + half) % size) for h in range(size)]
        return lax.ppermute(x, ("section", "head"), pairs)

    def across_from_zero(self, x):
        size, half = self.size, self.half
        pairs = [(h, size + (h + half) % size) for h in range(size)]
        return lax.ppermute(x, ("section", "head"), pairs)

    def beside(self, x, shift):
        half = self.half
        pairs = [(h, h // half * half + (h % half + shift) % half) for h in range(self.size)]
        return lax.ppermute(x, "head", pairs)

    def around(self, x, shift):
        return lax.ppermute(x, "head", [(h, (h + shift) % self.size) for h in range(self.size)])

    def flip(self, x, bits):
        return lax.ppermute(x, "dp", [(d, d ^ bits) for d in range(self.data)])

    def by_seat(self, own, shifted):
        blocks = jnp.zeros((self.half, *own.shape), own.dtype)
        blocks = lax.dynamic_update_index_in_dim(blocks, own, self.seat, 0)
        for shift, block in enumerate(shifted, 1):
            seat = (self.seat - shift) % self.half
            blocks = lax.dynamic_update_index_in_dim(blocks, block, seat, 0)
        return blocks

    def by_region(self, own, other):
        return jnp.where(
            self.region == 0, jnp.concatenate([own, other]), jnp.concatenate([other, own])
        )

    def gather_row(self, block):
        shifted = [self.beside(block, shift) for shift in range(1, self.half)]
        own = self.by_seat(block, shifted).reshape(-1, block.shape[1])
        return self.by_region(own, self.swap(own))

    def regions(self, rows):
        pair = rows.reshape(2, rows.shape[0] // 2, *rows.shape[1:])
        own = lax.dynamic_index_in_dim(pair, self.region, 0, keepdims=False)
        other = lax.dynamic_index_in_dim(pair, 1 - self.region, 0, keepdims=False)
        return own, other

    def seat_block(self, blocks, shift):
        return lax.dynamic_index_in_dim(blocks, (self.seat + shift) % self.half, 0, keepdims=False)

    def scatter_row(self, partial):
        own, other = self.regions(partial)
        summed = own + self.swap(other.astype(BF16)).astype(F32)
        summed = summed.reshape(self.half, -1, partial.shape[1])
        total = self.seat_block(summed, 0)
        for shift in range(1, self.half):
            sent = self.seat_block(summed, shift).astype(BF16)
            total = total + self.beside(sent, shift).astype(F32)
        return total

    def heads_to_slots(self, rows):
        own, other = self.regions(rows)
        pair = jnp.stack([own, self.swap(other)])
        pair = pair.reshape(2, self.half, -1, rows.shape[1]).swapaxes(0, 1)
        shifted = [
            self.beside(self.seat_block(pair, shift), shift) for shift in range(1, self.half)
        ]
        blocks = self.by_seat(self.seat_block(pair, 0), shifted)
        blocks = self.by_region(blocks[:, 0], blocks[:, 1])
        return jnp.concatenate([blocks[i] for i in range(self.size)], axis=1)

    def slots_to_heads(self, block):
        width = block.shape[1] // self.size
        cut = jnp.stack([block[:, i * width : (i + 1) * width] for i in range(self.size)])
        own, other = self.regions(cut)
        pair = jnp.stack([own, other], axis=1)
        shifted = [
            self.beside(self.seat_block(pair, shift), shift) for shift in range(1, self.half)
        ]
        rows = self.by_seat(self.seat_block(pair, 0), shifted)
        return self.by_region(
            rows[:, 0].reshape(-1, width), self.swap(rows[:, 1].reshape(-1, width))
        )

    def data_block(self, x, bits):
        return lax.dynamic_index_in_dim(x, self.dp ^ bits, 0, keepdims=False)

    def scatter_data(self, first, second):
        def half_way(x, near, far):
            sent = jnp.stack([self.data_block(x, near), self.data_block(x, near ^ far)])
            kept = jnp.stack([self.data_block(x, 0), self.data_block(x, far)])
            return kept.astype(F32) + self.flip(sent.astype(BF16), near).astype(F32)

        first, second = half_way(first, 1, 2), half_way(second, 2, 1)
        first = first[0] + self.flip(first[1].astype(BF16), 2).astype(F32)
        second = second[0] + self.flip(second[1].astype(BF16), 1).astype(F32)
        return first, second

    def gather_data(self, x):
        blocks = jnp.zeros((self.data, *x.shape), x.dtype)
        blocks = lax.dynamic_update_index_in_dim(blocks, x, self.dp, 0)
        for bits in range(1, self.data):
            blocks = lax.dynamic_update_index_in_dim(blocks, self.flip(x, bits), self.dp ^ bits, 0)
        return blocks

    def head_block(self, x, shift):
        return lax.dynamic_index_in_dim(x, (self.head + shift) % self.size, 0, keepdims=False)

    def scatter_heads(self, x):
        total = self.head_block(x, 0).astype(F32)
        for shift in range(1, self.size):
            sent = self.head_block(x, shift).astype(BF16)
            total = total + self.around(sent, shift).astype(F32)
        return total

    def pick(self, zero, one):
        return jnp.where(self.core == 0, zero, one)


def weight_pieces(place, w_gate, w_up, w_down, w_out):
    kinds = (w_gate.T, w_up.T, w_down, w_out)
    cut = [item.reshape(place.data, 2, -1, D) for item in kinds]
    mine = jnp.concatenate(
        [lax.dynamic_index_in_dim(item, place.dp, 0, keepdims=False) for item in cut], axis=1
    )
    own = lax.dynamic_index_in_dim(mine, place.core, 0, keepdims=False)
    sent = lax.dynamic_index_in_dim(mine, 1 - place.core, 0, keepdims=False)
    other = place.swap(sent)
    return place.pick(own, other), place.pick(other, own)


def spread_weights(place, piece, units):
    full = lax.all_gather(piece, ("section", "dp", "head"), axis=0)
    gate, up, down = (full[:, i * units : (i + 1) * units].reshape(-1, D) for i in range(3))
    out = full[:, 3 * units :].reshape(2, place.data, place.size, -1, D)
    out = out.transpose(2, 1, 0, 3, 4).reshape(-1, D)
    return gate, up, down, out


def reduce_weights(place, gate, up, down, out):
    out = out.reshape(place.size, place.data, 2, -1, D).transpose(2, 1, 0, 3, 4)
    cut = [item.reshape(2, place.data, place.size, -1, D) for item in (gate, up, down)] + [out]

    def core_part(core):
        parts = [lax.dynamic_index_in_dim(item, core, 0, keepdims=False) for item in cut]
        return jnp.concatenate([part.astype(BF16) for part in parts], axis=2)

    own = core_part(place.core)
    summed = own.astype(F32) + place.swap(core_part(1 - place.core)).astype(F32)
    summed = summed.astype(BF16)
    first, second = place.scatter_data(summed[:, : place.half], summed[:, place.half :])
    piece = place.scatter_heads(jnp.concatenate([first, second]))
    return place.gather_data(piece.astype(BF16))


def norm(rows, gain):
    inverse = lax.rsqrt(jnp.mean(rows * rows, axis=1, keepdims=True) + EPSILON)
    return rows * inverse * gain


def norm_back(rows, gain, grad):
    inverse = lax.rsqrt(jnp.mean(rows * rows, axis=1, keepdims=True) + EPSILON)
    scaled = grad * gain
    gain_grad = jnp.sum(grad * rows * inverse, axis=0)
    rows_grad = inverse * scaled - rows * inverse**3 * jnp.mean(
        scaled * rows, axis=1, keepdims=True
    )
    return rows_grad, gain_grad


def layer_forward(place, rows, first_values, w_qkv, spread, gains, tables):
    cosine, sine, half_tables, low, high, meta, tile = tables
    gate_w, up_w, down_w, out_w = spread
    gathered = place.gather_row(norm(rows, gains[0]).astype(BF16))
    queries, keys, own_values, mixed = project(gathered, w_qkv, cosine, sine, first_values)
    attended_heads, sums = attend(queries, keys, mixed, low, high, meta, tile)
    attended = place.heads_to_slots(attended_heads)
    middle = rows + dot_nn(attended, out_w)
    ffn_normed = norm(middle, gains[1]).astype(BF16)
    gate = dot_nt(ffn_normed, gate_w)
    up = dot_nt(ffn_normed, up_w)
    activation = (jax.nn.silu(gate) * up).astype(BF16)
    result = middle + dot_nn(activation, down_w)
    kept = (
        rows, gathered, queries, keys, mixed, attended_heads, sums, attended, middle, ffn_normed,
        gate, up, activation,
    )
    return result, own_values, kept


def layer_backward(place, grad, share, carry, w_qkv, spread, gains, kept, tables):
    cosine, sine, half_tables, low, high, meta, tile = tables
    gate_w, up_w, down_w, out_w = spread
    (
        rows, gathered, queries, keys, mixed, attended_heads, sums, attended, middle, ffn_normed,
        gate, up, activation,
    ) = kept
    down_grad = grad.astype(BF16)
    act_grad = dot_nt(down_grad, down_w)
    sigma = jax.nn.sigmoid(gate)
    gate_grad = (act_grad * up * sigma * (1.0 + gate * (1.0 - sigma))).astype(BF16)
    up_grad = (act_grad * gate * sigma).astype(BF16)
    normed_grad = dot_nn(gate_grad, gate_w) + dot_nn(up_grad, up_w)
    middle_back, grad_ffn_gain = norm_back(middle, gains[1], normed_grad)
    middle_grad = grad + middle_back
    attn_grad = middle_grad.astype(BF16)
    attended_grad = dot_nt(attn_grad, out_w).astype(BF16)
    heads_grad = place.slots_to_heads(attended_grad)
    weight_grads = reduce_weights(
        place,
        dot_tn(gate_grad, ffn_normed),
        dot_tn(up_grad, ffn_normed),
        dot_tn(activation, down_grad),
        dot_tn(attended, attn_grad),
    )
    delta = heads_grad.astype(F32) * attended_heads.astype(F32)
    delta = jnp.sum(delta.reshape(SLOTS, -1, HD), axis=2).T
    query_grad, key_grad, value_grad = attend_back(
        queries, keys, mixed, heads_grad, sums, delta, low, high, meta, cosine, sine, half_tables,
        share, carry, tile,
    )
    lin_grad = jnp.concatenate([query_grad, key_grad, value_grad], axis=1)
    input_back = place.scatter_row(dot_nt(lin_grad, w_qkv))
    qkv_grad = dot_tn(gathered, lin_grad).astype(BF16)
    qkv_grad = qkv_grad.reshape(place.data, 2, -1, qkv_grad.shape[1])
    qkv_grad = jnp.stack(place.scatter_data(qkv_grad[:, 0], qkv_grad[:, 1])).astype(BF16)
    rows_back, grad_attn_gain = norm_back(rows, gains[0], input_back)
    return middle_grad + rows_back, value_grad, weight_grads, qkv_grad, (grad_attn_gain, grad_ffn_gain)


def local(
    hidden_in, lengths, w_query, w_key, w_value, w_out, w_gate, w_up, w_down, attn_gain, ffn_gain,
    cotangent,
):
    place = Place()
    width = w_query.shape[2]
    units = w_gate.shape[2] // (2 * place.data)
    tile = min(256, SLOTS // place.size)

    def mine_and_sent(x):
        mine = lax.dynamic_index_in_dim(x, place.row, 0, keepdims=False)
        sent = lax.dynamic_index_in_dim(x, 1 - place.row, 0, keepdims=False)
        return mine, sent

    mine, sent = mine_and_sent(hidden_in)
    rows = place.pick(mine, place.across(sent, 1)).astype(F32)

    w_qkv = jnp.concatenate([w_query[0], w_key[0], w_value[0]], axis=1)
    w_qkv_1 = place.pick(w_qkv, place.across_from_zero(w_qkv))
    w_qkv_2 = place.pick(place.to_core(w_qkv, 0), place.across(w_qkv, 1))
    piece_1, piece_2 = weight_pieces(place, w_gate[0], w_up[0], w_down[0], w_out[0])
    spread_1 = spread_weights(place, piece_1, units)
    spread_2 = spread_weights(place, piece_2, units)
    own_gains = jnp.concatenate([attn_gain, ffn_gain])
    other_gains = place.swap(own_gains)
    gains_1 = place.pick(own_gains, other_gains)
    gains_2 = place.pick(other_gains, own_gains)

    begin, last, cosine, sine = slot_tables(
        lax.dynamic_index_in_dim(lengths, place.row, 0, keepdims=False)
    )
    repeat = min(128, width) // HD
    half_tables = (cosine[:, HD // 2 :].T, sine[:, HD // 2 :].T)
    tables = (
        jnp.tile(cosine, (1, repeat)), jnp.tile(sine, (1, repeat)), half_tables,
        begin[None], last[None], tile_tables(begin, tile), tile,
    )

    result_1, values_1, kept_1 = layer_forward(
        place, rows, None, w_qkv_1, spread_1, gains_1, tables
    )
    hidden_1 = result_1.astype(BF16)
    result_2, _, kept_2 = layer_forward(
        place, hidden_1.astype(F32), values_1, w_qkv_2, spread_2, gains_2, tables
    )
    hidden_2 = result_2.astype(BF16)

    mine, sent = mine_and_sent(cotangent)
    grad = place.pick(mine, place.across(sent.astype(BF16), 1).astype(F32))
    grad_2, carry, ffn_2, qkv_2, gain_2 = layer_backward(
        place, grad, 0.5, None, w_qkv_2, spread_2, gains_2, kept_2, tables
    )
    grad_2 = grad_2.astype(BF16)
    grad_1, _, ffn_1, qkv_1, gain_1 = layer_backward(
        place, grad_2.astype(F32), 1.0, carry, w_qkv_1, spread_1, gains_1, kept_1, tables
    )

    def both_rows(first, second):
        near = place.pick(first, place.to_core(second.astype(BF16), 1).astype(first.dtype))
        far = place.pick(
            place.across(first.astype(BF16), 0), place.across(second.astype(BF16), 1)
        ).astype(first.dtype)
        return jnp.where(place.row == 0, jnp.stack([near, far]), jnp.stack([far, near]))[None]

    layer_outputs = both_rows(hidden_1, hidden_2)
    input_grads = both_rows(grad_1, grad_2.astype(F32))

    qkv_1 = qkv_1.astype(F32) + place.across(qkv_1, 0).astype(F32)
    qkv_2 = place.to_core(qkv_2, 1).astype(F32) + place.across(qkv_2, 1).astype(F32)
    qkv = place.gather_data(place.pick(qkv_1, qkv_2).astype(BF16)).astype(F32)
    qkv = qkv.reshape(D, 3, width)

    own = place.pick(ffn_1, ffn_2)
    other = place.swap(place.pick(ffn_2, ffn_1))
    ffn = jnp.where(place.core == 0, jnp.stack([own, other], 1), jnp.stack([other, own], 1))
    ffn = ffn.astype(F32)
    kinds = [ffn[:, :, i * units : (i + 1) * units].reshape(-1, D) for i in range(3)]
    out = ffn[:, :, 3 * units :].reshape(-1, D)

    gains = lax.psum(jnp.stack([*gain_1, *gain_2]), ("section", "dp", "head"))
    gains = place.pick(gains[:2], gains[2:])
    return (
        layer_outputs, input_grads, qkv[None, :, 0], qkv[None, :, 1], qkv[None, :, 2], out[None],
        kinds[0].T[None], kinds[1].T[None], kinds[2][None], gains[:1], gains[1:],
    )


def solution(mesh):
    in_specs = (
        P("dp", "head", None),
        P("dp", None),
        P("section", None, "head"),
        P("section", None, "head"),
        P("section", None, "head"),
        P("section", "head", None),
        P("section", None, "head"),
        P("section", None, "head"),
        P("section", "head", None),
        P("section", None),
        P("section", None),
        P("dp", "head", None),
    )
    out_specs = (
        P("section", "dp", "head", None),
        P("section", "dp", "head", None),
        P("section", None, "head"),
        P("section", None, "head"),
        P("section", None, "head"),
        P("section", "head", None),
        P("section", None, "head"),
        P("section", None, "head"),
        P("section", "head", None),
        P("section", None),
        P("section", None),
    )
    return jax.shard_map(local, mesh=mesh, in_specs=in_specs, out_specs=out_specs, check_vma=False)
```

```python
import functools

import jax
import jax.numpy as jnp
from jax import lax
from jax.experimental import pallas as pl
from jax.experimental.pallas import tpu as pltpu
from jax.sharding import PartitionSpec as P

D = 1024
HD = 64
SLOTS = 2048
PAD = 128

EPSILON = 1e-05
MASKED = -1e30
SCALE = HD ** (-0.5)
VMEM_LIMIT = 56 * 1024 * 1024


def lasting(microseconds):
    return pl.CostEstimate(flops=microseconds * 10**9, bytes_accessed=1, transcendentals=0)


F32 = jnp.float32
BF16 = jnp.bfloat16


def dot_nn(a, b):
    return lax.dot_general(a, b, (((1,), (0,)), ((), ())), preferred_element_type=F32)


def dot_nt(a, b):
    return lax.dot_general(a, b, (((1,), (1,)), ((), ())), preferred_element_type=F32)


def dot_tn(a, b):
    return lax.dot_general(a, b, (((0,), (0,)), ((), ())), preferred_element_type=F32)


def slot_tables(length_row):
    padded = (length_row + PAD - 1) // PAD * PAD
    starts = jnp.cumsum(padded) - padded
    slots = jnp.arange(SLOTS, dtype=jnp.int32)
    inside = (slots[:, None] >= starts[None, :]) & (slots[:, None] < (starts + padded)[None, :])
    begin = jnp.sum(jnp.where(inside, starts[None, :], 0), axis=1).astype(jnp.int32)
    end = jnp.sum(jnp.where(inside, (starts + length_row)[None, :], 0), axis=1).astype(jnp.int32)
    last = jnp.minimum(slots, end - 1)
    freq = 10000.0 ** (-2.0 * jnp.arange(HD // 2, dtype=F32) / HD)
    angle = (slots - begin).astype(F32)[:, None] * freq[None, :]
    cosine = jnp.concatenate([jnp.cos(angle), jnp.cos(angle)], axis=1)
    sine = jnp.concatenate([-jnp.sin(angle), jnp.sin(angle)], axis=1)
    return begin, last, cosine, sine


def tile_tables(begin, tile):
    count = SLOTS // tile
    index = jnp.arange(count, dtype=jnp.int32)
    low = begin[::tile]
    high = begin[tile - 1 :: tile]
    first = low // tile
    free = jnp.minimum((high + tile - 1) // tile, index)
    later = index[None, :] > index[:, None]
    free_end = index + 1 + jnp.sum(
        jnp.where(later & (high[None, :] <= index[:, None] * tile), 1, 0), axis=1
    )
    seen_end = index + 1 + jnp.sum(
        jnp.where(later & (low[None, :] < (index[:, None] + 1) * tile), 1, 0), axis=1
    )
    return jnp.stack([first, free, free_end.astype(jnp.int32), seen_end.astype(jnp.int32)])


def lane_in_head(shape):
    return lax.broadcasted_iota(jnp.int32, shape, 1) % HD


def turn(rows, cosine, sine):
    width = rows.shape[1]
    low = lane_in_head(rows.shape) < HD // 2
    if width == HD:
        swapped = jnp.concatenate([rows[:, HD // 2 :], rows[:, : HD // 2]], axis=1)
    else:
        swapped = jnp.where(
            low,
            pltpu.roll(rows, width - HD // 2, 1),
            pltpu.roll(rows, HD // 2, 1),
        )
    return rows * cosine + swapped * sine


def qkv_kernel(width, x_ref, w_ref, cos_ref, sin_ref, first_ref, q_ref, k_ref, v_ref, m_ref):
    product = dot_nn(x_ref[...], w_ref[...])
    repeat = width // cos_ref.shape[1]
    cosine = jnp.concatenate([cos_ref[...]] * repeat, axis=1)
    sine = jnp.concatenate([sin_ref[...]] * repeat, axis=1)
    q_ref[...] = (turn(product[:, :width], cosine, sine).astype(BF16).astype(F32) * SCALE).astype(BF16)
    k_ref[...] = turn(product[:, width : 2 * width], cosine, sine).astype(BF16)
    own = product[:, 2 * width :].astype(BF16)
    v_ref[...] = own
    if first_ref is not None:
        m_ref[...] = (0.5 * own.astype(F32) + 0.5 * first_ref[...].astype(F32)).astype(BF16)


def project(gathered, w_qkv, cosine, sine, first_values):
    width = w_qkv.shape[1] // 3
    tile = min(256, SLOTS)
    table = cosine.shape[1]
    row = lambda cols: pl.BlockSpec((tile, cols), lambda i: (i, 0))
    shape = jax.ShapeDtypeStruct((SLOTS, width), BF16)
    if first_values is None:
        kernel = lambda x, w, c, s, q, k, v: qkv_kernel(width, x, w, c, s, None, q, k, v, None)
        extra, specs, outs = (), [], 3
    else:
        kernel = functools.partial(qkv_kernel, width)
        extra, specs, outs = (first_values,), [row(width)], 4
    result = pl.pallas_call(
        kernel,
        grid=(SLOTS // tile,),
        in_specs=[
            row(D),
            pl.BlockSpec((D, 3 * width), lambda i: (0, 0)),
            row(table),
            row(table),
        ]
        + specs,
        out_specs=[row(width)] * outs,
        out_shape=[shape] * outs,
        compiler_params=pltpu.CompilerParams(vmem_limit_bytes=VMEM_LIMIT),
        cost_estimate=lasting(10),
        name="project",
    )(gathered, w_qkv, cosine, sine, *extra)
    return result if first_values is not None else (*result, result[2])


def head_mask(rows, width, head):
    lanes = lax.broadcasted_iota(jnp.int32, (rows, width), 1)
    return (lanes >= head * HD) & (lanes < (head + 1) * HD)


def attend_kernel(tile, heads, meta, q_ref, k_ref, vt_ref, low_ref, high_ref, o_ref, lse_ref, acc, peak, mass):
    width = heads * HD
    index = pl.program_id(0)
    q = q_ref[...]
    low = low_ref[...]
    high = high_ref[...]
    queries = [jnp.where(head_mask(tile, width, hh), q, jnp.zeros_like(q)) for hh in range(heads)]
    acc[...] = jnp.zeros_like(acc)
    peak[...] = jnp.full_like(peak, MASKED)
    mass[...] = jnp.zeros_like(mass)

    def step(kt, masked):
        start = pl.multiple_of(kt * tile, tile)
        keys = k_ref[pl.ds(start, tile), :]
        every = range(heads)
        rows = [slice(hh * HD, (hh + 1) * HD) for hh in every]
        scores = [dot_nt(keys, queries[hh]) for hh in every]
        if masked:
            slots = start + lax.broadcasted_iota(jnp.int32, scores[0].shape, 0)
            allowed = (slots >= low) & (slots <= high)
            scores = [jnp.where(allowed, x, MASKED) for x in scores]
        before = [peak[hh : hh + 1, :] for hh in every]
        tops = [jnp.maximum(before[hh], jnp.max(scores[hh], axis=0, keepdims=True)) for hh in every]
        weights = [jnp.exp(scores[hh] - tops[hh]) for hh in every]
        shrink = [jnp.exp(before[hh] - tops[hh]) for hh in every]
        sums = [
            mass[hh : hh + 1, :] * shrink[hh] + jnp.sum(weights[hh], axis=0, keepdims=True)
            for hh in every
        ]
        updates = [
            acc[rows[hh], :] * shrink[hh]
            + dot_nn(vt_ref[rows[hh], pl.ds(start, tile)], weights[hh].astype(BF16))
            for hh in every
        ]
        for hh in every:
            peak[hh : hh + 1, :] = tops[hh]
            mass[hh : hh + 1, :] = sums[hh]
            acc[rows[hh], :] = updates[hh]

    step(index, True)

    def masked_step(kt, carry):
        step(kt, True)
        return carry

    def free_step(kt, carry):
        step(kt, False)
        return carry

    lax.fori_loop(meta[0, index], meta[1, index], masked_step, 0)
    lax.fori_loop(meta[1, index], index, free_step, 0)
    for hh in range(heads):
        rows = slice(hh * HD, (hh + 1) * HD)
        acc[rows, :] = acc[rows, :] / mass[hh : hh + 1, :]
    o_ref[...] = acc[...].T.astype(BF16)
    lse_ref[...] = peak[...] + jnp.log(mass[...])


def attend(queries, keys, mixed, low, high, meta, tile):
    width = queries.shape[1]
    heads = width // HD
    whole = lambda shape: pl.BlockSpec(shape, lambda i, meta: (0, 0))
    return pl.pallas_call(
        functools.partial(attend_kernel, tile, heads),
        grid_spec=pltpu.PrefetchScalarGridSpec(
            num_scalar_prefetch=1,
            grid=(SLOTS // tile,),
            in_specs=[
                pl.BlockSpec((tile, width), lambda i, meta: (i, 0)),
                whole((SLOTS, width)),
                whole((width, SLOTS)),
                pl.BlockSpec((1, tile), lambda i, meta: (0, i)),
                pl.BlockSpec((1, tile), lambda i, meta: (0, i)),
            ],
            out_specs=[
                pl.BlockSpec((tile, width), lambda i, meta: (i, 0)),
                pl.BlockSpec((heads, tile), lambda i, meta: (0, i)),
            ],
            scratch_shapes=[
                pltpu.VMEM((width, tile), F32),
                pltpu.VMEM((heads, tile), F32),
                pltpu.VMEM((heads, tile), F32),
            ],
        ),
        out_shape=[
            jax.ShapeDtypeStruct((SLOTS, width), BF16),
            jax.ShapeDtypeStruct((heads, SLOTS), F32),
        ],
        compiler_params=pltpu.CompilerParams(vmem_limit_bytes=VMEM_LIMIT),
        cost_estimate=lasting(25),
        name="attend",
    )(meta, queries, keys, mixed.T, low, high)


def attend_back_kernel(
    tile, heads, share, meta, q_ref, k_ref, kt_ref, v_ref, do_ref, lse_ref, delta_ref, low_ref, high_ref,
    cos_ref, sin_ref, cost_ref, sint_ref, carry_ref, dq_ref, dk_ref, dv_ref, dqt, dk, dv
):
    width = heads * HD
    index = pl.program_id(0)
    count = pl.num_programs(0)

    @pl.when(index == 0)
    def _():
        dqt[...] = jnp.zeros_like(dqt)

    dk[...] = jnp.zeros_like(dk)
    dv[...] = jnp.zeros_like(dv)
    keys = k_ref[...]
    values = v_ref[...]
    key_start = index * tile
    masks = [head_mask(tile, width, hh) for hh in range(heads)]
    transposed = [kt_ref[hh * HD : (hh + 1) * HD, :] for hh in range(heads)]

    def step(qt, masked):
        start = pl.multiple_of(qt * tile, tile)
        here = pl.ds(start, tile)
        q = q_ref[here, :]
        do = do_ref[here, :]
        low = low_ref[:, here]
        high = high_ref[:, here]
        every = range(heads)
        rows = [slice(hh * HD, (hh + 1) * HD) for hh in every]
        q_h = [jnp.where(masks[hh], q, jnp.zeros_like(q)) for hh in every]
        do_h = [jnp.where(masks[hh], do, jnp.zeros_like(do)) for hh in every]
        scores = [dot_nt(keys, q_h[hh]) for hh in every]
        prob_grad = [dot_nt(values, do_h[hh]) for hh in every]
        if masked:
            slots = key_start + lax.broadcasted_iota(jnp.int32, scores[0].shape, 0)
            allowed = (slots >= low) & (slots <= high)
            scores = [jnp.where(allowed, x, MASKED) for x in scores]
        probs = [jnp.exp(scores[hh] - lse_ref[hh : hh + 1, here]) for hh in every]
        score_grad = [
            (probs[hh] * (prob_grad[hh] - delta_ref[hh : hh + 1, here])).astype(BF16)
            for hh in every
        ]
        dv[...] += sum(dot_nn(probs[hh].astype(BF16), do_h[hh]) for hh in every)
        dk[...] += sum(dot_nn(score_grad[hh], q_h[hh]) for hh in every)
        updates = [dqt[rows[hh], here] + dot_nn(transposed[hh], score_grad[hh]) for hh in every]
        for hh in every:
            dqt[rows[hh], here] = updates[hh]

    step(index, True)

    def masked_step(qt, carry):
        step(qt, True)
        return carry

    def free_step(qt, carry):
        step(qt, False)
        return carry

    lax.fori_loop(index + 1, meta[2, index], free_step, 0)
    lax.fori_loop(meta[2, index], meta[3, index], masked_step, 0)
    repeat = width // cos_ref.shape[1]
    cosine = jnp.concatenate([cos_ref[...]] * repeat, axis=1)
    sine = jnp.concatenate([sin_ref[...]] * repeat, axis=1)
    dk_ref[...] = turn(dk[...], cosine, -sine).astype(BF16)
    if carry_ref is None:
        dv_ref[...] = (share * dv[...]).astype(BF16)
    else:
        dv_ref[...] = (share * dv[...] + carry_ref[...].astype(F32)).astype(BF16)

    @pl.when(index == count - 1)
    def _():
        half = HD // 2

        def finish(qt, carry):
            here = pl.ds(pl.multiple_of(qt * tile, tile), tile)
            cosine_t = cost_ref[:, here] * SCALE
            sine_t = sint_ref[:, here] * SCALE
            parts = []
            for hh in range(heads):
                u1 = dqt[hh * HD : hh * HD + half, here]
                u2 = dqt[hh * HD + half : (hh + 1) * HD, here]
                parts.append(u1 * cosine_t + u2 * sine_t)
                parts.append(u2 * cosine_t - u1 * sine_t)
            dq_ref[here, :] = jnp.concatenate(parts, axis=0).T.astype(BF16)
            return carry

        lax.fori_loop(0, count, finish, 0)


def attend_back(queries, keys, mixed, out_grad, sums, delta, low, high, meta, cosine, sine, half_tables, share, carry, tile):
    width = queries.shape[1]
    heads = width // HD
    whole = lambda shape: pl.BlockSpec(shape, lambda i, meta: (0, 0))
    rows = lambda cols: pl.BlockSpec((tile, cols), lambda i, meta: (i, 0))
    table = cosine.shape[1]
    base = functools.partial(attend_back_kernel, tile, heads, share)
    if carry is None:
        kernel = lambda *refs: base(*refs[:14], None, *refs[14:])
        extra, specs = (), []
    else:
        kernel = base
        extra, specs = (carry,), [rows(width)]
    return pl.pallas_call(
        kernel,
        grid_spec=pltpu.PrefetchScalarGridSpec(
            num_scalar_prefetch=1,
            grid=(SLOTS // tile,),
            in_specs=[
                whole((SLOTS, width)),
                rows(width),
                pl.BlockSpec((width, tile), lambda i, meta: (0, i)),
                rows(width),
                whole((SLOTS, width)),
                whole((heads, SLOTS)),
                whole((heads, SLOTS)),
                whole((1, SLOTS)),
                whole((1, SLOTS)),
                rows(table),
                rows(table),
                whole((HD // 2, SLOTS)),
                whole((HD // 2, SLOTS)),
            ]
            + specs,
            out_specs=[whole((SLOTS, width)), rows(width), rows(width)],
            scratch_shapes=[
                pltpu.VMEM((width, SLOTS), F32),
                pltpu.VMEM((tile, width), F32),
                pltpu.VMEM((tile, width), F32),
            ],
        ),
        out_shape=[jax.ShapeDtypeStruct((SLOTS, width), BF16)] * 3,
        compiler_params=pltpu.CompilerParams(vmem_limit_bytes=VMEM_LIMIT),
        cost_estimate=lasting(36),
        name="attend_back",
    )(meta, queries, keys, keys.T, mixed, out_grad, sums, delta, low, high, cosine, sine, *half_tables, *extra)


class Place:
    def __init__(self):
        self.size = lax.axis_size("head")
        self.half = self.size // 2
        self.data = lax.axis_size("dp")
        self.core = lax.axis_index("section")
        self.dp = lax.axis_index("dp")
        self.head = lax.axis_index("head")
        self.row = self.head // self.half
        self.seat = self.head % self.half
        self.region = (self.row + self.core) % 2

    def swap(self, x):
        return lax.ppermute(x, "section", [(0, 1), (1, 0)])

    def to_core(self, x, core):
        return lax.ppermute(x, "section", [(1 - core, core)])

    def across(self, x, core):
        size, half = self.size, self.half
        pairs = [(size + h, core * size + (h + half) % size) for h in range(size)]
        return lax.ppermute(x, ("section", "head"), pairs)

    def across_from_zero(self, x):
        size, half = self.size, self.half
        pairs = [(h, size + (h + half) % size) for h in range(size)]
        return lax.ppermute(x, ("section", "head"), pairs)

    def beside(self, x, shift):
        half = self.half
        pairs = [(h, h // half * half + (h % half + shift) % half) for h in range(self.size)]
        return lax.ppermute(x, "head", pairs)

    def around(self, x, shift):
        return lax.ppermute(x, "head", [(h, (h + shift) % self.size) for h in range(self.size)])

    def flip(self, x, bits):
        return lax.ppermute(x, "dp", [(d, d ^ bits) for d in range(self.data)])

    def by_seat(self, own, shifted):
        blocks = jnp.zeros((self.half, *own.shape), own.dtype)
        blocks = lax.dynamic_update_index_in_dim(blocks, own, self.seat, 0)
        for shift, block in enumerate(shifted, 1):
            seat = (self.seat - shift) % self.half
            blocks = lax.dynamic_update_index_in_dim(blocks, block, seat, 0)
        return blocks

    def by_region(self, own, other):
        return jnp.where(
            self.region == 0, jnp.concatenate([own, other]), jnp.concatenate([other, own])
        )

    def gather_row(self, block):
        shifted = [self.beside(block, shift) for shift in range(1, self.half)]
        own = self.by_seat(block, shifted).reshape(-1, block.shape[1])
        return self.by_region(own, self.swap(own))

    def regions(self, rows):
        pair = rows.reshape(2, rows.shape[0] // 2, *rows.shape[1:])
        own = lax.dynamic_index_in_dim(pair, self.region, 0, keepdims=False)
        other = lax.dynamic_index_in_dim(pair, 1 - self.region, 0, keepdims=False)
        return own, other

    def seat_block(self, blocks, shift):
        return lax.dynamic_index_in_dim(blocks, (self.seat + shift) % self.half, 0, keepdims=False)

    def scatter_row(self, partial, tied):
        own, other = self.regions(partial)
        summed = own + self.swap(other.astype(BF16)).astype(F32)
        summed = tied(summed.reshape(self.half, -1, partial.shape[1]))
        total = self.seat_block(summed, 0)
        for shift in range(1, self.half):
            sent = self.seat_block(summed, shift).astype(BF16)
            total = total + self.beside(sent, shift).astype(F32)
        return total

    def heads_to_slots(self, rows):
        own, other = self.regions(rows)
        pair = jnp.stack([own, self.swap(other)])
        pair = pair.reshape(2, self.half, -1, rows.shape[1]).swapaxes(0, 1)
        shifted = [
            self.beside(self.seat_block(pair, shift), shift) for shift in range(1, self.half)
        ]
        blocks = self.by_seat(self.seat_block(pair, 0), shifted)
        blocks = self.by_region(blocks[:, 0], blocks[:, 1])
        return jnp.concatenate([blocks[i] for i in range(self.size)], axis=1)

    def slots_to_heads(self, block):
        width = block.shape[1] // self.size
        cut = jnp.stack([block[:, i * width : (i + 1) * width] for i in range(self.size)])
        own, other = self.regions(cut)
        pair = jnp.stack([own, other], axis=1)
        shifted = [
            self.beside(self.seat_block(pair, shift), shift) for shift in range(1, self.half)
        ]
        rows = self.by_seat(self.seat_block(pair, 0), shifted)
        return self.by_region(
            rows[:, 0].reshape(-1, width), self.swap(rows[:, 1].reshape(-1, width))
        )

    def data_block(self, x, bits):
        return lax.dynamic_index_in_dim(x, self.dp ^ bits, 0, keepdims=False)

    def by_data(self, own, flipped):
        blocks = jnp.zeros((self.data, *own.shape), own.dtype)
        blocks = lax.dynamic_update_index_in_dim(blocks, own, self.dp, 0)
        for bits, block in enumerate(flipped, 1):
            blocks = lax.dynamic_update_index_in_dim(blocks, block, self.dp ^ bits, 0)
        return blocks

    def gather_data(self, x):
        return self.by_data(x, [self.flip(x, bits) for bits in range(1, self.data)])

    def head_block(self, x, shift):
        return lax.dynamic_index_in_dim(x, (self.head + shift) % self.size, 0, keepdims=False)

    def scatter_heads(self, x):
        total = self.head_block(x, 0).astype(F32)
        for shift in range(1, self.size):
            sent = self.head_block(x, shift).astype(BF16)
            total = total + self.around(sent, shift).astype(F32)
        return total

    def spot(self):
        return jnp.stack([self.dp, self.head]).astype(jnp.int32)

    def by_core(self, own, other, axis):
        return jnp.where(
            self.core == 0, jnp.stack([own, other], axis), jnp.stack([other, own], axis)
        )

    def gather_cores(self, x):
        return self.by_core(x, self.swap(x), 0).reshape(-1, x.shape[1])

    def scatter_cores(self, partial):
        pair = partial.reshape(2, -1, partial.shape[1])
        own = lax.dynamic_index_in_dim(pair, self.core, 0, keepdims=False)
        other = lax.dynamic_index_in_dim(pair, 1 - self.core, 0, keepdims=False)
        return own + self.swap(other.astype(BF16)).astype(F32)

    def by_row(self, own, other):
        return jnp.where(
            self.row == 0, jnp.concatenate([own, other]), jnp.concatenate([other, own])
        )

    def pick(self, zero, one):
        return jnp.where(self.core == 0, zero, one)


class Chain:
    def __init__(self, stages):
        self.stages = stages
        self.result = None
        self.flight = next(stages)

    def advance(self, arrived):
        try:
            self.flight = self.stages.send(arrived)
        except StopIteration as stop:
            self.result = stop.value

    def step(self, x):
        x, arrived = lax.optimization_barrier((x, self.flight))
        self.advance(arrived)
        return x


def lockstep(*chains):
    while active := [chain for chain in chains if chain.result is None]:
        arrived = lax.optimization_barrier([chain.flight for chain in active])
        for chain, item in zip(active, arrived):
            chain.advance(item)
    return [chain.result for chain in chains]


def after(x, *others):
    return lax.optimization_barrier((x, *others))[0]


class Cut:
    def __init__(self, place, w_gate, w_out):
        self.heads = place.size
        self.units = w_gate.shape[2] // 2
        self.outs = w_out.shape[1] // 2
        self.rows = 3 * self.units + self.outs
        self.down = (self.rows // 2 - self.units - self.outs) // 16 * 16
        self.first = self.units + self.outs + self.down
        self.second = self.rows - self.first
        self.columns = D // place.data

    def pieces(self):
        units, outs, down = self.units, self.outs, self.down
        return (
            ("gate", 0, units, 0, 0),
            ("out", 0, outs, 0, units),
            ("down", 0, down, 0, units + outs),
            ("down", down, units - down, 1, 0),
            ("up", 0, units, 1, units - down),
        )


def pack_weights(place, cut, w_gate, w_up, w_down, w_out):
    kinds = (w_gate.T, w_out, w_down, w_up.T)
    halves = [item.reshape(2, -1, D) for item in kinds]

    def half(core):
        return jnp.concatenate(
            [lax.dynamic_index_in_dim(item, core, 0, keepdims=False) for item in halves]
        )

    own = half(place.core)
    other = place.swap(half(1 - place.core))
    return place.pick(own, other), place.pick(other, own)


def any_specs(count):
    return [pl.BlockSpec(memory_space=pl.ANY)] * count


def run_copies(copies):
    for copy in copies:
        copy.start()
    for copy in copies:
        copy.wait()


def assemble_kernel(cut, groups, spot, share, *refs):
    dp, head = spot[0], spot[1]
    gu, down, out, sems = refs[5 * len(groups) :]
    kinds = {"gate": gu.at[0], "up": gu.at[1], "down": down, "out": out}
    copies = []

    def add(source, kind, step, row, count, columns):
        index = lax.rem(head - step + cut.heads, cut.heads) if kind == "out" else step
        target = kinds[kind].at[index, pl.ds(row, count), columns]
        copies.append(pltpu.make_async_copy(source, target, sems.at[len(copies)]))

    for kind, row, count, part, at in cut.pieces():
        base = at + part * cut.first
        add(share.at[pl.ds(base, count), :], kind, 0, row, count, slice(None))
    for number, steps in enumerate(groups):
        ring, first_x, second_y, first_y, second_x = refs[5 * number : 5 * number + 5]
        for i, step in enumerate(steps):
            firsts = (
                ring.at[i, pl.ds(0, cut.first)], first_x.at[i], first_y.at[0, i], first_y.at[1, i],
            )
            seconds = (
                ring.at[i, pl.ds(cut.first, cut.second)], second_x.at[0, i], second_y.at[i],
                second_x.at[1, i],
            )
            for bits in range(4):
                start = pl.multiple_of((dp ^ bits) * cut.columns, cut.columns)
                for kind, row, count, part, at in cut.pieces():
                    source = (firsts, seconds)[part][bits].at[pl.ds(at, count), :]
                    add(source, kind, step, row, count, pl.ds(start, cut.columns))
    run_copies(copies)


def near_flips(place, cut, ring):
    return place.flip(ring[:, : cut.first], 1), place.flip(ring[:, cut.first :], 2)


def far_flips(place, cut, ring, first_x, second_y):
    first = jnp.stack([ring[:, : cut.first], first_x])
    second = jnp.stack([ring[:, cut.first :], second_y])
    return place.flip(first, 2), place.flip(second, 1)


def spread_at_once(place, cut, share, piece):
    size = cut.heads
    ring = jnp.stack((yield [place.around(piece, step) for step in range(1, size)]))
    near = yield near_flips(place, cut, ring)
    far = yield far_flips(place, cut, ring, *near)
    return assemble(place, cut, share, [(list(range(1, size)), (ring, *near, *far))])


def spread_in_turn(place, cut, share, piece):
    size = cut.heads
    piece = yield place.around(piece, 1)
    ring_1 = piece[None]
    piece, near_1 = yield place.around(piece, 1), near_flips(place, cut, ring_1)
    ring = [piece]
    for _ in range(3, size):
        ring.append(place.around(ring[-1], 1))
    ring, far_1 = yield ring, far_flips(place, cut, ring_1, *near_1)
    ring = jnp.stack(ring)
    near = yield near_flips(place, cut, ring)
    far = yield far_flips(place, cut, ring, *near)
    groups = [([1], (ring_1, *near_1, *far_1)), (list(range(2, size)), (ring, *near, *far))]
    return assemble(place, cut, share, groups)


def first_qkv(place, w_qkv, part):
    part = yield place.across_from_zero(part)
    flipped = yield [place.flip(part, bits) for bits in range(1, place.data)]
    return place.pick(w_qkv, place.by_data(part, flipped).reshape(w_qkv.shape))


def second_qkv(place, w_qkv, part):
    own, part = yield place.to_core(w_qkv, 0), place.across(part, 1)
    flipped = yield [place.flip(part, bits) for bits in range(1, place.data)]
    return place.pick(own, place.by_data(part, flipped).reshape(w_qkv.shape))


def gather_far(place, far, gain):
    far = yield far
    shifted = yield [
        place.beside(norm(far.astype(F32), gain).astype(BF16), shift)
        for shift in range(1, place.half)
    ]
    return far, shifted


def assemble(place, cut, share, groups):
    steps = [group[0] for group in groups]
    parts = [part for group in groups for part in group[1]]
    copies = 5 * (1 + 4 * (cut.heads - 1))
    shape = lambda *dims: jax.ShapeDtypeStruct(dims, BF16)
    gate_up, down, out = pl.pallas_call(
        functools.partial(assemble_kernel, cut, steps),
        in_specs=[pl.BlockSpec(memory_space=pltpu.SMEM)] + any_specs(1 + len(parts)),
        out_specs=[pl.BlockSpec(memory_space=pltpu.VMEM)] * 3,
        out_shape=[
            shape(2, cut.heads, cut.units, D), shape(cut.heads, cut.units, D),
            shape(cut.heads, cut.outs, D),
        ],
        scratch_shapes=[pltpu.SemaphoreType.DMA((copies,))],
        compiler_params=pltpu.CompilerParams(vmem_limit_bytes=VMEM_LIMIT),
        cost_estimate=lasting(8),
        name="assemble",
    )(place.spot(), share, *parts)
    out = place.by_core(out, place.swap(out), 1).reshape(-1, D)
    return gate_up[0].reshape(-1, D), gate_up[1].reshape(-1, D), down.reshape(-1, D), out


def split_kernel(cut, chunks, spot, gate, up, down, out, *refs):
    dp, head = spot[0], spot[1]
    sems = refs[-1]
    kinds = {"gate": gate, "up": up, "down": down, "out": out}
    copies = []
    for number, steps in enumerate(chunks):
        first_kept, first_sent, second_kept, second_sent = refs[4 * number : 4 * number + 4]
        firsts = (first_kept.at[0], first_sent.at[0], first_kept.at[1], first_sent.at[1])
        seconds = (second_kept.at[0], second_kept.at[1], second_sent.at[0], second_sent.at[1])
        for bits in range(4):
            start = pl.multiple_of((dp ^ bits) * cut.columns, cut.columns)
            for i, step in enumerate(steps):
                for kind, row, count, part, at in cut.pieces():
                    index = step
                    if kind == "out":
                        index = lax.rem(head - step + cut.heads, cut.heads)
                    source = kinds[kind].at[index, pl.ds(row, count), pl.ds(start, cut.columns)]
                    target = (firsts, seconds)[part][bits].at[i, pl.ds(at, count), :]
                    copies.append(pltpu.make_async_copy(source, target, sems.at[len(copies)]))
    run_copies(copies)


def split_grads(place, cut, gate, up, down, out):
    half = cut.heads // 2
    chunks = [list(range(half, cut.heads)), list(range(half))]
    shape = lambda steps, rows: jax.ShapeDtypeStruct((2, len(steps), rows, cut.columns), BF16)
    shapes = []
    for steps in chunks:
        shapes += [shape(steps, cut.first)] * 2 + [shape(steps, cut.second)] * 2
    split = pl.pallas_call(
        functools.partial(split_kernel, cut, chunks),
        in_specs=[pl.BlockSpec(memory_space=pltpu.SMEM)]
        + [pl.BlockSpec(memory_space=pltpu.VMEM)] * 4,
        out_specs=any_specs(8),
        out_shape=shapes,
        scratch_shapes=[pltpu.SemaphoreType.DMA((20 * cut.heads,))],
        compiler_params=pltpu.CompilerParams(vmem_limit_bytes=VMEM_LIMIT),
        cost_estimate=lasting(8),
        name="split",
    )(place.spot(), *(item.reshape(cut.heads, -1, D) for item in (gate, up, down, out)))
    return split[:4], split[4:]


def exchange(place, part):
    first, second = yield place.flip(part[1], 1), place.flip(part[3], 2)
    first = part[0].astype(F32) + first.astype(F32)
    second = part[2].astype(F32) + second.astype(F32)
    moved = yield place.flip(first[1].astype(BF16), 2), place.flip(second[1].astype(BF16), 1)
    kept = first[0], second[0]
    return jnp.concatenate([x + y.astype(F32) for x, y in zip(kept, moved)], axis=1)


def reduce_far(place, cut, part):
    half = cut.heads // 2
    blocks = yield from exchange(place, part)
    arrived = yield [
        place.around(blocks[step - half].astype(BF16), -step) for step in range(half, cut.heads)
    ]
    return sum(item.astype(F32) for item in arrived)


def reduce_near(place, cut, part, far):
    blocks = yield from exchange(place, part)
    total = blocks[0]
    if cut.heads > 2:
        arrived = yield [
            place.around(blocks[step].astype(BF16), -step) for step in range(1, cut.heads // 2)
        ]
        total = total + sum(item.astype(F32) for item in arrived)
    total = (total + far.result).astype(BF16)
    flipped = yield [place.flip(total, bits) for bits in range(1, place.data)]
    parts = place.by_data(total, flipped)
    return jnp.concatenate([parts[d] for d in range(place.data)], axis=1)


def reduce_qkv(place, grad, core):
    grad = grad.reshape(place.data, 2, -1, grad.shape[1])
    first, second = grad[:, 0], grad[:, 1]
    sent = [
        jnp.stack([place.data_block(x, bits) for bits in pair])
        for x, pair in ((first, (1, 3)), (second, (2, 3)))
    ]
    kept = [
        jnp.stack([place.data_block(x, bits) for bits in pair])
        for x, pair in ((first, (0, 2)), (second, (0, 1)))
    ]
    arrived = yield place.flip(sent[0], 1), place.flip(sent[1], 2)
    first, second = (a.astype(F32) + b.astype(F32) for a, b in zip(kept, arrived))
    arrived = yield place.flip(first[1].astype(BF16), 2), place.flip(second[1].astype(BF16), 1)
    piece = jnp.concatenate([first[0] + arrived[0].astype(F32), second[0] + arrived[1].astype(F32)])
    piece = piece.astype(BF16)
    if core == 0:
        other = yield place.across(piece, 0)
        return piece.astype(F32) + other.astype(F32)
    own, other = yield place.to_core(piece, 1), place.across(piece, 1)
    return own.astype(F32) + other.astype(F32)


def norm(rows, gain):
    inverse = lax.rsqrt(jnp.mean(rows * rows, axis=1, keepdims=True) + EPSILON)
    return rows * inverse * gain


def norm_back(rows, gain, grad):
    inverse = lax.rsqrt(jnp.mean(rows * rows, axis=1, keepdims=True) + EPSILON)
    scaled = grad * gain
    gain_grad = jnp.sum(grad * rows * inverse, axis=0)
    rows_grad = inverse * scaled - rows * inverse**3 * jnp.mean(
        scaled * rows, axis=1, keepdims=True
    )
    return rows_grad, gain_grad


def layer_forward(place, rows, gathered, first_values, w_qkv, chain, gains, tables, later=()):
    cosine, sine, half_tables, low, high, meta, tile = tables
    if later:
        gathered = chain.step(gathered)
    later = [Chain(begin(gathered)) for begin in later]
    queries, keys, own_values, mixed = project(gathered, w_qkv, cosine, sine, first_values)
    queries = chain.step(queries)
    attended_heads, sums = attend(queries, keys, mixed, low, high, meta, tile)
    if later:
        attended_heads = chain.step(attended_heads)
    attended = place.heads_to_slots(attended_heads)
    for other in later:
        attended = other.step(attended)
    gate_w, up_w, down_w, out_w = spread = chain.result
    middle = rows + dot_nn(attended, out_w)
    ffn_normed = place.gather_cores(norm(middle, gains[1]).astype(BF16))
    gate = dot_nt(ffn_normed, gate_w)
    up = dot_nt(ffn_normed, up_w)
    activation = (jax.nn.silu(gate) * up).astype(BF16)
    result = middle + place.scatter_cores(dot_nn(activation, down_w))
    for other in later:
        result = other.step(result)
    kept = (
        rows, gathered, queries, keys, mixed, attended_heads, sums, attended, middle, ffn_normed,
        gate, up, activation,
    )
    return result, own_values, spread, kept, later


def join_halves(place, x, shifted):
    own = place.by_seat(x, shifted)
    return place.by_core(own, place.swap(own), 1).reshape(-1, x.shape[1])


def layer_backward(place, cut, grad, share, carry, w_qkv, spread, gains, kept, tables, earlier=((), (), ())):
    cosine, sine, half_tables, low, high, meta, tile = tables
    gate_w, up_w, down_w, out_w = spread
    (
        rows, gathered, queries, keys, mixed, attended_heads, sums, attended, middle, ffn_normed,
        gate, up, activation,
    ) = kept
    down_grad = place.gather_cores(grad.astype(BF16))
    act_grad = dot_nt(down_grad, down_w)
    sigma = jax.nn.sigmoid(gate)
    gate_grad = (act_grad * up * sigma * (1.0 + gate * (1.0 - sigma))).astype(BF16)
    up_grad = (act_grad * gate * sigma).astype(BF16)
    normed_grad = place.scatter_cores(dot_nn(gate_grad, gate_w) + dot_nn(up_grad, up_w))
    middle_back, grad_ffn_gain = norm_back(middle, gains[1], normed_grad)
    middle_grad = grad + middle_back
    attn_grad = middle_grad.astype(BF16)
    attended_grad = dot_nt(attn_grad, out_w).astype(BF16)
    heads_grad = place.slots_to_heads(attended_grad)
    gate_grad, up_grad, activation = after((gate_grad, up_grad, activation), attended_grad)
    out_grad = dot_tn(attended, attn_grad).reshape(place.size, 2, -1, D).swapaxes(0, 1)
    out_grad = place.scatter_cores(out_grad.reshape(-1, D))
    split = split_grads(
        place, cut, dot_tn(gate_grad, ffn_normed).astype(BF16),
        dot_tn(up_grad, ffn_normed).astype(BF16), dot_tn(activation, down_grad).astype(BF16),
        out_grad.astype(BF16),
    )
    heads_grad = after(heads_grad, *split[0], *split[1])
    for other in earlier[0]:
        heads_grad = other.step(heads_grad)
    far = Chain(reduce_far(place, cut, split[0]))
    delta = heads_grad.astype(F32) * attended_heads.astype(F32)
    delta = jnp.sum(delta.reshape(SLOTS, -1, HD), axis=2).T
    query_grad, key_grad, value_grad = attend_back(
        queries, keys, mixed, heads_grad, sums, delta, low, high, meta, cosine, sine, half_tables,
        share, carry, tile,
    )
    lin_grad = jnp.concatenate([query_grad, key_grad, value_grad], axis=1)
    partial = far.step(dot_nt(lin_grad, w_qkv))
    for other in earlier[1]:
        partial = other.step(partial)
    near = Chain(reduce_near(place, cut, after(split[1], partial), far))
    lin_grad = after(lin_grad, partial)
    qkv_grad = dot_tn(gathered, lin_grad).astype(BF16)
    input_back = place.scatter_row(partial, far.step)
    input_back = near.step(input_back)
    for other in earlier[2]:
        input_back = other.step(input_back)
    qkv_grad = after(qkv_grad, input_back)
    rows_back, grad_attn_gain = norm_back(rows, gains[0], input_back)
    return middle_grad + rows_back, value_grad, (far, near), qkv_grad, (grad_attn_gain, grad_ffn_gain)


def local(
    hidden_in, lengths, w_query, w_key, w_value, w_out, w_gate, w_up, w_down, attn_gain, ffn_gain,
    cotangent,
):
    place = Place()
    width = w_query.shape[2]
    cut = Cut(place, w_gate, w_out)
    tile = min(512, SLOTS)

    def mine_and_sent(x):
        mine = lax.dynamic_index_in_dim(x, place.row, 0, keepdims=False)
        sent = lax.dynamic_index_in_dim(x, 1 - place.row, 0, keepdims=False)
        return mine, sent

    count = hidden_in.shape[1] // 2
    mine, sent = mine_and_sent(hidden_in)
    half_block = lambda x: lax.dynamic_slice_in_dim(x, place.core * count, count, 0)
    far = place.around(half_block(sent), place.half)

    w_qkv = jnp.concatenate([w_query[0], w_key[0], w_value[0]], axis=1)
    part = lax.dynamic_slice_in_dim(w_qkv, place.dp * cut.columns, cut.columns, 0)
    share_1, share_2 = pack_weights(place, cut, w_gate[0], w_up[0], w_down[0], w_out[0])
    piece_1, piece_2 = (
        lax.dynamic_slice_in_dim(share, place.dp * cut.columns, cut.columns, 1)
        for share in (share_1, share_2)
    )
    own_gains = jnp.concatenate([attn_gain, ffn_gain])
    other_gains = place.swap(own_gains)
    gains_1 = place.pick(own_gains, other_gains)
    gains_2 = place.pick(other_gains, own_gains)

    begin, last, cosine, sine = slot_tables(
        lax.dynamic_index_in_dim(lengths, place.row, 0, keepdims=False)
    )
    repeat = min(128, width) // HD
    half_tables = (cosine[:, HD // 2 :].T, sine[:, HD // 2 :].T)
    tables = (
        jnp.tile(cosine, (1, repeat)), jnp.tile(sine, (1, repeat)), half_tables,
        begin[None], last[None], tile_tables(begin, tile), tile,
    )

    near = norm(half_block(mine).astype(F32), gains_1[0]).astype(BF16)
    near_shifted = [place.beside(near, shift) for shift in range(1, place.half)]
    chain_1 = Chain(spread_in_turn(place, cut, share_1, piece_1))
    chain_far = Chain(gather_far(place, far, gains_1[0]))
    chain_qkv = Chain(first_qkv(place, w_qkv, part))
    for _ in range(2):
        started = (chain_far, chain_qkv, chain_1)
        arrived = lax.optimization_barrier([chain.flight for chain in started])
        for chain, item in zip(started, arrived):
            chain.advance(item)
    (far, far_shifted), w_qkv_1 = chain_far.result, chain_qkv.result
    blocks = [
        join_halves(place, near, near_shifted),
        join_halves(place, norm(far.astype(F32), gains_1[0]).astype(BF16), far_shifted),
    ]
    gathered = place.by_row(*blocks)
    rows = place.pick(mine, place.by_core(far, place.swap(far), 0).reshape(mine.shape))
    rows = rows.astype(F32)
    result_1, values_1, spread_1, kept_1, (chain_2, chain_qkv) = layer_forward(
        place, rows, gathered, None, w_qkv_1, chain_1, gains_1, tables,
        (
            lambda x: spread_at_once(place, cut, share_2, after(piece_2, x)),
            lambda x: second_qkv(place, w_qkv, after(part, x)),
        ),
    )
    hidden_1 = result_1.astype(BF16)
    w_qkv_2 = chain_qkv.result
    rows = hidden_1.astype(F32)
    gathered = place.gather_row(norm(rows, gains_2[0]).astype(BF16))
    result_2, _, spread_2, kept_2, _ = layer_forward(
        place, rows, gathered, values_1, w_qkv_2, chain_2, gains_2, tables
    )
    hidden_2 = result_2.astype(BF16)

    mine, sent = mine_and_sent(cotangent)
    grad = place.pick(mine, place.across(sent.astype(BF16), 1).astype(F32))
    grad_2, carry, ffn_2, qkv_2, gain_2 = layer_backward(
        place, cut, grad, 0.5, None, w_qkv_2, spread_2, gains_2, kept_2, tables
    )
    grad_2 = grad_2.astype(BF16)
    far_2, near_2 = ffn_2
    qkv_2 = Chain(reduce_qkv(place, qkv_2, 1))

    def bring(first, second):
        near = place.to_core(second.astype(BF16), 1)
        near, *far = yield near, place.across(first.astype(BF16), 0), place.across(second.astype(BF16), 1)
        return near, place.pick(*far)

    def bring_one(block, core):
        moved = (place.across(block.astype(BF16), core),)
        moved = yield moved if core == 0 else (*moved, place.to_core(block.astype(BF16), 1))
        return moved

    def both_rows(near, far):
        return jnp.where(place.row == 0, jnp.stack([near, far]), jnp.stack([far, near]))[None]

    outputs = Chain(bring(hidden_1, hidden_2))
    grads_2 = Chain(bring_one(grad_2, 1))
    grad_1, _, (far_1, near_1), qkv_1, gain_1 = layer_backward(
        place, cut, grad_2.astype(F32), 1.0, carry, w_qkv_1, spread_1, gains_1, kept_1, tables,
        ((far_2, near_2, qkv_2), (near_2, qkv_2, outputs), (near_2, qkv_2, grads_2)),
    )

    def sum_gains(gains):
        gains = gains + (yield place.swap(gains))
        gains = gains + sum((yield [place.flip(gains, bits) for bits in range(1, place.data)]))
        return gains + sum((yield [place.around(gains, k) for k in range(1, place.size)]))

    grads_1 = Chain(bring_one(grad_1, 0))
    qkv_1 = Chain(reduce_qkv(place, qkv_1, 0))
    gains = Chain(sum_gains(jnp.stack([*gain_1, *gain_2])))
    _, ffn_1, qkv_1, gains, grads_1 = lockstep(far_1, near_1, qkv_1, gains, grads_1)

    ffn_2, qkv_2, grads_2 = near_2.result, qkv_2.result, grads_2.result
    near, far = outputs.result
    layer_outputs = both_rows(place.pick(hidden_1, near), far)
    near = place.pick(grad_1, grads_2[1].astype(F32))
    input_grads = both_rows(near, place.pick(grads_1[0], grads_2[0]).astype(F32))

    own = place.pick(ffn_1, ffn_2)
    other = place.swap(place.pick(ffn_2, ffn_1))
    qkv = place.pick(qkv_1, qkv_2).astype(BF16)
    flipped = [place.flip(qkv, bits) for bits in range(1, place.data)]
    other, flipped = lax.optimization_barrier((other, flipped))
    qkv = place.by_data(qkv, flipped).astype(F32).reshape(D, 3 * width)

    ffn = place.by_core(own, other, 0).astype(F32)
    units, outs = cut.units, cut.outs
    grad_gate = ffn[:, :units].reshape(-1, D).T
    grad_out = ffn[:, units : units + outs].reshape(-1, D)
    grad_down = ffn[:, units + outs : 2 * units + outs].reshape(-1, D)
    grad_up = ffn[:, 2 * units + outs :].reshape(-1, D).T
    gains = place.pick(gains[:2], gains[2:])
    return (
        layer_outputs, input_grads, *(qkv[None, :, i * width : (i + 1) * width] for i in range(3)), grad_out[None],
        grad_gate[None], grad_up[None], grad_down[None], gains[:1], gains[1:],
    )


def solution(mesh):
    in_specs = (
        P("dp", "head", None),
        P("dp", None),
        P("section", None, "head"),
        P("section", None, "head"),
        P("section", None, "head"),
        P("section", "head", None),
        P("section", None, "head"),
        P("section", None, "head"),
        P("section", "head", None),
        P("section", None),
        P("section", None),
        P("dp", "head", None),
    )
    out_specs = (
        P("section", "dp", "head", None),
        P("section", "dp", "head", None),
        P("section", None, "head"),
        P("section", None, "head"),
        P("section", None, "head"),
        P("section", "head", None),
        P("section", None, "head"),
        P("section", None, "head"),
        P("section", "head", None),
        P("section", None),
        P("section", None),
    )
    return jax.shard_map(local, mesh=mesh, in_specs=in_specs, out_specs=out_specs, check_vma=False)
```

```python
import functools

import jax
import jax.numpy as jnp
from jax import lax
from jax.experimental import pallas as pl
from jax.experimental.pallas import tpu as pltpu
from jax.sharding import PartitionSpec as P

D = 1024
HD = 64
SLOTS = 2048
PAD = 128

EPSILON = 1e-05
MASKED = -1e30
SCALE = HD ** (-0.5)
VMEM_LIMIT = 56 * 1024 * 1024


def lasting(microseconds):
    return pl.CostEstimate(flops=microseconds * 10**9, bytes_accessed=1, transcendentals=0)


F32 = jnp.float32
BF16 = jnp.bfloat16


def dot_nn(a, b):
    return lax.dot_general(a, b, (((1,), (0,)), ((), ())), preferred_element_type=F32)


def dot_nt(a, b):
    return lax.dot_general(a, b, (((1,), (1,)), ((), ())), preferred_element_type=F32)


def dot_tn(a, b):
    return lax.dot_general(a, b, (((0,), (0,)), ((), ())), preferred_element_type=F32)


def slot_tables(length_row):
    padded = (length_row + PAD - 1) // PAD * PAD
    starts = jnp.cumsum(padded) - padded
    slots = jnp.arange(SLOTS, dtype=jnp.int32)
    inside = (slots[:, None] >= starts[None, :]) & (slots[:, None] < (starts + padded)[None, :])
    begin = jnp.sum(jnp.where(inside, starts[None, :], 0), axis=1).astype(jnp.int32)
    end = jnp.sum(jnp.where(inside, (starts + length_row)[None, :], 0), axis=1).astype(jnp.int32)
    last = jnp.minimum(slots, end - 1)
    freq = 10000.0 ** (-2.0 * jnp.arange(HD // 2, dtype=F32) / HD)
    angle = (slots - begin).astype(F32)[:, None] * freq[None, :]
    cosine = jnp.concatenate([jnp.cos(angle), jnp.cos(angle)], axis=1)
    sine = jnp.concatenate([-jnp.sin(angle), jnp.sin(angle)], axis=1)
    return begin, last, cosine, sine


def tile_tables(begin, tile):
    count = SLOTS // tile
    index = jnp.arange(count, dtype=jnp.int32)
    low = begin[::tile]
    high = begin[tile - 1 :: tile]
    first = low // tile
    free = jnp.minimum((high + tile - 1) // tile, index)
    later = index[None, :] > index[:, None]
    free_end = index + 1 + jnp.sum(
        jnp.where(later & (high[None, :] <= index[:, None] * tile), 1, 0), axis=1
    )
    seen_end = index + 1 + jnp.sum(
        jnp.where(later & (low[None, :] < (index[:, None] + 1) * tile), 1, 0), axis=1
    )
    return jnp.stack([first, free, free_end.astype(jnp.int32), seen_end.astype(jnp.int32)])


def lane_in_head(shape):
    return lax.broadcasted_iota(jnp.int32, shape, 1) % HD


def turn(rows, cosine, sine):
    width = rows.shape[1]
    low = lane_in_head(rows.shape) < HD // 2
    if width == HD:
        swapped = jnp.concatenate([rows[:, HD // 2 :], rows[:, : HD // 2]], axis=1)
    else:
        swapped = jnp.where(
            low,
            pltpu.roll(rows, width - HD // 2, 1),
            pltpu.roll(rows, HD // 2, 1),
        )
    return rows * cosine + swapped * sine


def qkv_kernel(width, x_ref, w_ref, cos_ref, sin_ref, first_ref, q_ref, k_ref, v_ref, m_ref):
    product = dot_nn(x_ref[...], w_ref[...])
    repeat = width // cos_ref.shape[1]
    cosine = jnp.concatenate([cos_ref[...]] * repeat, axis=1)
    sine = jnp.concatenate([sin_ref[...]] * repeat, axis=1)
    q_ref[...] = (turn(product[:, :width], cosine, sine).astype(BF16).astype(F32) * SCALE).astype(BF16)
    k_ref[...] = turn(product[:, width : 2 * width], cosine, sine).astype(BF16)
    own = product[:, 2 * width :].astype(BF16)
    v_ref[...] = own
    if first_ref is not None:
        m_ref[...] = (0.5 * own.astype(F32) + 0.5 * first_ref[...].astype(F32)).astype(BF16)


def project(gathered, w_qkv, cosine, sine, first_values):
    width = w_qkv.shape[1] // 3
    tile = min(256, SLOTS)
    table = cosine.shape[1]
    row = lambda cols: pl.BlockSpec((tile, cols), lambda i: (i, 0))
    shape = jax.ShapeDtypeStruct((SLOTS, width), BF16)
    if first_values is None:
        kernel = lambda x, w, c, s, q, k, v: qkv_kernel(width, x, w, c, s, None, q, k, v, None)
        extra, specs, outs = (), [], 3
    else:
        kernel = functools.partial(qkv_kernel, width)
        extra, specs, outs = (first_values,), [row(width)], 4
    result = pl.pallas_call(
        kernel,
        grid=(SLOTS // tile,),
        in_specs=[
            row(D),
            pl.BlockSpec((D, 3 * width), lambda i: (0, 0)),
            row(table),
            row(table),
        ]
        + specs,
        out_specs=[row(width)] * outs,
        out_shape=[shape] * outs,
        compiler_params=pltpu.CompilerParams(vmem_limit_bytes=VMEM_LIMIT),
        cost_estimate=lasting(10),
        name="project",
    )(gathered, w_qkv, cosine, sine, *extra)
    return result if first_values is not None else (*result, result[2])


def head_mask(rows, width, head):
    lanes = lax.broadcasted_iota(jnp.int32, (rows, width), 1)
    return (lanes >= head * HD) & (lanes < (head + 1) * HD)


def attend_kernel(tile, heads, meta, q_ref, k_ref, vt_ref, low_ref, high_ref, o_ref, lse_ref, acc, peak, mass):
    width = heads * HD
    index = pl.program_id(0)
    q = q_ref[...]
    low = low_ref[...]
    high = high_ref[...]
    queries = [jnp.where(head_mask(tile, width, hh), q, jnp.zeros_like(q)) for hh in range(heads)]
    acc[...] = jnp.zeros_like(acc)
    peak[...] = jnp.full_like(peak, MASKED)
    mass[...] = jnp.zeros_like(mass)

    def step(kt, masked):
        start = pl.multiple_of(kt * tile, tile)
        keys = k_ref[pl.ds(start, tile), :]
        every = range(heads)
        rows = [slice(hh * HD, (hh + 1) * HD) for hh in every]
        scores = [dot_nt(keys, queries[hh]) for hh in every]
        if masked:
            slots = start + lax.broadcasted_iota(jnp.int32, scores[0].shape, 0)
            allowed = (slots >= low) & (slots <= high)
            scores = [jnp.where(allowed, x, MASKED) for x in scores]
        before = [peak[hh : hh + 1, :] for hh in every]
        tops = [jnp.maximum(before[hh], jnp.max(scores[hh], axis=0, keepdims=True)) for hh in every]
        weights = [jnp.exp(scores[hh] - tops[hh]) for hh in every]
        shrink = [jnp.exp(before[hh] - tops[hh]) for hh in every]
        sums = [
            mass[hh : hh + 1, :] * shrink[hh] + jnp.sum(weights[hh], axis=0, keepdims=True)
            for hh in every
        ]
        updates = [
            acc[rows[hh], :] * shrink[hh]
            + dot_nn(vt_ref[rows[hh], pl.ds(start, tile)], weights[hh].astype(BF16))
            for hh in every
        ]
        for hh in every:
            peak[hh : hh + 1, :] = tops[hh]
            mass[hh : hh + 1, :] = sums[hh]
            acc[rows[hh], :] = updates[hh]

    step(index, True)

    def masked_step(kt, carry):
        step(kt, True)
        return carry

    def free_step(kt, carry):
        step(kt, False)
        return carry

    lax.fori_loop(meta[0, index], meta[1, index], masked_step, 0)
    lax.fori_loop(meta[1, index], index, free_step, 0)
    for hh in range(heads):
        rows = slice(hh * HD, (hh + 1) * HD)
        acc[rows, :] = acc[rows, :] / mass[hh : hh + 1, :]
    o_ref[...] = acc[...].T.astype(BF16)
    lse_ref[...] = peak[...] + jnp.log(mass[...])


def attend(queries, keys, mixed, low, high, meta, tile):
    width = queries.shape[1]
    heads = width // HD
    whole = lambda shape: pl.BlockSpec(shape, lambda i, meta: (0, 0))
    return pl.pallas_call(
        functools.partial(attend_kernel, tile, heads),
        grid_spec=pltpu.PrefetchScalarGridSpec(
            num_scalar_prefetch=1,
            grid=(SLOTS // tile,),
            in_specs=[
                pl.BlockSpec((tile, width), lambda i, meta: (i, 0)),
                whole((SLOTS, width)),
                whole((width, SLOTS)),
                pl.BlockSpec((1, tile), lambda i, meta: (0, i)),
                pl.BlockSpec((1, tile), lambda i, meta: (0, i)),
            ],
            out_specs=[
                pl.BlockSpec((tile, width), lambda i, meta: (i, 0)),
                pl.BlockSpec((heads, tile), lambda i, meta: (0, i)),
            ],
            scratch_shapes=[
                pltpu.VMEM((width, tile), F32),
                pltpu.VMEM((heads, tile), F32),
                pltpu.VMEM((heads, tile), F32),
            ],
        ),
        out_shape=[
            jax.ShapeDtypeStruct((SLOTS, width), BF16),
            jax.ShapeDtypeStruct((heads, SLOTS), F32),
        ],
        compiler_params=pltpu.CompilerParams(vmem_limit_bytes=VMEM_LIMIT),
        cost_estimate=lasting(25),
        name="attend",
    )(meta, queries, keys, mixed.T, low, high)


def attend_back_kernel(
    tile, heads, share, meta, q_ref, k_ref, kt_ref, v_ref, do_ref, lse_ref, delta_ref, low_ref, high_ref,
    cos_ref, sin_ref, cost_ref, sint_ref, carry_ref, dq_ref, dk_ref, dv_ref, dqt, dk, dv
):
    width = heads * HD
    index = pl.program_id(0)
    count = pl.num_programs(0)

    @pl.when(index == 0)
    def _():
        dqt[...] = jnp.zeros_like(dqt)

    dk[...] = jnp.zeros_like(dk)
    dv[...] = jnp.zeros_like(dv)
    keys = k_ref[...]
    values = v_ref[...]
    key_start = index * tile
    masks = [head_mask(tile, width, hh) for hh in range(heads)]
    transposed = [kt_ref[hh * HD : (hh + 1) * HD, :] for hh in range(heads)]

    def step(qt, masked):
        start = pl.multiple_of(qt * tile, tile)
        here = pl.ds(start, tile)
        q = q_ref[here, :]
        do = do_ref[here, :]
        low = low_ref[:, here]
        high = high_ref[:, here]
        every = range(heads)
        rows = [slice(hh * HD, (hh + 1) * HD) for hh in every]
        q_h = [jnp.where(masks[hh], q, jnp.zeros_like(q)) for hh in every]
        do_h = [jnp.where(masks[hh], do, jnp.zeros_like(do)) for hh in every]
        scores = [dot_nt(keys, q_h[hh]) for hh in every]
        prob_grad = [dot_nt(values, do_h[hh]) for hh in every]
        if masked:
            slots = key_start + lax.broadcasted_iota(jnp.int32, scores[0].shape, 0)
            allowed = (slots >= low) & (slots <= high)
            scores = [jnp.where(allowed, x, MASKED) for x in scores]
        probs = [jnp.exp(scores[hh] - lse_ref[hh : hh + 1, here]) for hh in every]
        score_grad = [
            (probs[hh] * (prob_grad[hh] - delta_ref[hh : hh + 1, here])).astype(BF16)
            for hh in every
        ]
        dv[...] += sum(dot_nn(probs[hh].astype(BF16), do_h[hh]) for hh in every)
        dk[...] += sum(dot_nn(score_grad[hh], q_h[hh]) for hh in every)
        updates = [dqt[rows[hh], here] + dot_nn(transposed[hh], score_grad[hh]) for hh in every]
        for hh in every:
            dqt[rows[hh], here] = updates[hh]

    step(index, True)

    def masked_step(qt, carry):
        step(qt, True)
        return carry

    def free_step(qt, carry):
        step(qt, False)
        return carry

    lax.fori_loop(index + 1, meta[2, index], free_step, 0)
    lax.fori_loop(meta[2, index], meta[3, index], masked_step, 0)
    repeat = width // cos_ref.shape[1]
    cosine = jnp.concatenate([cos_ref[...]] * repeat, axis=1)
    sine = jnp.concatenate([sin_ref[...]] * repeat, axis=1)
    dk_ref[...] = turn(dk[...], cosine, -sine).astype(BF16)
    if carry_ref is None:
        dv_ref[...] = (share * dv[...]).astype(BF16)
    else:
        dv_ref[...] = (share * dv[...] + carry_ref[...].astype(F32)).astype(BF16)

    @pl.when(index == count - 1)
    def _():
        half = HD // 2

        def finish(qt, carry):
            here = pl.ds(pl.multiple_of(qt * tile, tile), tile)
            cosine_t = cost_ref[:, here] * SCALE
            sine_t = sint_ref[:, here] * SCALE
            parts = []
            for hh in range(heads):
                u1 = dqt[hh * HD : hh * HD + half, here]
                u2 = dqt[hh * HD + half : (hh + 1) * HD, here]
                parts.append(u1 * cosine_t + u2 * sine_t)
                parts.append(u2 * cosine_t - u1 * sine_t)
            dq_ref[here, :] = jnp.concatenate(parts, axis=0).T.astype(BF16)
            return carry

        lax.fori_loop(0, count, finish, 0)


def attend_back(queries, keys, mixed, out_grad, sums, delta, low, high, meta, cosine, sine, half_tables, share, carry, tile):
    width = queries.shape[1]
    heads = width // HD
    whole = lambda shape: pl.BlockSpec(shape, lambda i, meta: (0, 0))
    rows = lambda cols: pl.BlockSpec((tile, cols), lambda i, meta: (i, 0))
    table = cosine.shape[1]
    base = functools.partial(attend_back_kernel, tile, heads, share)
    if carry is None:
        kernel = lambda *refs: base(*refs[:14], None, *refs[14:])
        extra, specs = (), []
    else:
        kernel = base
        extra, specs = (carry,), [rows(width)]
    return pl.pallas_call(
        kernel,
        grid_spec=pltpu.PrefetchScalarGridSpec(
            num_scalar_prefetch=1,
            grid=(SLOTS // tile,),
            in_specs=[
                whole((SLOTS, width)),
                rows(width),
                pl.BlockSpec((width, tile), lambda i, meta: (0, i)),
                rows(width),
                whole((SLOTS, width)),
                whole((heads, SLOTS)),
                whole((heads, SLOTS)),
                whole((1, SLOTS)),
                whole((1, SLOTS)),
                rows(table),
                rows(table),
                whole((HD // 2, SLOTS)),
                whole((HD // 2, SLOTS)),
            ]
            + specs,
            out_specs=[whole((SLOTS, width)), rows(width), rows(width)],
            scratch_shapes=[
                pltpu.VMEM((width, SLOTS), F32),
                pltpu.VMEM((tile, width), F32),
                pltpu.VMEM((tile, width), F32),
            ],
        ),
        out_shape=[jax.ShapeDtypeStruct((SLOTS, width), BF16)] * 3,
        compiler_params=pltpu.CompilerParams(vmem_limit_bytes=VMEM_LIMIT),
        cost_estimate=lasting(36),
        name="attend_back",
    )(meta, queries, keys, keys.T, mixed, out_grad, sums, delta, low, high, cosine, sine, *half_tables, *extra)


class Place:
    def __init__(self):
        self.size = lax.axis_size("head")
        self.half = self.size // 2
        self.data = lax.axis_size("dp")
        self.core = lax.axis_index("section")
        self.dp = lax.axis_index("dp")
        self.head = lax.axis_index("head")
        self.row = self.head // self.half
        self.seat = self.head % self.half
        self.region = (self.row + self.core) % 2

    def swap(self, x):
        return lax.ppermute(x, "section", [(0, 1), (1, 0)])

    def to_core(self, x, core):
        return lax.ppermute(x, "section", [(1 - core, core)])

    def across(self, x, core):
        size, half = self.size, self.half
        pairs = [(size + h, core * size + (h + half) % size) for h in range(size)]
        return lax.ppermute(x, ("section", "head"), pairs)

    def across_from_zero(self, x):
        size, half = self.size, self.half
        pairs = [(h, size + (h + half) % size) for h in range(size)]
        return lax.ppermute(x, ("section", "head"), pairs)

    def beside(self, x, shift):
        half = self.half
        pairs = [(h, h // half * half + (h % half + shift) % half) for h in range(self.size)]
        return lax.ppermute(x, "head", pairs)

    def around(self, x, shift):
        return lax.ppermute(x, "head", [(h, (h + shift) % self.size) for h in range(self.size)])

    def flip(self, x, bits):
        return lax.ppermute(x, "dp", [(d, d ^ bits) for d in range(self.data)])

    def by_seat(self, own, shifted):
        blocks = jnp.zeros((self.half, *own.shape), own.dtype)
        blocks = lax.dynamic_update_index_in_dim(blocks, own, self.seat, 0)
        for shift, block in enumerate(shifted, 1):
            seat = (self.seat - shift) % self.half
            blocks = lax.dynamic_update_index_in_dim(blocks, block, seat, 0)
        return blocks

    def by_region(self, own, other):
        return jnp.where(
            self.region == 0, jnp.concatenate([own, other]), jnp.concatenate([other, own])
        )

    def gather_row(self, block):
        shifted = [self.beside(block, shift) for shift in range(1, self.half)]
        own = self.by_seat(block, shifted).reshape(-1, block.shape[1])
        return self.by_region(own, self.swap(own))

    def regions(self, rows):
        pair = rows.reshape(2, rows.shape[0] // 2, *rows.shape[1:])
        own = lax.dynamic_index_in_dim(pair, self.region, 0, keepdims=False)
        other = lax.dynamic_index_in_dim(pair, 1 - self.region, 0, keepdims=False)
        return own, other

    def seat_block(self, blocks, shift):
        return lax.dynamic_index_in_dim(blocks, (self.seat + shift) % self.half, 0, keepdims=False)

    def scatter_row(self, partial, tied):
        own, other = self.regions(partial)
        summed = own + self.swap(other.astype(BF16)).astype(F32)
        summed = tied(summed.reshape(self.half, -1, partial.shape[1]))
        total = self.seat_block(summed, 0)
        for shift in range(1, self.half):
            sent = self.seat_block(summed, shift).astype(BF16)
            total = total + self.beside(sent, shift).astype(F32)
        return total

    def heads_to_slots(self, rows):
        own, other = self.regions(rows)
        pair = jnp.stack([own, self.swap(other)])
        pair = pair.reshape(2, self.half, -1, rows.shape[1]).swapaxes(0, 1)
        shifted = [
            self.beside(self.seat_block(pair, shift), shift) for shift in range(1, self.half)
        ]
        blocks = self.by_seat(self.seat_block(pair, 0), shifted)
        blocks = self.by_region(blocks[:, 0], blocks[:, 1])
        return jnp.concatenate([blocks[i] for i in range(self.size)], axis=1)

    def slots_to_heads(self, block):
        width = block.shape[1] // self.size
        cut = jnp.stack([block[:, i * width : (i + 1) * width] for i in range(self.size)])
        own, other = self.regions(cut)
        pair = jnp.stack([own, other], axis=1)
        shifted = [
            self.beside(self.seat_block(pair, shift), shift) for shift in range(1, self.half)
        ]
        rows = self.by_seat(self.seat_block(pair, 0), shifted)
        return self.by_region(
            rows[:, 0].reshape(-1, width), self.swap(rows[:, 1].reshape(-1, width))
        )

    def data_block(self, x, bits):
        return lax.dynamic_index_in_dim(x, self.dp ^ bits, 0, keepdims=False)

    def by_data(self, own, flipped):
        blocks = jnp.zeros((self.data, *own.shape), own.dtype)
        blocks = lax.dynamic_update_index_in_dim(blocks, own, self.dp, 0)
        for bits, block in enumerate(flipped, 1):
            blocks = lax.dynamic_update_index_in_dim(blocks, block, self.dp ^ bits, 0)
        return blocks

    def gather_data(self, x):
        return self.by_data(x, [self.flip(x, bits) for bits in range(1, self.data)])

    def head_block(self, x, shift):
        return lax.dynamic_index_in_dim(x, (self.head + shift) % self.size, 0, keepdims=False)

    def scatter_heads(self, x):
        total = self.head_block(x, 0).astype(F32)
        for shift in range(1, self.size):
            sent = self.head_block(x, shift).astype(BF16)
            total = total + self.around(sent, shift).astype(F32)
        return total

    def spot(self):
        return jnp.stack([self.dp, self.head]).astype(jnp.int32)

    def by_core(self, own, other, axis):
        return jnp.where(
            self.core == 0, jnp.stack([own, other], axis), jnp.stack([other, own], axis)
        )

    def gather_cores(self, x):
        return self.by_core(x, self.swap(x), 0).reshape(-1, x.shape[1])

    def scatter_cores(self, partial):
        pair = partial.reshape(2, -1, partial.shape[1])
        own = lax.dynamic_index_in_dim(pair, self.core, 0, keepdims=False)
        other = lax.dynamic_index_in_dim(pair, 1 - self.core, 0, keepdims=False)
        return own + self.swap(other.astype(BF16)).astype(F32)

    def by_row(self, own, other):
        return jnp.where(
            self.row == 0, jnp.concatenate([own, other]), jnp.concatenate([other, own])
        )

    def pick(self, zero, one):
        return jnp.where(self.core == 0, zero, one)


class Chain:
    def __init__(self, stages):
        self.stages = stages
        self.result = None
        self.flight = next(stages)

    def advance(self, arrived):
        try:
            self.flight = self.stages.send(arrived)
        except StopIteration as stop:
            self.result = stop.value

    def step(self, x):
        x, arrived = lax.optimization_barrier((x, self.flight))
        self.advance(arrived)
        return x


def lockstep(*chains):
    while active := [chain for chain in chains if chain.result is None]:
        arrived = lax.optimization_barrier([chain.flight for chain in active])
        for chain, item in zip(active, arrived):
            chain.advance(item)
    return [chain.result for chain in chains]


def after(x, *others):
    return lax.optimization_barrier((x, *others))[0]


class Cut:
    def __init__(self, place, w_gate, w_out):
        self.heads = place.size
        self.units = w_gate.shape[2] // 2
        self.outs = w_out.shape[1] // 2
        self.rows = 3 * self.units + self.outs
        self.down = (self.rows // 2 - self.units - self.outs) // 16 * 16
        self.first = self.units + self.outs + self.down
        self.second = self.rows - self.first
        self.columns = D // place.data

    def part(self, share, place):
        return lax.dynamic_slice_in_dim(share, place.dp * self.columns, self.columns, 1)

    def pieces(self):
        units, outs, down = self.units, self.outs, self.down
        return (
            ("gate", 0, units, 0, 0),
            ("out", 0, outs, 0, units),
            ("down", 0, down, 0, units + outs),
            ("down", down, units - down, 1, 0),
            ("up", 0, units, 1, units - down),
        )


def pack_weights(place, w_gate, w_up, w_down, w_out):
    kinds = (w_gate.T, w_out, w_down, w_up.T)
    halves = [item.reshape(2, -1, D) for item in kinds]

    def half(core):
        return jnp.concatenate(
            [lax.dynamic_index_in_dim(item, core, 0, keepdims=False) for item in halves]
        )

    return half(place.core), half(1 - place.core)


def share_weights(place, cut, own, sent):
    piece = place.pick(cut.part(own, place), place.to_core(cut.part(sent, place), 1))
    other = place.swap(after(sent, piece))
    return place.pick(own, other), place.pick(other, own), piece


def any_specs(count):
    return [pl.BlockSpec(memory_space=pl.ANY)] * count


def run_copies(copies):
    for copy in copies:
        copy.start()
    for copy in copies:
        copy.wait()


def assemble_kernel(cut, groups, spot, share, *refs):
    dp, head = spot[0], spot[1]
    gu, down, out, sems = refs[5 * len(groups) :]
    kinds = {"gate": gu.at[0], "up": gu.at[1], "down": down, "out": out}
    copies = []

    def add(source, kind, step, row, count, columns):
        index = lax.rem(head - step + cut.heads, cut.heads) if kind == "out" else step
        target = kinds[kind].at[index, pl.ds(row, count), columns]
        copies.append(pltpu.make_async_copy(source, target, sems.at[len(copies)]))

    for kind, row, count, part, at in cut.pieces():
        base = at + part * cut.first
        add(share.at[pl.ds(base, count), :], kind, 0, row, count, slice(None))
    for number, steps in enumerate(groups):
        ring, first_x, second_y, first_y, second_x = refs[5 * number : 5 * number + 5]
        for i, step in enumerate(steps):
            firsts = (
                ring.at[i, pl.ds(0, cut.first)], first_x.at[i], first_y.at[0, i], first_y.at[1, i],
            )
            seconds = (
                ring.at[i, pl.ds(cut.first, cut.second)], second_x.at[0, i], second_y.at[i],
                second_x.at[1, i],
            )
            for bits in range(4):
                start = pl.multiple_of((dp ^ bits) * cut.columns, cut.columns)
                for kind, row, count, part, at in cut.pieces():
                    source = (firsts, seconds)[part][bits].at[pl.ds(at, count), :]
                    add(source, kind, step, row, count, pl.ds(start, cut.columns))
    run_copies(copies)


def near_flips(place, cut, ring):
    return place.flip(ring[:, : cut.first], 1), place.flip(ring[:, cut.first :], 2)


def far_flips(place, cut, ring, first_x, second_y):
    first = jnp.stack([ring[:, : cut.first], first_x])
    second = jnp.stack([ring[:, cut.first :], second_y])
    return place.flip(first, 2), place.flip(second, 1)


def fill_kernel(cut, spot, full, gu, down, out, sems):
    head = spot[1]
    kinds = {"gate": gu.at[0], "up": gu.at[1], "down": down, "out": out}
    copies = []
    for step in range(cut.heads):
        source = lax.rem(head - step + cut.heads, cut.heads)
        for part in range(D // cut.columns):
            columns = pl.ds(part * cut.columns, cut.columns)
            for kind, row, count, second, at in cut.pieces():
                index = source if kind == "out" else step
                block = full.at[part * cut.heads + source, pl.ds(at + second * cut.first, count), :]
                target = kinds[kind].at[index, pl.ds(row, count), columns]
                copies.append(pltpu.make_async_copy(block, target, sems.at[len(copies)]))
    run_copies(copies)


def spread_at_once(place, cut, piece):
    full = yield lax.all_gather(piece, ("dp", "head"), axis=0)
    return fill(place, cut, fill_kernel, 5 * place.data * cut.heads, (full,))


def spread_in_turn(place, cut, share, piece):
    size = cut.heads
    piece = yield place.around(piece, 1)
    ring_1 = piece[None]
    piece, near_1 = yield place.around(piece, 1), near_flips(place, cut, ring_1)
    ring = [piece]
    for _ in range(3, size):
        ring.append(place.around(ring[-1], 1))
    ring, far_1 = yield ring, far_flips(place, cut, ring_1, *near_1)
    ring = jnp.stack(ring)
    near = yield near_flips(place, cut, ring)
    far = yield far_flips(place, cut, ring, *near)
    groups = [([1], (ring_1, *near_1, *far_1)), (list(range(2, size)), (ring, *near, *far))]
    return assemble(place, cut, share, groups)


def first_qkv(place, w_qkv, part):
    flipped = yield [place.flip(part, bits) for bits in range(1, place.data)]
    return place.pick(w_qkv, place.by_data(part, flipped).reshape(w_qkv.shape))


def second_qkv(place, w_qkv):
    own, other = yield place.to_core(w_qkv, 0), place.across(w_qkv, 1)
    return place.pick(own, other)


def gather_far(place, far, gain):
    normed = norm(far.astype(F32), gain).astype(BF16)
    return (yield [place.beside(normed, shift) for shift in range(1, place.half)])


def assemble(place, cut, share, groups):
    steps = [group[0] for group in groups]
    parts = [part for group in groups for part in group[1]]
    kernel = lambda cut, *refs: assemble_kernel(cut, steps, *refs)
    return fill(place, cut, kernel, 5 * (1 + 4 * (cut.heads - 1)), (share, *parts))


def fill(place, cut, kernel, copies, sources):
    shape = lambda *dims: jax.ShapeDtypeStruct(dims, BF16)
    gate_up, down, out = pl.pallas_call(
        functools.partial(kernel, cut),
        in_specs=[pl.BlockSpec(memory_space=pltpu.SMEM)] + any_specs(len(sources)),
        out_specs=[pl.BlockSpec(memory_space=pltpu.VMEM)] * 3,
        out_shape=[
            shape(2, cut.heads, cut.units, D), shape(cut.heads, cut.units, D),
            shape(cut.heads, cut.outs, D),
        ],
        scratch_shapes=[pltpu.SemaphoreType.DMA((copies,))],
        compiler_params=pltpu.CompilerParams(vmem_limit_bytes=VMEM_LIMIT),
        cost_estimate=lasting(8),
        name="assemble",
    )(place.spot(), *sources)
    out = place.by_core(out, place.swap(out), 1).reshape(-1, D)
    return gate_up[0].reshape(-1, D), gate_up[1].reshape(-1, D), down.reshape(-1, D), out


def split_kernel(cut, chunks, spot, gate, up, down, out, *refs):
    dp, head = spot[0], spot[1]
    sems = refs[-1]
    kinds = {"gate": gate, "up": up, "down": down, "out": out}
    copies = []
    for number, steps in enumerate(chunks):
        first_kept, first_sent, second_kept, second_sent = refs[4 * number : 4 * number + 4]
        firsts = (first_kept.at[0], first_sent.at[0], first_kept.at[1], first_sent.at[1])
        seconds = (second_kept.at[0], second_kept.at[1], second_sent.at[0], second_sent.at[1])
        for bits in range(4):
            start = pl.multiple_of((dp ^ bits) * cut.columns, cut.columns)
            for i, step in enumerate(steps):
                for kind, row, count, part, at in cut.pieces():
                    index = step
                    if kind == "out":
                        index = lax.rem(head - step + cut.heads, cut.heads)
                    source = kinds[kind].at[index, pl.ds(row, count), pl.ds(start, cut.columns)]
                    target = (firsts, seconds)[part][bits].at[i, pl.ds(at, count), :]
                    copies.append(pltpu.make_async_copy(source, target, sems.at[len(copies)]))
    run_copies(copies)


def split_grads(place, cut, gate, up, down, out):
    half = cut.heads // 2
    chunks = [list(range(half, cut.heads)), list(range(half))]
    shape = lambda steps, rows: jax.ShapeDtypeStruct((2, len(steps), rows, cut.columns), BF16)
    shapes = []
    for steps in chunks:
        shapes += [shape(steps, cut.first)] * 2 + [shape(steps, cut.second)] * 2
    split = pl.pallas_call(
        functools.partial(split_kernel, cut, chunks),
        in_specs=[pl.BlockSpec(memory_space=pltpu.SMEM)]
        + [pl.BlockSpec(memory_space=pltpu.VMEM)] * 4,
        out_specs=any_specs(8),
        out_shape=shapes,
        scratch_shapes=[pltpu.SemaphoreType.DMA((20 * cut.heads,))],
        compiler_params=pltpu.CompilerParams(vmem_limit_bytes=VMEM_LIMIT),
        cost_estimate=lasting(8),
        name="split",
    )(place.spot(), *(item.reshape(cut.heads, -1, D) for item in (gate, up, down, out)))
    return split[:4], split[4:]


def exchange(place, part):
    first, second = yield place.flip(part[1], 1), place.flip(part[3], 2)
    first = part[0].astype(F32) + first.astype(F32)
    second = part[2].astype(F32) + second.astype(F32)
    moved = yield place.flip(first[1].astype(BF16), 2), place.flip(second[1].astype(BF16), 1)
    kept = first[0], second[0]
    return jnp.concatenate([x + y.astype(F32) for x, y in zip(kept, moved)], axis=1)


def reduce_far(place, cut, part):
    half = cut.heads // 2
    blocks = yield from exchange(place, part)
    arrived = yield [
        place.around(blocks[step - half].astype(BF16), -step) for step in range(half, cut.heads)
    ]
    return sum(item.astype(F32) for item in arrived)


def reduce_near(place, cut, part, far):
    blocks = yield from exchange(place, part)
    total = blocks[0]
    if cut.heads > 2:
        arrived = yield [
            place.around(blocks[step].astype(BF16), -step) for step in range(1, cut.heads // 2)
        ]
        total = total + sum(item.astype(F32) for item in arrived)
    total = (total + far.result).astype(BF16)
    flipped = yield [place.flip(total, bits) for bits in range(1, place.data)]
    parts = place.by_data(total, flipped)
    return jnp.concatenate([parts[d] for d in range(place.data)], axis=1)


def reduce_qkv(place, grad, core, second_layer):
    grad = grad.reshape(place.data, 2, -1, grad.shape[1])
    first, second = grad[:, 0], grad[:, 1]
    sent = [
        jnp.stack([place.data_block(x, bits) for bits in pair])
        for x, pair in ((first, (1, 3)), (second, (2, 3)))
    ]
    kept = [
        jnp.stack([place.data_block(x, bits) for bits in pair])
        for x, pair in ((first, (0, 2)), (second, (0, 1)))
    ]
    arrived = yield place.flip(sent[0], 1), place.flip(sent[1], 2)
    first, second = (a.astype(F32) + b.astype(F32) for a, b in zip(kept, arrived))
    arrived = yield place.flip(first[1].astype(BF16), 2), place.flip(second[1].astype(BF16), 1)
    piece = jnp.concatenate([first[0] + arrived[0].astype(F32), second[0] + arrived[1].astype(F32)])
    piece = piece.astype(BF16)
    if core == 0:
        other = yield place.across(piece, 0)
        first = (piece.astype(F32) + other.astype(F32)).astype(BF16)
        summed = place.pick(first, second_layer())
        flipped = yield [place.flip(summed, bits) for bits in range(1, place.data)]
        return place.by_data(summed, flipped).astype(F32).reshape(D, -1)
    own, other = yield place.to_core(piece, 1), place.across(piece, 1)
    return (own.astype(F32) + other.astype(F32)).astype(BF16)


def norm(rows, gain):
    inverse = lax.rsqrt(jnp.mean(rows * rows, axis=1, keepdims=True) + EPSILON)
    return rows * inverse * gain


def norm_back(rows, gain, grad):
    inverse = lax.rsqrt(jnp.mean(rows * rows, axis=1, keepdims=True) + EPSILON)
    scaled = grad * gain
    gain_grad = jnp.sum(grad * rows * inverse, axis=0)
    rows_grad = inverse * scaled - rows * inverse**3 * jnp.mean(
        scaled * rows, axis=1, keepdims=True
    )
    return rows_grad, gain_grad


def layer_forward(place, rows, gathered, first_values, w_qkv, chain, gains, tables, later=()):
    cosine, sine, half_tables, low, high, meta, tile = tables
    if later:
        gathered = chain.step(chain.step(gathered))
    later = [Chain(begin(gathered)) for begin in later]
    queries, keys, own_values, mixed = project(gathered, w_qkv, cosine, sine, first_values)
    queries = chain.step(queries)
    attended_heads, sums = attend(queries, keys, mixed, low, high, meta, tile)
    for other in (chain, *later[1:]) if later else ():
        attended_heads = other.step(attended_heads)
    attended = place.heads_to_slots(attended_heads)
    gate_w, up_w, down_w, out_w = spread = chain.result
    middle = rows + dot_nn(attended, out_w)
    ffn_normed = place.gather_cores(norm(middle, gains[1]).astype(BF16))
    gate = dot_nt(ffn_normed, gate_w)
    up = dot_nt(ffn_normed, up_w)
    activation = (jax.nn.silu(gate) * up).astype(BF16)
    result = middle + place.scatter_cores(dot_nn(activation, down_w))
    kept = (
        rows, gathered, queries, keys, mixed, attended_heads, sums, attended, middle, ffn_normed,
        gate, up, activation,
    )
    return result, own_values, spread, kept, later


def join_halves(place, x, shifted):
    own = place.by_seat(x, shifted)
    return place.by_core(own, place.swap(own), 1).reshape(-1, x.shape[1])


def layer_backward(place, cut, grad, share, carry, w_qkv, spread, gains, kept, tables, layer, earlier, second_layer=None):
    cosine, sine, half_tables, low, high, meta, tile = tables
    gate_w, up_w, down_w, out_w = spread
    (
        rows, gathered, queries, keys, mixed, attended_heads, sums, attended, middle, ffn_normed,
        gate, up, activation,
    ) = kept
    down_grad = place.gather_cores(grad.astype(BF16))
    act_grad = dot_nt(down_grad, down_w)
    sigma = jax.nn.sigmoid(gate)
    gate_grad = (act_grad * up * sigma * (1.0 + gate * (1.0 - sigma))).astype(BF16)
    up_grad = (act_grad * gate * sigma).astype(BF16)
    for other in earlier[0]:
        up_grad = other.step(up_grad)
    normed_grad = place.scatter_cores(dot_nn(gate_grad, gate_w) + dot_nn(up_grad, up_w))
    middle_back, grad_ffn_gain = norm_back(middle, gains[1], normed_grad)
    middle_grad = grad + middle_back
    attn_grad = middle_grad.astype(BF16)
    attended_grad = dot_nt(attn_grad, out_w).astype(BF16)
    heads_grad = place.slots_to_heads(attended_grad)
    gate_grad, up_grad, activation = after((gate_grad, up_grad, activation), attended_grad)
    out_grad = dot_tn(attended, attn_grad).reshape(place.size, 2, -1, D).swapaxes(0, 1)
    out_grad = place.scatter_cores(out_grad.reshape(-1, D))
    split = split_grads(
        place, cut, dot_tn(gate_grad, ffn_normed).astype(BF16),
        dot_tn(up_grad, ffn_normed).astype(BF16), dot_tn(activation, down_grad).astype(BF16),
        out_grad.astype(BF16),
    )
    heads_grad = after(heads_grad, *split[0], *split[1])
    for other in earlier[1]:
        heads_grad = other.step(heads_grad)
    far = Chain(reduce_far(place, cut, split[0]))
    near = Chain(reduce_near(place, cut, split[1], far))
    delta = heads_grad.astype(F32) * attended_heads.astype(F32)
    delta = jnp.sum(delta.reshape(SLOTS, -1, HD), axis=2).T
    query_grad, key_grad, value_grad = attend_back(
        queries, keys, mixed, heads_grad, sums, delta, low, high, meta, cosine, sine, half_tables,
        share, carry, tile,
    )
    for other in (far, near, *earlier[2]):
        query_grad = other.step(query_grad)
    lin_grad = jnp.concatenate([query_grad, key_grad, value_grad], axis=1)
    partial = dot_nt(lin_grad, w_qkv)
    qkv_grad = dot_tn(gathered, after(lin_grad, partial)).astype(BF16)
    qkv_grad = Chain(reduce_qkv(place, qkv_grad, layer, second_layer))
    input_back = place.scatter_row(partial, lambda x: qkv_grad.step(far.step(x)))
    for other in (near, qkv_grad, far) if layer == 0 else (near, qkv_grad):
        input_back = other.step(input_back)
    rows_back, grad_attn_gain = norm_back(rows, gains[0], input_back)
    return middle_grad + rows_back, value_grad, (far, near), qkv_grad, (grad_attn_gain, grad_ffn_gain)


def local(
    hidden_in, lengths, w_query, w_key, w_value, w_out, w_gate, w_up, w_down, attn_gain, ffn_gain,
    cotangent,
):
    place = Place()
    width = w_query.shape[2]
    cut = Cut(place, w_gate, w_out)
    tile = min(512, SLOTS)

    def mine_and_sent(x):
        mine = lax.dynamic_index_in_dim(x, place.row, 0, keepdims=False)
        sent = lax.dynamic_index_in_dim(x, 1 - place.row, 0, keepdims=False)
        return mine, sent

    count = hidden_in.shape[1] // 2
    mine, sent = mine_and_sent(hidden_in)
    half_block = lambda x: lax.dynamic_slice_in_dim(x, place.core * count, count, 0)
    far = place.around(half_block(sent), place.half)
    w_qkv = jnp.concatenate([w_query[0], w_key[0], w_value[0]], axis=1)
    part = lax.dynamic_slice_in_dim(w_qkv, place.dp * cut.columns, cut.columns, 0)
    part_1 = place.across_from_zero(part)
    own_packed, sent_packed = pack_weights(place, w_gate[0], w_up[0], w_down[0], w_out[0])
    own_gains = jnp.concatenate([attn_gain, ffn_gain])
    other_gains = place.swap(own_gains)
    gains_1 = place.pick(own_gains, other_gains)
    gains_2 = place.pick(other_gains, own_gains)

    begin, last, cosine, sine = slot_tables(
        lax.dynamic_index_in_dim(lengths, place.row, 0, keepdims=False)
    )
    repeat = min(128, width) // HD
    half_tables = (cosine[:, HD // 2 :].T, sine[:, HD // 2 :].T)
    tables = (
        jnp.tile(cosine, (1, repeat)), jnp.tile(sine, (1, repeat)), half_tables,
        begin[None], last[None], tile_tables(begin, tile), tile,
    )

    near = norm(half_block(mine).astype(F32), gains_1[0]).astype(BF16)
    near_shifted = [place.beside(near, shift) for shift in range(1, place.half)]
    far, part_1, own_packed, sent_packed = lax.optimization_barrier(
        (far, part_1, own_packed, sent_packed)
    )
    share_1, share_2, piece_1 = share_weights(place, cut, own_packed, sent_packed)
    piece_2 = cut.part(share_2, place)
    chain_far = Chain(gather_far(place, far, gains_1[0]))
    chain_1 = Chain(spread_in_turn(place, cut, share_1, piece_1))
    chain_qkv = Chain(first_qkv(place, w_qkv, part_1))
    started = (chain_far, chain_qkv, chain_1)
    arrived = lax.optimization_barrier([chain.flight for chain in started])
    for chain, item in zip(started, arrived):
        chain.advance(item)
    far_shifted, w_qkv_1 = chain_far.result, chain_qkv.result
    blocks = [
        join_halves(place, near, near_shifted),
        join_halves(place, norm(far.astype(F32), gains_1[0]).astype(BF16), far_shifted),
    ]
    gathered = place.by_row(*blocks)
    rows = place.pick(mine, place.by_core(far, place.swap(far), 0).reshape(mine.shape))
    rows = rows.astype(F32)
    result_1, values_1, spread_1, kept_1, (chain_2, chain_qkv) = layer_forward(
        place, rows, gathered, None, w_qkv_1, chain_1, gains_1, tables,
        (
            lambda x: spread_at_once(place, cut, after(piece_2, x)),
            lambda x: second_qkv(place, after(w_qkv, x)),
        ),
    )
    hidden_1 = result_1.astype(BF16)
    rows = hidden_1.astype(F32)
    gathered = place.gather_row(norm(rows, gains_2[0]).astype(BF16))
    w_qkv_2 = chain_qkv.result
    result_2, _, spread_2, kept_2, _ = layer_forward(
        place, rows, gathered, values_1, w_qkv_2, chain_2, gains_2, tables
    )
    hidden_2 = result_2.astype(BF16)

    def bring(first, second):
        near = place.to_core(second.astype(BF16), 1)
        near, *far = yield near, place.across(first.astype(BF16), 0), place.across(second.astype(BF16), 1)
        return near, place.pick(*far)

    outputs = Chain(bring(hidden_1, hidden_2))
    mine, sent = mine_and_sent(cotangent)
    grad = place.pick(mine, place.across(sent.astype(BF16), 1).astype(F32))
    grad_2, carry, ffn_2, qkv_2, gain_2 = layer_backward(
        place, cut, grad, 0.5, None, w_qkv_2, spread_2, gains_2, kept_2, tables, 1,
        ((), (), (outputs,)),
    )
    grad_2 = grad_2.astype(BF16)
    far_2, near_2 = ffn_2

    def bring_one(block, core, wait=0):
        for _ in range(wait):
            block = yield block
        moved = (place.across(block.astype(BF16), core),)
        moved = yield moved if core == 0 else (*moved, place.to_core(block.astype(BF16), 1))
        return moved

    def both_rows(near, far):
        return jnp.where(place.row == 0, jnp.stack([near, far]), jnp.stack([far, near]))[None]

    grads_2 = Chain(bring_one(grad_2, 1))
    grad_1, _, (far_1, near_1), qkv_1, gain_1 = layer_backward(
        place, cut, grad_2.astype(F32), 1.0, carry, w_qkv_1, spread_1, gains_1, kept_1, tables, 0,
        ((far_2, near_2, qkv_2), (near_2, grads_2), ()), lambda: qkv_2.result,
    )

    def sum_gains(gains):
        gains = gains + (yield place.swap(gains))
        gains = gains + sum((yield [place.flip(gains, bits) for bits in range(1, place.data)]))
        return gains + sum((yield [place.around(gains, k) for k in range(1, place.size)]))

    grads_1 = Chain(bring_one(grad_1, 0, 1))
    gains = Chain(sum_gains(jnp.stack([*gain_1, *gain_2])))
    ffn_1, qkv_1, gains, grads_1 = lockstep(near_1, qkv_1, gains, grads_1)

    ffn_2, grads_2 = near_2.result, grads_2.result
    near, far = outputs.result
    layer_outputs = both_rows(place.pick(hidden_1, near), far)
    near = place.pick(grad_1, grads_2[1].astype(F32))
    input_grads = both_rows(near, place.pick(grads_1[0], grads_2[0]).astype(F32))

    own = place.pick(ffn_1, ffn_2)
    other = place.swap(place.pick(ffn_2, ffn_1))
    ffn = place.by_core(own, other, 0).astype(F32)
    units, outs = cut.units, cut.outs
    grad_gate = ffn[:, :units].reshape(-1, D).T
    grad_out = ffn[:, units : units + outs].reshape(-1, D)
    grad_down = ffn[:, units + outs : 2 * units + outs].reshape(-1, D)
    grad_up = ffn[:, 2 * units + outs :].reshape(-1, D).T
    gains = place.pick(gains[:2], gains[2:])
    return (
        layer_outputs, input_grads, *(qkv_1[None, :, i * width : (i + 1) * width] for i in range(3)), grad_out[None],
        grad_gate[None], grad_up[None], grad_down[None], gains[:1], gains[1:],
    )


def solution(mesh):
    in_specs = (
        P("dp", "head", None),
        P("dp", None),
        P("section", None, "head"),
        P("section", None, "head"),
        P("section", None, "head"),
        P("section", "head", None),
        P("section", None, "head"),
        P("section", None, "head"),
        P("section", "head", None),
        P("section", None),
        P("section", None),
        P("dp", "head", None),
    )
    out_specs = (
        P("section", "dp", "head", None),
        P("section", "dp", "head", None),
        P("section", None, "head"),
        P("section", None, "head"),
        P("section", None, "head"),
        P("section", "head", None),
        P("section", None, "head"),
        P("section", None, "head"),
        P("section", "head", None),
        P("section", None),
        P("section", None),
    )
    return jax.shard_map(local, mesh=mesh, in_specs=in_specs, out_specs=out_specs, check_vma=False)
```

```python
import functools

import jax
import jax.numpy as jnp
from jax import lax
from jax.experimental import pallas as pl
from jax.experimental.pallas import tpu as pltpu
from jax.sharding import PartitionSpec as P

D = 1024
HD = 64
SLOTS = 2048
PAD = 128

EPSILON = 1e-05
MASKED = -1e30
SCALE = HD ** (-0.5)
VMEM_LIMIT = 56 * 1024 * 1024


def lasting(microseconds):
    return pl.CostEstimate(flops=microseconds * 10**9, bytes_accessed=1, transcendentals=0)


F32 = jnp.float32
BF16 = jnp.bfloat16


def dot_nn(a, b):
    return lax.dot_general(a, b, (((1,), (0,)), ((), ())), preferred_element_type=F32)


def dot_nt(a, b):
    return lax.dot_general(a, b, (((1,), (1,)), ((), ())), preferred_element_type=F32)


def dot_tn(a, b):
    return lax.dot_general(a, b, (((0,), (0,)), ((), ())), preferred_element_type=F32)


def slot_tables(length_row):
    padded = (length_row + PAD - 1) // PAD * PAD
    starts = jnp.cumsum(padded) - padded
    slots = jnp.arange(SLOTS, dtype=jnp.int32)
    inside = (slots[:, None] >= starts[None, :]) & (slots[:, None] < (starts + padded)[None, :])
    begin = jnp.sum(jnp.where(inside, starts[None, :], 0), axis=1).astype(jnp.int32)
    end = jnp.sum(jnp.where(inside, (starts + length_row)[None, :], 0), axis=1).astype(jnp.int32)
    last = jnp.minimum(slots, end - 1)
    freq = 10000.0 ** (-2.0 * jnp.arange(HD // 2, dtype=F32) / HD)
    angle = (slots - begin).astype(F32)[:, None] * freq[None, :]
    cosine = jnp.concatenate([jnp.cos(angle), jnp.cos(angle)], axis=1)
    sine = jnp.concatenate([-jnp.sin(angle), jnp.sin(angle)], axis=1)
    return begin, last, cosine, sine


def tile_tables(begin, tile):
    count = SLOTS // tile
    index = jnp.arange(count, dtype=jnp.int32)
    low = begin[::tile]
    high = begin[tile - 1 :: tile]
    first = low // tile
    free = jnp.minimum((high + tile - 1) // tile, index)
    later = index[None, :] > index[:, None]
    free_end = index + 1 + jnp.sum(
        jnp.where(later & (high[None, :] <= index[:, None] * tile), 1, 0), axis=1
    )
    seen_end = index + 1 + jnp.sum(
        jnp.where(later & (low[None, :] < (index[:, None] + 1) * tile), 1, 0), axis=1
    )
    return jnp.stack([first, free, free_end.astype(jnp.int32), seen_end.astype(jnp.int32)])


def lane_in_head(shape):
    return lax.broadcasted_iota(jnp.int32, shape, 1) % HD


def turn(rows, cosine, sine):
    width = rows.shape[1]
    low = lane_in_head(rows.shape) < HD // 2
    if width == HD:
        swapped = jnp.concatenate([rows[:, HD // 2 :], rows[:, : HD // 2]], axis=1)
    else:
        swapped = jnp.where(
            low,
            pltpu.roll(rows, width - HD // 2, 1),
            pltpu.roll(rows, HD // 2, 1),
        )
    return rows * cosine + swapped * sine


def qkv_kernel(width, x_ref, w_ref, cos_ref, sin_ref, first_ref, q_ref, k_ref, v_ref, m_ref):
    product = dot_nn(x_ref[...], w_ref[...])
    repeat = width // cos_ref.shape[1]
    cosine = jnp.concatenate([cos_ref[...]] * repeat, axis=1)
    sine = jnp.concatenate([sin_ref[...]] * repeat, axis=1)
    q_ref[...] = (turn(product[:, :width], cosine, sine).astype(BF16).astype(F32) * SCALE).astype(BF16)
    k_ref[...] = turn(product[:, width : 2 * width], cosine, sine).astype(BF16)
    own = product[:, 2 * width :].astype(BF16)
    v_ref[...] = own
    if first_ref is not None:
        m_ref[...] = (0.5 * own.astype(F32) + 0.5 * first_ref[...].astype(F32)).astype(BF16)


def project(gathered, w_qkv, cosine, sine, first_values):
    width = w_qkv.shape[1] // 3
    tile = min(256, SLOTS)
    table = cosine.shape[1]
    row = lambda cols: pl.BlockSpec((tile, cols), lambda i: (i, 0))
    shape = jax.ShapeDtypeStruct((SLOTS, width), BF16)
    if first_values is None:
        kernel = lambda x, w, c, s, q, k, v: qkv_kernel(width, x, w, c, s, None, q, k, v, None)
        extra, specs, outs = (), [], 3
    else:
        kernel = functools.partial(qkv_kernel, width)
        extra, specs, outs = (first_values,), [row(width)], 4
    result = pl.pallas_call(
        kernel,
        grid=(SLOTS // tile,),
        in_specs=[
            row(D),
            pl.BlockSpec((D, 3 * width), lambda i: (0, 0)),
            row(table),
            row(table),
        ]
        + specs,
        out_specs=[row(width)] * outs,
        out_shape=[shape] * outs,
        compiler_params=pltpu.CompilerParams(vmem_limit_bytes=VMEM_LIMIT),
        cost_estimate=lasting(10),
        name="project",
    )(gathered, w_qkv, cosine, sine, *extra)
    return result if first_values is not None else (*result, result[2])


def head_mask(rows, width, head):
    lanes = lax.broadcasted_iota(jnp.int32, (rows, width), 1)
    return (lanes >= head * HD) & (lanes < (head + 1) * HD)


def attend_kernel(tile, heads, meta, q_ref, k_ref, vt_ref, low_ref, high_ref, o_ref, lse_ref, acc, peak, mass):
    width = heads * HD
    index = pl.program_id(0)
    q = q_ref[...]
    low = low_ref[...]
    high = high_ref[...]
    queries = [jnp.where(head_mask(tile, width, hh), q, jnp.zeros_like(q)) for hh in range(heads)]
    acc[...] = jnp.zeros_like(acc)
    peak[...] = jnp.full_like(peak, MASKED)
    mass[...] = jnp.zeros_like(mass)

    def step(kt, masked):
        start = pl.multiple_of(kt * tile, tile)
        keys = k_ref[pl.ds(start, tile), :]
        every = range(heads)
        rows = [slice(hh * HD, (hh + 1) * HD) for hh in every]
        scores = [dot_nt(keys, queries[hh]) for hh in every]
        if masked:
            slots = start + lax.broadcasted_iota(jnp.int32, scores[0].shape, 0)
            allowed = (slots >= low) & (slots <= high)
            scores = [jnp.where(allowed, x, MASKED) for x in scores]
        before = [peak[hh : hh + 1, :] for hh in every]
        tops = [jnp.maximum(before[hh], jnp.max(scores[hh], axis=0, keepdims=True)) for hh in every]
        weights = [jnp.exp(scores[hh] - tops[hh]) for hh in every]
        shrink = [jnp.exp(before[hh] - tops[hh]) for hh in every]
        sums = [
            mass[hh : hh + 1, :] * shrink[hh] + jnp.sum(weights[hh], axis=0, keepdims=True)
            for hh in every
        ]
        updates = [
            acc[rows[hh], :] * shrink[hh]
            + dot_nn(vt_ref[rows[hh], pl.ds(start, tile)], weights[hh].astype(BF16))
            for hh in every
        ]
        for hh in every:
            peak[hh : hh + 1, :] = tops[hh]
            mass[hh : hh + 1, :] = sums[hh]
            acc[rows[hh], :] = updates[hh]

    step(index, True)

    def masked_step(kt, carry):
        step(kt, True)
        return carry

    def free_step(kt, carry):
        step(kt, False)
        return carry

    lax.fori_loop(meta[0, index], meta[1, index], masked_step, 0)
    lax.fori_loop(meta[1, index], index, free_step, 0)
    for hh in range(heads):
        rows = slice(hh * HD, (hh + 1) * HD)
        acc[rows, :] = acc[rows, :] / mass[hh : hh + 1, :]
    o_ref[...] = acc[...].T.astype(BF16)
    lse_ref[...] = peak[...] + jnp.log(mass[...])


def attend(queries, keys, mixed, low, high, meta, tile):
    width = queries.shape[1]
    heads = width // HD
    whole = lambda shape: pl.BlockSpec(shape, lambda i, meta: (0, 0))
    return pl.pallas_call(
        functools.partial(attend_kernel, tile, heads),
        grid_spec=pltpu.PrefetchScalarGridSpec(
            num_scalar_prefetch=1,
            grid=(SLOTS // tile,),
            in_specs=[
                pl.BlockSpec((tile, width), lambda i, meta: (i, 0)),
                whole((SLOTS, width)),
                whole((width, SLOTS)),
                pl.BlockSpec((1, tile), lambda i, meta: (0, i)),
                pl.BlockSpec((1, tile), lambda i, meta: (0, i)),
            ],
            out_specs=[
                pl.BlockSpec((tile, width), lambda i, meta: (i, 0)),
                pl.BlockSpec((heads, tile), lambda i, meta: (0, i)),
            ],
            scratch_shapes=[
                pltpu.VMEM((width, tile), F32),
                pltpu.VMEM((heads, tile), F32),
                pltpu.VMEM((heads, tile), F32),
            ],
        ),
        out_shape=[
            jax.ShapeDtypeStruct((SLOTS, width), BF16),
            jax.ShapeDtypeStruct((heads, SLOTS), F32),
        ],
        compiler_params=pltpu.CompilerParams(vmem_limit_bytes=VMEM_LIMIT),
        cost_estimate=lasting(25),
        name="attend",
    )(meta, queries, keys, mixed.T, low, high)


def attend_back_kernel(
    tile, heads, share, meta, q_ref, k_ref, kt_ref, v_ref, do_ref, o_ref, lse_ref, low_ref, high_ref,
    cos_ref, sin_ref, cost_ref, sint_ref, carry_ref, dq_ref, dk_ref, dv_ref, dqt, dk, dv, delta_ref
):
    width = heads * HD
    index = pl.program_id(0)
    count = pl.num_programs(0)

    @pl.when(index == 0)
    def _():
        dqt[...] = jnp.zeros_like(dqt)
        lanes = lax.broadcasted_iota(jnp.int32, (delta_ref.shape[0], width), 1)
        owner = lax.broadcasted_iota(jnp.int32, (delta_ref.shape[0], width), 0)
        select = jnp.where(
            (lanes >= owner * HD) & (lanes < (owner + 1) * HD), 1.0, 0.0
        ).astype(F32)

        def row_sums(qt, carry):
            here = pl.ds(pl.multiple_of(qt * tile, tile), tile)
            product = do_ref[here, :].astype(F32) * o_ref[here, :].astype(F32)
            delta_ref[:, here] = lax.dot_general(
                select, product, (((1,), (1,)), ((), ())), precision=lax.Precision.HIGHEST,
                preferred_element_type=F32,
            )
            return carry

        lax.fori_loop(0, count, row_sums, 0)

    dk[...] = jnp.zeros_like(dk)
    dv[...] = jnp.zeros_like(dv)
    keys = k_ref[...]
    values = v_ref[...]
    key_start = index * tile
    masks = [head_mask(tile, width, hh) for hh in range(heads)]
    transposed = [kt_ref[hh * HD : (hh + 1) * HD, :] for hh in range(heads)]

    def step(qt, masked):
        start = pl.multiple_of(qt * tile, tile)
        here = pl.ds(start, tile)
        q = q_ref[here, :]
        do = do_ref[here, :]
        low = low_ref[:, here]
        high = high_ref[:, here]
        every = range(heads)
        rows = [slice(hh * HD, (hh + 1) * HD) for hh in every]
        q_h = [jnp.where(masks[hh], q, jnp.zeros_like(q)) for hh in every]
        do_h = [jnp.where(masks[hh], do, jnp.zeros_like(do)) for hh in every]
        scores = [dot_nt(keys, q_h[hh]) for hh in every]
        prob_grad = [dot_nt(values, do_h[hh]) for hh in every]
        if masked:
            slots = key_start + lax.broadcasted_iota(jnp.int32, scores[0].shape, 0)
            allowed = (slots >= low) & (slots <= high)
            scores = [jnp.where(allowed, x, MASKED) for x in scores]
        probs = [jnp.exp(scores[hh] - lse_ref[hh : hh + 1, here]) for hh in every]
        score_grad = [
            (probs[hh] * (prob_grad[hh] - delta_ref[hh : hh + 1, here])).astype(BF16)
            for hh in every
        ]
        dv[...] += sum(dot_nn(probs[hh].astype(BF16), do_h[hh]) for hh in every)
        dk[...] += sum(dot_nn(score_grad[hh], q_h[hh]) for hh in every)
        updates = [dqt[rows[hh], here] + dot_nn(transposed[hh], score_grad[hh]) for hh in every]
        for hh in every:
            dqt[rows[hh], here] = updates[hh]

    step(index, True)

    def masked_step(qt, carry):
        step(qt, True)
        return carry

    def free_step(qt, carry):
        step(qt, False)
        return carry

    lax.fori_loop(index + 1, meta[2, index], free_step, 0)
    lax.fori_loop(meta[2, index], meta[3, index], masked_step, 0)
    repeat = width // cos_ref.shape[1]
    cosine = jnp.concatenate([cos_ref[...]] * repeat, axis=1)
    sine = jnp.concatenate([sin_ref[...]] * repeat, axis=1)
    dk_ref[...] = turn(dk[...], cosine, -sine).astype(BF16)
    if carry_ref is None:
        dv_ref[...] = (share * dv[...]).astype(BF16)
    else:
        dv_ref[...] = (share * dv[...] + carry_ref[...].astype(F32)).astype(BF16)

    @pl.when(index == count - 1)
    def _():
        half = HD // 2

        def finish(qt, carry):
            here = pl.ds(pl.multiple_of(qt * tile, tile), tile)
            cosine_t = cost_ref[:, here] * SCALE
            sine_t = sint_ref[:, here] * SCALE
            parts = []
            for hh in range(heads):
                u1 = dqt[hh * HD : hh * HD + half, here]
                u2 = dqt[hh * HD + half : (hh + 1) * HD, here]
                parts.append(u1 * cosine_t + u2 * sine_t)
                parts.append(u2 * cosine_t - u1 * sine_t)
            dq_ref[here, :] = jnp.concatenate(parts, axis=0).T.astype(BF16)
            return carry

        lax.fori_loop(0, count, finish, 0)


def attend_back(queries, keys, keys_t, mixed, out_grad, attended, sums, low, high, meta, cosine, sine, half_tables, share, carry, tile):
    width = queries.shape[1]
    heads = width // HD
    whole = lambda shape: pl.BlockSpec(shape, lambda i, meta: (0, 0))
    rows = lambda cols: pl.BlockSpec((tile, cols), lambda i, meta: (i, 0))
    table = cosine.shape[1]
    base = functools.partial(attend_back_kernel, tile, heads, share)
    if carry is None:
        kernel = lambda *refs: base(*refs[:14], None, *refs[14:])
        extra, specs = (), []
    else:
        kernel = base
        extra, specs = (carry,), [rows(width)]
    return pl.pallas_call(
        kernel,
        grid_spec=pltpu.PrefetchScalarGridSpec(
            num_scalar_prefetch=1,
            grid=(SLOTS // tile,),
            in_specs=[
                whole((SLOTS, width)),
                rows(width),
                pl.BlockSpec((width, tile), lambda i, meta: (0, i)),
                rows(width),
                whole((SLOTS, width)),
                whole((SLOTS, width)),
                whole((heads, SLOTS)),
                whole((1, SLOTS)),
                whole((1, SLOTS)),
                rows(table),
                rows(table),
                whole((HD // 2, SLOTS)),
                whole((HD // 2, SLOTS)),
            ]
            + specs,
            out_specs=[whole((SLOTS, width)), rows(width), rows(width)],
            scratch_shapes=[
                pltpu.VMEM((width, SLOTS), F32),
                pltpu.VMEM((tile, width), F32),
                pltpu.VMEM((tile, width), F32),
                pltpu.VMEM((8, SLOTS), F32),
            ],
        ),
        out_shape=[jax.ShapeDtypeStruct((SLOTS, width), BF16)] * 3,
        compiler_params=pltpu.CompilerParams(vmem_limit_bytes=VMEM_LIMIT),
        cost_estimate=lasting(36),
        name="attend_back",
    )(meta, queries, keys, keys_t, mixed, out_grad, attended, sums, low, high, cosine, sine, *half_tables, *extra)


class Place:
    def __init__(self):
        self.size = lax.axis_size("head")
        self.half = self.size // 2
        self.data = lax.axis_size("dp")
        self.core = lax.axis_index("section")
        self.dp = lax.axis_index("dp")
        self.head = lax.axis_index("head")
        self.row = self.head // self.half
        self.seat = self.head % self.half
        self.region = (self.row + self.core) % 2

    def swap(self, x):
        return lax.ppermute(x, "section", [(0, 1), (1, 0)])

    def to_core(self, x, core):
        return lax.ppermute(x, "section", [(1 - core, core)])

    def across(self, x, core):
        size, half = self.size, self.half
        pairs = [(size + h, core * size + (h + half) % size) for h in range(size)]
        return lax.ppermute(x, ("section", "head"), pairs)

    def across_from_zero(self, x):
        size, half = self.size, self.half
        pairs = [(h, size + (h + half) % size) for h in range(size)]
        return lax.ppermute(x, ("section", "head"), pairs)

    def beside(self, x, shift):
        half = self.half
        pairs = [(h, h // half * half + (h % half + shift) % half) for h in range(self.size)]
        return lax.ppermute(x, "head", pairs)

    def around(self, x, shift):
        return lax.ppermute(x, "head", [(h, (h + shift) % self.size) for h in range(self.size)])

    def flip(self, x, bits):
        return lax.ppermute(x, "dp", [(d, d ^ bits) for d in range(self.data)])

    def by_seat(self, own, shifted):
        blocks = jnp.zeros((self.half, *own.shape), own.dtype)
        blocks = lax.dynamic_update_index_in_dim(blocks, own, self.seat, 0)
        for shift, block in enumerate(shifted, 1):
            seat = (self.seat - shift) % self.half
            blocks = lax.dynamic_update_index_in_dim(blocks, block, seat, 0)
        return blocks

    def by_region(self, own, other):
        return jnp.where(
            self.region == 0, jnp.concatenate([own, other]), jnp.concatenate([other, own])
        )

    def gather_row(self, block):
        shifted = [self.beside(block, shift) for shift in range(1, self.half)]
        own = self.by_seat(block, shifted).reshape(-1, block.shape[1])
        return self.by_region(own, self.swap(own))

    def regions(self, rows):
        pair = rows.reshape(2, rows.shape[0] // 2, *rows.shape[1:])
        own = lax.dynamic_index_in_dim(pair, self.region, 0, keepdims=False)
        other = lax.dynamic_index_in_dim(pair, 1 - self.region, 0, keepdims=False)
        return own, other

    def seat_block(self, blocks, shift):
        return lax.dynamic_index_in_dim(blocks, (self.seat + shift) % self.half, 0, keepdims=False)

    def scatter_row(self, partial, tied):
        own, other = self.regions(partial)
        summed = own + self.swap(other.astype(BF16)).astype(F32)
        summed = tied(summed.reshape(self.half, -1, partial.shape[1]))
        total = self.seat_block(summed, 0)
        for shift in range(1, self.half):
            sent = self.seat_block(summed, shift).astype(BF16)
            total = total + self.beside(sent, shift).astype(F32)
        return total

    def heads_to_slots(self, rows):
        own, other = self.regions(rows)
        pair = jnp.stack([own, self.swap(other)])
        pair = pair.reshape(2, self.half, -1, rows.shape[1]).swapaxes(0, 1)
        shifted = [
            self.beside(self.seat_block(pair, shift), shift) for shift in range(1, self.half)
        ]
        blocks = self.by_seat(self.seat_block(pair, 0), shifted)
        blocks = self.by_region(blocks[:, 0], blocks[:, 1])
        return jnp.concatenate([blocks[i] for i in range(self.size)], axis=1)

    def slots_to_heads(self, block):
        width = block.shape[1] // self.size
        cut = jnp.stack([block[:, i * width : (i + 1) * width] for i in range(self.size)])
        own, other = self.regions(cut)
        pair = jnp.stack([own, other], axis=1)
        shifted = [
            self.beside(self.seat_block(pair, shift), shift) for shift in range(1, self.half)
        ]
        rows = self.by_seat(self.seat_block(pair, 0), shifted)
        return self.by_region(
            rows[:, 0].reshape(-1, width), self.swap(rows[:, 1].reshape(-1, width))
        )

    def data_block(self, x, bits):
        return lax.dynamic_index_in_dim(x, self.dp ^ bits, 0, keepdims=False)

    def by_data(self, own, flipped):
        blocks = jnp.zeros((self.data, *own.shape), own.dtype)
        blocks = lax.dynamic_update_index_in_dim(blocks, own, self.dp, 0)
        for bits, block in enumerate(flipped, 1):
            blocks = lax.dynamic_update_index_in_dim(blocks, block, self.dp ^ bits, 0)
        return blocks

    def gather_data(self, x):
        return self.by_data(x, [self.flip(x, bits) for bits in range(1, self.data)])

    def head_block(self, x, shift):
        return lax.dynamic_index_in_dim(x, (self.head + shift) % self.size, 0, keepdims=False)

    def scatter_heads(self, x):
        total = self.head_block(x, 0).astype(F32)
        for shift in range(1, self.size):
            sent = self.head_block(x, shift).astype(BF16)
            total = total + self.around(sent, shift).astype(F32)
        return total

    def spot(self):
        return jnp.stack([self.dp, self.head]).astype(jnp.int32)

    def by_core(self, own, other, axis):
        return jnp.where(
            self.core == 0, jnp.stack([own, other], axis), jnp.stack([other, own], axis)
        )

    def gather_cores(self, x):
        return self.by_core(x, self.swap(x), 0).reshape(-1, x.shape[1])

    def scatter_cores(self, partial):
        pair = partial.reshape(2, -1, partial.shape[1])
        own = lax.dynamic_index_in_dim(pair, self.core, 0, keepdims=False)
        other = lax.dynamic_index_in_dim(pair, 1 - self.core, 0, keepdims=False)
        return own + self.swap(other.astype(BF16)).astype(F32)

    def by_row(self, own, other):
        return jnp.where(
            self.row == 0, jnp.concatenate([own, other]), jnp.concatenate([other, own])
        )

    def pick(self, zero, one):
        return jnp.where(self.core == 0, zero, one)


class Chain:
    def __init__(self, stages):
        self.stages = stages
        self.result = None
        self.flight = next(stages)

    def advance(self, arrived):
        try:
            self.flight = self.stages.send(arrived)
        except StopIteration as stop:
            self.result = stop.value

    def step(self, x):
        x, arrived = lax.optimization_barrier((x, self.flight))
        self.advance(arrived)
        return x


def lockstep(*chains):
    while active := [chain for chain in chains if chain.result is None]:
        arrived = lax.optimization_barrier([chain.flight for chain in active])
        for chain, item in zip(active, arrived):
            chain.advance(item)
    return [chain.result for chain in chains]


def after(x, *others):
    return lax.optimization_barrier((x, *others))[0]


class Cut:
    def __init__(self, place, w_gate, w_out):
        self.heads = place.size
        self.units = w_gate.shape[2] // 2
        self.outs = w_out.shape[1] // 2
        self.rows = 3 * self.units + self.outs
        self.down = (self.rows // 2 - self.units - self.outs) // 16 * 16
        self.first = self.units + self.outs + self.down
        self.second = self.rows - self.first
        self.columns = D // place.data

    def part(self, share, place):
        return lax.dynamic_slice_in_dim(share, place.dp * self.columns, self.columns, 1)

    def pieces(self):
        units, outs, down = self.units, self.outs, self.down
        return (
            ("gate", 0, units, 0, 0),
            ("out", 0, outs, 0, units),
            ("down", 0, down, 0, units + outs),
            ("down", down, units - down, 1, 0),
            ("up", 0, units, 1, units - down),
        )


def pack_weights(place, w_gate, w_up, w_down, w_out):
    kinds = (w_gate.T, w_out, w_down, w_up.T)
    halves = [item.reshape(2, -1, D) for item in kinds]

    def half(core):
        return jnp.concatenate(
            [lax.dynamic_index_in_dim(item, core, 0, keepdims=False) for item in halves]
        )

    return half(place.core), half(1 - place.core)


def share_weights(place, cut, own, sent):
    piece = place.pick(cut.part(own, place), place.to_core(cut.part(sent, place), 1))
    other = place.swap(after(sent, piece))
    return place.pick(own, other), place.pick(other, own), piece


def any_specs(count):
    return [pl.BlockSpec(memory_space=pl.ANY)] * count


def run_copies(copies):
    for copy in copies:
        copy.start()
    for copy in copies:
        copy.wait()


def assemble_kernel(cut, groups, spot, share, *refs):
    dp, head = spot[0], spot[1]
    gu, down, out, sems = refs[5 * len(groups) :]
    kinds = {"gate": gu.at[0], "up": gu.at[1], "down": down, "out": out}
    copies = []

    def add(source, kind, step, row, count, columns):
        index = lax.rem(head - step + cut.heads, cut.heads) if kind == "out" else step
        target = kinds[kind].at[index, pl.ds(row, count), columns]
        copies.append(pltpu.make_async_copy(source, target, sems.at[len(copies)]))

    for kind, row, count, part, at in cut.pieces():
        base = at + part * cut.first
        add(share.at[pl.ds(base, count), :], kind, 0, row, count, slice(None))
    for number, steps in enumerate(groups):
        ring, first_x, second_y, first_y, second_x = refs[5 * number : 5 * number + 5]
        for i, step in enumerate(steps):
            firsts = (
                ring.at[i, pl.ds(0, cut.first)], first_x.at[i], first_y.at[0, i], first_y.at[1, i],
            )
            seconds = (
                ring.at[i, pl.ds(cut.first, cut.second)], second_x.at[0, i], second_y.at[i],
                second_x.at[1, i],
            )
            for bits in range(4):
                start = pl.multiple_of((dp ^ bits) * cut.columns, cut.columns)
                for kind, row, count, part, at in cut.pieces():
                    source = (firsts, seconds)[part][bits].at[pl.ds(at, count), :]
                    add(source, kind, step, row, count, pl.ds(start, cut.columns))
    run_copies(copies)


def near_flips(place, cut, ring):
    return place.flip(ring[:, : cut.first], 1), place.flip(ring[:, cut.first :], 2)


def far_flips(place, cut, ring, first_x, second_y):
    first = jnp.stack([ring[:, : cut.first], first_x])
    second = jnp.stack([ring[:, cut.first :], second_y])
    return place.flip(first, 2), place.flip(second, 1)


def fill_kernel(cut, spot, full, gu, down, out, sems):
    head = spot[1]
    kinds = {"gate": gu.at[0], "up": gu.at[1], "down": down, "out": out}
    copies = []
    for step in range(cut.heads):
        source = lax.rem(head - step + cut.heads, cut.heads)
        for part in range(D // cut.columns):
            columns = pl.ds(part * cut.columns, cut.columns)
            for kind, row, count, late, at in cut.pieces():
                index = source if kind == "out" else step
                block = full.at[part * cut.heads + source, pl.ds(at + late * cut.first, count), :]
                target = kinds[kind].at[index, pl.ds(row, count), columns]
                copies.append(pltpu.make_async_copy(block, target, sems.at[len(copies)]))
    run_copies(copies)


def spread_at_once(place, cut, piece):
    full = yield lax.all_gather(piece, ("dp", "head"), axis=0)
    return fill(place, cut, fill_kernel, 5 * place.data * cut.heads, (full,))


def spread_in_turn(place, cut, share, piece):
    size = cut.heads
    piece = yield place.around(piece, 1)
    ring_1 = piece[None]
    piece, near_1 = yield place.around(piece, 1), near_flips(place, cut, ring_1)
    ring = [piece]
    for _ in range(3, size):
        ring.append(place.around(ring[-1], 1))
    ring, far_1 = yield ring, far_flips(place, cut, ring_1, *near_1)
    ring = jnp.stack(ring)
    near = yield near_flips(place, cut, ring)
    far = yield far_flips(place, cut, ring, *near)
    groups = [([1], (ring_1, *near_1, *far_1)), (list(range(2, size)), (ring, *near, *far))]
    return assemble(place, cut, share, groups)


def first_qkv(place, w_qkv, part):
    flipped = yield [place.flip(part, bits) for bits in range(1, place.data)]
    return place.pick(w_qkv, place.by_data(part, flipped).reshape(w_qkv.shape))


def second_qkv(place, w_qkv):
    own, other = yield place.to_core(w_qkv, 0), place.across(w_qkv, 1)
    return place.pick(own, other)


def gather_far(place, far, gain):
    normed = norm(far.astype(F32), gain).astype(BF16)
    return (yield [place.beside(normed, shift) for shift in range(1, place.half)])


def assemble(place, cut, share, groups):
    steps = [group[0] for group in groups]
    parts = [part for group in groups for part in group[1]]
    kernel = lambda cut, *refs: assemble_kernel(cut, steps, *refs)
    return fill(place, cut, kernel, 5 * (1 + 4 * (cut.heads - 1)), (share, *parts))


def fill(place, cut, kernel, copies, sources):
    shape = lambda *dims: jax.ShapeDtypeStruct(dims, BF16)
    gate_up, down, out = pl.pallas_call(
        functools.partial(kernel, cut),
        in_specs=[pl.BlockSpec(memory_space=pltpu.SMEM)] + any_specs(len(sources)),
        out_specs=[pl.BlockSpec(memory_space=pltpu.VMEM)] * 3,
        out_shape=[
            shape(2, cut.heads, cut.units, D), shape(cut.heads, cut.units, D),
            shape(cut.heads, cut.outs, D),
        ],
        scratch_shapes=[pltpu.SemaphoreType.DMA((copies,))],
        compiler_params=pltpu.CompilerParams(vmem_limit_bytes=VMEM_LIMIT),
        cost_estimate=lasting(8),
        name="assemble",
    )(place.spot(), *sources)
    out = place.by_core(out, place.swap(out), 1).reshape(-1, D)
    return gate_up[0].reshape(-1, D), gate_up[1].reshape(-1, D), down.reshape(-1, D), out


def split_kernel(cut, chunks, spot, gate, up, down, out, *refs):
    dp, head = spot[0], spot[1]
    sems = refs[-1]
    kinds = {"gate": gate, "up": up, "down": down, "out": out}
    copies = []
    for number, steps in enumerate(chunks):
        first_kept, first_sent, second_kept, second_sent = refs[4 * number : 4 * number + 4]
        firsts = (first_kept.at[0], first_sent.at[0], first_kept.at[1], first_sent.at[1])
        seconds = (second_kept.at[0], second_kept.at[1], second_sent.at[0], second_sent.at[1])
        for bits in range(4):
            start = pl.multiple_of((dp ^ bits) * cut.columns, cut.columns)
            for i, step in enumerate(steps):
                for kind, row, count, part, at in cut.pieces():
                    index = step
                    if kind == "out":
                        index = lax.rem(head - step + cut.heads, cut.heads)
                    source = kinds[kind].at[index, pl.ds(row, count), pl.ds(start, cut.columns)]
                    target = (firsts, seconds)[part][bits].at[i, pl.ds(at, count), :]
                    copies.append(pltpu.make_async_copy(source, target, sems.at[len(copies)]))
    run_copies(copies)


def split_grads(place, cut, gate, up, down, out):
    half = cut.heads // 2
    chunks = [list(range(half, cut.heads)), list(range(half))]
    shape = lambda steps, rows: jax.ShapeDtypeStruct((2, len(steps), rows, cut.columns), BF16)
    shapes = []
    for steps in chunks:
        shapes += [shape(steps, cut.first)] * 2 + [shape(steps, cut.second)] * 2
    split = pl.pallas_call(
        functools.partial(split_kernel, cut, chunks),
        in_specs=[pl.BlockSpec(memory_space=pltpu.SMEM)]
        + [pl.BlockSpec(memory_space=pltpu.VMEM)] * 4,
        out_specs=any_specs(8),
        out_shape=shapes,
        scratch_shapes=[pltpu.SemaphoreType.DMA((20 * cut.heads,))],
        compiler_params=pltpu.CompilerParams(vmem_limit_bytes=VMEM_LIMIT),
        cost_estimate=lasting(8),
        name="split",
    )(place.spot(), *(item.reshape(cut.heads, -1, D) for item in (gate, up, down, out)))
    return split[:4], split[4:]


def exchange(place, part):
    first, second = yield place.flip(part[1], 1), place.flip(part[3], 2)
    first = part[0].astype(F32) + first.astype(F32)
    second = part[2].astype(F32) + second.astype(F32)
    moved = yield place.flip(first[1].astype(BF16), 2), place.flip(second[1].astype(BF16), 1)
    kept = first[0], second[0]
    return jnp.concatenate([x + y.astype(F32) for x, y in zip(kept, moved)], axis=1)


def reduce_far(place, cut, part):
    half = cut.heads // 2
    blocks = yield from exchange(place, part)
    moved = [
        place.around(blocks[step - half].astype(BF16), -step) for step in range(half, cut.heads)
    ]
    arrived = [(yield moved[0])]
    arrived += yield moved[1:]
    return sum(item.astype(F32) for item in arrived)


def reduce_near(place, cut, part, far):
    blocks = yield from exchange(place, part)
    total = blocks[0]
    if cut.heads > 2:
        arrived = yield [
            place.around(blocks[step].astype(BF16), -step) for step in range(1, cut.heads // 2)
        ]
        total = total + sum(item.astype(F32) for item in arrived)
    total = (total + far.result).astype(BF16)
    flipped = yield [place.flip(total, bits) for bits in range(1, place.data - 1)]
    total, across = yield total, place.flip(total, place.data - 1)
    parts = place.by_data(total, [*flipped, across])
    return jnp.concatenate([parts[d] for d in range(place.data)], axis=1)


def reduce_qkv(place, grad, core, second_layer):
    grad = grad.reshape(place.data, 2, -1, grad.shape[1])
    first, second = grad[:, 0], grad[:, 1]
    sent = [
        jnp.stack([place.data_block(x, bits) for bits in pair])
        for x, pair in ((first, (1, 3)), (second, (2, 3)))
    ]
    kept = [
        jnp.stack([place.data_block(x, bits) for bits in pair])
        for x, pair in ((first, (0, 2)), (second, (0, 1)))
    ]
    arrived = yield place.flip(sent[0], 1), place.flip(sent[1], 2)
    first, second = (a.astype(F32) + b.astype(F32) for a, b in zip(kept, arrived))
    arrived = yield place.flip(first[1].astype(BF16), 2), place.flip(second[1].astype(BF16), 1)
    piece = jnp.concatenate([first[0] + arrived[0].astype(F32), second[0] + arrived[1].astype(F32)])
    piece = piece.astype(BF16)
    if core == 0:
        other = yield place.across(piece, 0)
        first = (piece.astype(F32) + other.astype(F32)).astype(BF16)
        summed = place.pick(first, second_layer())
        flipped = yield [place.flip(summed, bits) for bits in range(1, place.data)]
        return place.by_data(summed, flipped).astype(F32).reshape(D, -1)
    own, other = yield place.to_core(piece, 1), place.across(piece, 1)
    return (own.astype(F32) + other.astype(F32)).astype(BF16)


def norm(rows, gain):
    inverse = lax.rsqrt(jnp.mean(rows * rows, axis=1, keepdims=True) + EPSILON)
    return rows * inverse * gain


def norm_back(rows, gain, grad):
    inverse = lax.rsqrt(jnp.mean(rows * rows, axis=1, keepdims=True) + EPSILON)
    scaled = grad * gain
    gain_grad = jnp.sum(grad * rows * inverse, axis=0)
    rows_grad = inverse * scaled - rows * inverse**3 * jnp.mean(
        scaled * rows, axis=1, keepdims=True
    )
    return rows_grad, gain_grad


def layer_forward(place, rows, gathered, first_values, w_qkv, chain, gains, tables, later=()):
    cosine, sine, half_tables, low, high, meta, tile = tables
    if later:
        gathered = chain.step(chain.step(gathered))
    later = [Chain(begin(gathered)) for begin in later]
    queries, keys, own_values, mixed = project(gathered, w_qkv, cosine, sine, first_values)
    queries = chain.step(queries)
    attended_heads, sums = attend(queries, keys, mixed, low, high, meta, tile)
    for other in (chain, *later[1:]) if later else ():
        attended_heads = other.step(attended_heads)
    attended = place.heads_to_slots(attended_heads)
    keys_t = keys.T
    gate_w, up_w, down_w, out_w = spread = chain.result
    middle = rows + dot_nn(attended, out_w)
    ffn_normed = place.gather_cores(norm(middle, gains[1]).astype(BF16))
    gate = dot_nt(ffn_normed, gate_w)
    up = dot_nt(ffn_normed, up_w)
    activation = (jax.nn.silu(gate) * up).astype(BF16)
    result = middle + place.scatter_cores(dot_nn(activation, down_w))
    kept = (
        rows, gathered, queries, keys, keys_t, mixed, attended_heads, sums, attended, middle,
        ffn_normed, gate, up, activation,
    )
    return result, own_values, spread, kept, later


def join_halves(place, x, shifted):
    own = place.by_seat(x, shifted)
    return place.by_core(own, place.swap(own), 1).reshape(-1, x.shape[1])


def layer_backward(place, cut, grad, share, carry, w_qkv, spread, gains, kept, tables, layer, earlier, second_layer=None):
    cosine, sine, half_tables, low, high, meta, tile = tables
    gate_w, up_w, down_w, out_w = spread
    (
        rows, gathered, queries, keys, keys_t, mixed, attended_heads, sums, attended, middle,
        ffn_normed, gate, up, activation,
    ) = kept
    down_grad = place.gather_cores(grad.astype(BF16))
    act_grad = dot_nt(down_grad, down_w)
    sigma = jax.nn.sigmoid(gate)
    gate_grad = (act_grad * up * sigma * (1.0 + gate * (1.0 - sigma))).astype(BF16)
    up_grad = (act_grad * gate * sigma).astype(BF16)
    for other in earlier[0]:
        up_grad = other.step(up_grad)
    normed_grad = place.scatter_cores(dot_nn(gate_grad, gate_w) + dot_nn(up_grad, up_w))
    middle_back, grad_ffn_gain = norm_back(middle, gains[1], normed_grad)
    middle_grad = grad + middle_back
    attn_grad = middle_grad.astype(BF16)
    attended_grad = dot_nt(attn_grad, out_w).astype(BF16)
    heads_grad = place.slots_to_heads(attended_grad)
    gate_grad, up_grad, activation = after((gate_grad, up_grad, activation), attended_grad)
    out_grad = dot_tn(attended, attn_grad).reshape(place.size, 2, -1, D).swapaxes(0, 1)
    out_grad = place.scatter_cores(out_grad.reshape(-1, D))
    split = split_grads(
        place, cut, dot_tn(gate_grad, ffn_normed).astype(BF16),
        dot_tn(up_grad, ffn_normed).astype(BF16), dot_tn(activation, down_grad).astype(BF16),
        out_grad.astype(BF16),
    )
    heads_grad = after(heads_grad, *split[0], *split[1])
    for other in earlier[1]:
        heads_grad = other.step(heads_grad)
    far = Chain(reduce_far(place, cut, split[0]))
    near = Chain(reduce_near(place, cut, split[1], far))
    query_grad, key_grad, value_grad = attend_back(
        queries, keys, keys_t, mixed, heads_grad, attended_heads, sums, low, high, meta, cosine, sine, half_tables,
        share, carry, tile,
    )
    for other in (far, near, *earlier[2]):
        query_grad = other.step(query_grad)
    lin_grad = jnp.concatenate([query_grad, key_grad, value_grad], axis=1)
    partial = dot_nt(lin_grad, w_qkv)
    qkv_grad = dot_tn(gathered, after(lin_grad, partial)).astype(BF16)
    qkv_grad = Chain(reduce_qkv(place, qkv_grad, layer, second_layer))
    input_back = place.scatter_row(partial, lambda x: qkv_grad.step(far.step(x)))
    for other in (near, qkv_grad, far):
        input_back = other.step(input_back)
    rows_back, grad_attn_gain = norm_back(rows, gains[0], input_back)
    return middle_grad + rows_back, value_grad, (far, near), qkv_grad, (grad_attn_gain, grad_ffn_gain)


def local(
    hidden_in, lengths, w_query, w_key, w_value, w_out, w_gate, w_up, w_down, attn_gain, ffn_gain,
    cotangent,
):
    place = Place()
    width = w_query.shape[2]
    cut = Cut(place, w_gate, w_out)
    tile = min(512, SLOTS)

    def mine_and_sent(x):
        mine = lax.dynamic_index_in_dim(x, place.row, 0, keepdims=False)
        sent = lax.dynamic_index_in_dim(x, 1 - place.row, 0, keepdims=False)
        return mine, sent

    count = hidden_in.shape[1] // 2
    mine, sent = mine_and_sent(hidden_in)
    half_block = lambda x: lax.dynamic_slice_in_dim(x, place.core * count, count, 0)
    far = place.around(half_block(sent), place.half)
    w_qkv = jnp.concatenate([w_query[0], w_key[0], w_value[0]], axis=1)
    part = lax.dynamic_slice_in_dim(w_qkv, place.dp * cut.columns, cut.columns, 0)
    part_1 = place.across_from_zero(part)
    own_packed, sent_packed = pack_weights(place, w_gate[0], w_up[0], w_down[0], w_out[0])
    own_gains = jnp.concatenate([attn_gain, ffn_gain])
    other_gains = place.swap(own_gains)
    gains_1 = place.pick(own_gains, other_gains)
    gains_2 = place.pick(other_gains, own_gains)

    begin, last, cosine, sine = slot_tables(
        lax.dynamic_index_in_dim(lengths, place.row, 0, keepdims=False)
    )
    repeat = min(128, width) // HD
    half_tables = (cosine[:, HD // 2 :].T, sine[:, HD // 2 :].T)
    tables = (
        jnp.tile(cosine, (1, repeat)), jnp.tile(sine, (1, repeat)), half_tables,
        begin[None], last[None], tile_tables(begin, tile), tile,
    )

    near = norm(half_block(mine).astype(F32), gains_1[0]).astype(BF16)
    near_shifted = [place.beside(near, shift) for shift in range(1, place.half)]
    far, part_1, own_packed, sent_packed = lax.optimization_barrier(
        (far, part_1, own_packed, sent_packed)
    )
    share_1, share_2, piece_1 = share_weights(place, cut, own_packed, sent_packed)
    piece_2 = cut.part(share_2, place)
    chain_far = Chain(gather_far(place, far, gains_1[0]))
    chain_1 = Chain(spread_in_turn(place, cut, share_1, piece_1))
    chain_qkv = Chain(first_qkv(place, w_qkv, part_1))
    started = (chain_far, chain_qkv, chain_1)
    arrived = lax.optimization_barrier([chain.flight for chain in started])
    for chain, item in zip(started, arrived):
        chain.advance(item)
    far_shifted, w_qkv_1 = chain_far.result, chain_qkv.result
    blocks = [
        join_halves(place, near, near_shifted),
        join_halves(place, norm(far.astype(F32), gains_1[0]).astype(BF16), far_shifted),
    ]
    gathered = place.by_row(*blocks)
    rows = place.pick(mine, place.by_core(far, place.swap(far), 0).reshape(mine.shape))
    rows = rows.astype(F32)
    result_1, values_1, spread_1, kept_1, (chain_2, chain_qkv) = layer_forward(
        place, rows, gathered, None, w_qkv_1, chain_1, gains_1, tables,
        (
            lambda x: spread_at_once(place, cut, after(piece_2, x)),
            lambda x: second_qkv(place, after(w_qkv, x)),
        ),
    )
    hidden_1 = result_1.astype(BF16)
    rows = hidden_1.astype(F32)
    gathered = place.gather_row(norm(rows, gains_2[0]).astype(BF16))
    w_qkv_2 = chain_qkv.result
    result_2, _, spread_2, kept_2, _ = layer_forward(
        place, rows, gathered, values_1, w_qkv_2, chain_2, gains_2, tables
    )
    hidden_2 = result_2.astype(BF16)

    def bring(first, second):
        near = place.to_core(second.astype(BF16), 1)
        near, *far = yield near, place.across(first.astype(BF16), 0), place.across(second.astype(BF16), 1)
        return near, place.pick(*far)

    outputs = Chain(bring(hidden_1, hidden_2))
    mine, sent = mine_and_sent(cotangent)
    grad = place.pick(mine, place.across(sent.astype(BF16), 1).astype(F32))
    grad_2, carry, ffn_2, qkv_2, gain_2 = layer_backward(
        place, cut, grad, 0.5, None, w_qkv_2, spread_2, gains_2, kept_2, tables, 1,
        ((), (), (outputs,)),
    )
    grad_2 = grad_2.astype(BF16)
    far_2, near_2 = ffn_2

    def bring_one(block, core, wait=0):
        for _ in range(wait):
            block = yield block
        moved = (place.across(block.astype(BF16), core),)
        moved = yield moved if core == 0 else (*moved, place.to_core(block.astype(BF16), 1))
        return moved

    def both_rows(near, far):
        return jnp.where(place.row == 0, jnp.stack([near, far]), jnp.stack([far, near]))[None]

    grads_2 = Chain(bring_one(grad_2, 1))
    grad_1, _, (far_1, near_1), qkv_1, gain_1 = layer_backward(
        place, cut, grad_2.astype(F32), 1.0, carry, w_qkv_1, spread_1, gains_1, kept_1, tables, 0,
        ((far_2, near_2, qkv_2), (near_2, grads_2), ()), lambda: qkv_2.result,
    )

    def sum_gains(gains):
        gains = gains + (yield place.swap(gains))
        gains = gains + sum((yield [place.flip(gains, bits) for bits in range(1, place.data)]))
        return gains + sum((yield [place.around(gains, k) for k in range(1, place.size)]))

    grads_1 = Chain(bring_one(grad_1, 0, 1))
    gains = Chain(sum_gains(jnp.stack([*gain_1, *gain_2])))
    _, ffn_1, ffn_2, qkv_1, gains, grads_1 = lockstep(
        far_1, near_1, near_2, qkv_1, gains, grads_1
    )

    grads_2 = grads_2.result
    near, far = outputs.result
    layer_outputs = both_rows(place.pick(hidden_1, near), far)
    near = place.pick(grad_1, grads_2[1].astype(F32))
    input_grads = both_rows(near, place.pick(grads_1[0], grads_2[0]).astype(F32))

    own = place.pick(ffn_1, ffn_2)
    other = place.swap(place.pick(ffn_2, ffn_1))
    ffn = place.by_core(own, other, 0).astype(F32)
    units, outs = cut.units, cut.outs
    grad_gate = ffn[:, :units].reshape(-1, D).T
    grad_out = ffn[:, units : units + outs].reshape(-1, D)
    grad_down = ffn[:, units + outs : 2 * units + outs].reshape(-1, D)
    grad_up = ffn[:, 2 * units + outs :].reshape(-1, D).T
    gains = place.pick(gains[:2], gains[2:])
    return (
        layer_outputs, input_grads, *(qkv_1[None, :, i * width : (i + 1) * width] for i in range(3)), grad_out[None],
        grad_gate[None], grad_up[None], grad_down[None], gains[:1], gains[1:],
    )


def solution(mesh):
    in_specs = (
        P("dp", "head", None),
        P("dp", None),
        P("section", None, "head"),
        P("section", None, "head"),
        P("section", None, "head"),
        P("section", "head", None),
        P("section", None, "head"),
        P("section", None, "head"),
        P("section", "head", None),
        P("section", None),
        P("section", None),
        P("dp", "head", None),
    )
    out_specs = (
        P("section", "dp", "head", None),
        P("section", "dp", "head", None),
        P("section", None, "head"),
        P("section", None, "head"),
        P("section", None, "head"),
        P("section", "head", None),
        P("section", None, "head"),
        P("section", None, "head"),
        P("section", "head", None),
        P("section", None),
        P("section", None),
    )
    return jax.shard_map(local, mesh=mesh, in_specs=in_specs, out_specs=out_specs, check_vma=False)
```

```python
import functools

import jax
import jax.numpy as jnp
from jax import lax
from jax.experimental import pallas as pl
from jax.experimental.pallas import tpu as pltpu
from jax.sharding import PartitionSpec as P

D = 1024
HD = 64
SLOTS = 2048
PAD = 128

EPSILON = 1e-05
MASKED = -1e30
SCALE = HD ** (-0.5)
VMEM_LIMIT = 56 * 1024 * 1024


def lasting(microseconds):
    return pl.CostEstimate(flops=microseconds * 10**9, bytes_accessed=1, transcendentals=0)


F32 = jnp.float32
BF16 = jnp.bfloat16


def dot_nn(a, b):
    return lax.dot_general(a, b, (((1,), (0,)), ((), ())), preferred_element_type=F32)


def dot_nt(a, b):
    return lax.dot_general(a, b, (((1,), (1,)), ((), ())), preferred_element_type=F32)


def dot_tn(a, b):
    return lax.dot_general(a, b, (((0,), (0,)), ((), ())), preferred_element_type=F32)


def slot_tables(length_row):
    padded = (length_row + PAD - 1) // PAD * PAD
    starts = jnp.cumsum(padded) - padded
    slots = jnp.arange(SLOTS, dtype=jnp.int32)
    inside = (slots[:, None] >= starts[None, :]) & (slots[:, None] < (starts + padded)[None, :])
    begin = jnp.sum(jnp.where(inside, starts[None, :], 0), axis=1).astype(jnp.int32)
    end = jnp.sum(jnp.where(inside, (starts + length_row)[None, :], 0), axis=1).astype(jnp.int32)
    last = jnp.minimum(slots, end - 1)
    freq = 10000.0 ** (-2.0 * jnp.arange(HD // 2, dtype=F32) / HD)
    angle = (slots - begin).astype(F32)[:, None] * freq[None, :]
    cosine = jnp.concatenate([jnp.cos(angle), jnp.cos(angle)], axis=1)
    sine = jnp.concatenate([-jnp.sin(angle), jnp.sin(angle)], axis=1)
    return begin, last, cosine, sine


def tile_tables(begin, tile):
    count = SLOTS // tile
    index = jnp.arange(count, dtype=jnp.int32)
    low = begin[::tile]
    high = begin[tile - 1 :: tile]
    first = low // tile
    free = jnp.minimum((high + tile - 1) // tile, index)
    later = index[None, :] > index[:, None]
    free_end = index + 1 + jnp.sum(
        jnp.where(later & (high[None, :] <= index[:, None] * tile), 1, 0), axis=1
    )
    seen_end = index + 1 + jnp.sum(
        jnp.where(later & (low[None, :] < (index[:, None] + 1) * tile), 1, 0), axis=1
    )
    return jnp.stack([first, free, free_end.astype(jnp.int32), seen_end.astype(jnp.int32)])


def lane_in_head(shape):
    return lax.broadcasted_iota(jnp.int32, shape, 1) % HD


def turn(rows, cosine, sine):
    width = rows.shape[1]
    low = lane_in_head(rows.shape) < HD // 2
    if width == HD:
        swapped = jnp.concatenate([rows[:, HD // 2 :], rows[:, : HD // 2]], axis=1)
    else:
        swapped = jnp.where(
            low,
            pltpu.roll(rows, width - HD // 2, 1),
            pltpu.roll(rows, HD // 2, 1),
        )
    return rows * cosine + swapped * sine


def qkv_kernel(width, x_ref, w_ref, cos_ref, sin_ref, first_ref, q_ref, k_ref, v_ref, m_ref):
    product = dot_nn(x_ref[...], w_ref[...])
    repeat = width // cos_ref.shape[1]
    cosine = jnp.concatenate([cos_ref[...]] * repeat, axis=1)
    sine = jnp.concatenate([sin_ref[...]] * repeat, axis=1)
    q_ref[...] = (turn(product[:, :width], cosine, sine).astype(BF16).astype(F32) * SCALE).astype(BF16)
    k_ref[...] = turn(product[:, width : 2 * width], cosine, sine).astype(BF16)
    own = product[:, 2 * width :].astype(BF16)
    v_ref[...] = own
    if first_ref is not None:
        m_ref[...] = (0.5 * own.astype(F32) + 0.5 * first_ref[...].astype(F32)).astype(BF16)


def project(gathered, w_qkv, cosine, sine, first_values):
    width = w_qkv.shape[1] // 3
    tile = min(1024, SLOTS)
    table = cosine.shape[1]
    row = lambda cols: pl.BlockSpec((tile, cols), lambda i: (i, 0))
    shape = jax.ShapeDtypeStruct((SLOTS, width), BF16)
    if first_values is None:
        kernel = lambda x, w, c, s, q, k, v: qkv_kernel(width, x, w, c, s, None, q, k, v, None)
        extra, specs, outs = (), [], 3
    else:
        kernel = functools.partial(qkv_kernel, width)
        extra, specs, outs = (first_values,), [row(width)], 4
    result = pl.pallas_call(
        kernel,
        grid=(SLOTS // tile,),
        in_specs=[
            row(D),
            pl.BlockSpec((D, 3 * width), lambda i: (0, 0)),
            row(table),
            row(table),
        ]
        + specs,
        out_specs=[row(width)] * outs,
        out_shape=[shape] * outs,
        compiler_params=pltpu.CompilerParams(vmem_limit_bytes=VMEM_LIMIT),
        cost_estimate=lasting(10),
        name="project",
    )(gathered, w_qkv, cosine, sine, *extra)
    return result if first_values is not None else (*result, result[2])


def head_mask(rows, width, head):
    lanes = lax.broadcasted_iota(jnp.int32, (rows, width), 1)
    return (lanes >= head * HD) & (lanes < (head + 1) * HD)


def attend_kernel(tile, heads, meta, q_ref, k_ref, vt_ref, low_ref, high_ref, o_ref, lse_ref, acc, peak, mass):
    width = heads * HD
    index = pl.program_id(0)
    q = q_ref[...]
    low = low_ref[...]
    high = high_ref[...]
    queries = [jnp.where(head_mask(tile, width, hh), q, jnp.zeros_like(q)) for hh in range(heads)]
    acc[...] = jnp.zeros_like(acc)
    peak[...] = jnp.full_like(peak, MASKED)
    mass[...] = jnp.zeros_like(mass)

    def step(kt, masked):
        start = pl.multiple_of(kt * tile, tile)
        keys = k_ref[pl.ds(start, tile), :]
        every = range(heads)
        rows = [slice(hh * HD, (hh + 1) * HD) for hh in every]
        scores = [dot_nt(keys, queries[hh]) for hh in every]
        if masked:
            slots = start + lax.broadcasted_iota(jnp.int32, scores[0].shape, 0)
            allowed = (slots >= low) & (slots <= high)
            scores = [jnp.where(allowed, x, MASKED) for x in scores]
        before = [peak[hh : hh + 1, :] for hh in every]
        tops = [jnp.maximum(before[hh], jnp.max(scores[hh], axis=0, keepdims=True)) for hh in every]
        weights = [jnp.exp(scores[hh] - tops[hh]) for hh in every]
        shrink = [jnp.exp(before[hh] - tops[hh]) for hh in every]
        sums = [
            mass[hh : hh + 1, :] * shrink[hh] + jnp.sum(weights[hh], axis=0, keepdims=True)
            for hh in every
        ]
        updates = [
            acc[rows[hh], :] * shrink[hh]
            + dot_nn(vt_ref[rows[hh], pl.ds(start, tile)], weights[hh].astype(BF16))
            for hh in every
        ]
        for hh in every:
            peak[hh : hh + 1, :] = tops[hh]
            mass[hh : hh + 1, :] = sums[hh]
            acc[rows[hh], :] = updates[hh]

    step(index, True)

    def masked_step(kt, carry):
        step(kt, True)
        return carry

    def free_step(kt, carry):
        step(kt, False)
        return carry

    lax.fori_loop(meta[0, index], meta[1, index], masked_step, 0)
    lax.fori_loop(meta[1, index], index, free_step, 0)
    for hh in range(heads):
        rows = slice(hh * HD, (hh + 1) * HD)
        acc[rows, :] = acc[rows, :] / mass[hh : hh + 1, :]
    o_ref[...] = acc[...].T.astype(BF16)
    lse_ref[...] = peak[...] + jnp.log(mass[...])


def attend(queries, keys, mixed, low, high, meta, tile):
    width = queries.shape[1]
    heads = width // HD
    whole = lambda shape: pl.BlockSpec(shape, lambda i, meta: (0, 0))
    return pl.pallas_call(
        functools.partial(attend_kernel, tile, heads),
        grid_spec=pltpu.PrefetchScalarGridSpec(
            num_scalar_prefetch=1,
            grid=(SLOTS // tile,),
            in_specs=[
                pl.BlockSpec((tile, width), lambda i, meta: (i, 0)),
                whole((SLOTS, width)),
                whole((width, SLOTS)),
                pl.BlockSpec((1, tile), lambda i, meta: (0, i)),
                pl.BlockSpec((1, tile), lambda i, meta: (0, i)),
            ],
            out_specs=[
                pl.BlockSpec((tile, width), lambda i, meta: (i, 0)),
                pl.BlockSpec((heads, tile), lambda i, meta: (0, i)),
            ],
            scratch_shapes=[
                pltpu.VMEM((width, tile), F32),
                pltpu.VMEM((heads, tile), F32),
                pltpu.VMEM((heads, tile), F32),
            ],
        ),
        out_shape=[
            jax.ShapeDtypeStruct((SLOTS, width), BF16),
            jax.ShapeDtypeStruct((heads, SLOTS), F32),
        ],
        compiler_params=pltpu.CompilerParams(vmem_limit_bytes=VMEM_LIMIT),
        cost_estimate=lasting(25),
        name="attend",
    )(meta, queries, keys, mixed.T, low, high)


def attend_back_kernel(
    tile, heads, share, meta, q_ref, k_ref, kt_ref, v_ref, do_ref, o_ref, lse_ref, low_ref, high_ref,
    cos_ref, sin_ref, cost_ref, sint_ref, carry_ref, dq_ref, dk_ref, dv_ref, dqt, dk, dv, delta_ref
):
    width = heads * HD
    index = pl.program_id(0)
    count = pl.num_programs(0)

    @pl.when(index == 0)
    def _():
        dqt[...] = jnp.zeros_like(dqt)
        lanes = lax.broadcasted_iota(jnp.int32, (delta_ref.shape[0], width), 1)
        owner = lax.broadcasted_iota(jnp.int32, (delta_ref.shape[0], width), 0)
        select = jnp.where(
            (lanes >= owner * HD) & (lanes < (owner + 1) * HD), 1.0, 0.0
        ).astype(F32)

        def row_sums(qt, carry):
            here = pl.ds(pl.multiple_of(qt * tile, tile), tile)
            product = do_ref[here, :].astype(F32) * o_ref[here, :].astype(F32)
            delta_ref[:, here] = lax.dot_general(
                select, product, (((1,), (1,)), ((), ())), precision=lax.Precision.HIGHEST,
                preferred_element_type=F32,
            )
            return carry

        lax.fori_loop(0, count, row_sums, 0)

    dk[...] = jnp.zeros_like(dk)
    dv[...] = jnp.zeros_like(dv)
    keys = k_ref[...]
    values = v_ref[...]
    key_start = index * tile
    masks = [head_mask(tile, width, hh) for hh in range(heads)]
    transposed = [kt_ref[hh * HD : (hh + 1) * HD, :] for hh in range(heads)]

    def step(qt, masked):
        start = pl.multiple_of(qt * tile, tile)
        here = pl.ds(start, tile)
        q = q_ref[here, :]
        do = do_ref[here, :]
        low = low_ref[:, here]
        high = high_ref[:, here]
        every = range(heads)
        rows = [slice(hh * HD, (hh + 1) * HD) for hh in every]
        q_h = [jnp.where(masks[hh], q, jnp.zeros_like(q)) for hh in every]
        do_h = [jnp.where(masks[hh], do, jnp.zeros_like(do)) for hh in every]
        scores = [dot_nt(keys, q_h[hh]) for hh in every]
        prob_grad = [dot_nt(values, do_h[hh]) for hh in every]
        if masked:
            slots = key_start + lax.broadcasted_iota(jnp.int32, scores[0].shape, 0)
            allowed = (slots >= low) & (slots <= high)
            scores = [jnp.where(allowed, x, MASKED) for x in scores]
        probs = [jnp.exp(scores[hh] - lse_ref[hh : hh + 1, here]) for hh in every]
        score_grad = [
            (probs[hh] * (prob_grad[hh] - delta_ref[hh : hh + 1, here])).astype(BF16)
            for hh in every
        ]
        dv[...] += sum(dot_nn(probs[hh].astype(BF16), do_h[hh]) for hh in every)
        dk[...] += sum(dot_nn(score_grad[hh], q_h[hh]) for hh in every)
        updates = [dqt[rows[hh], here] + dot_nn(transposed[hh], score_grad[hh]) for hh in every]
        for hh in every:
            dqt[rows[hh], here] = updates[hh]

    step(index, True)

    def masked_step(qt, carry):
        step(qt, True)
        return carry

    def free_step(qt, carry):
        step(qt, False)
        return carry

    lax.fori_loop(index + 1, meta[2, index], free_step, 0)
    lax.fori_loop(meta[2, index], meta[3, index], masked_step, 0)
    repeat = width // cos_ref.shape[1]
    cosine = jnp.concatenate([cos_ref[...]] * repeat, axis=1)
    sine = jnp.concatenate([sin_ref[...]] * repeat, axis=1)
    dk_ref[...] = turn(dk[...], cosine, -sine).astype(BF16)
    if carry_ref is None:
        dv_ref[...] = (share * dv[...]).astype(BF16)
    else:
        dv_ref[...] = (share * dv[...] + carry_ref[...].astype(F32)).astype(BF16)

    @pl.when(index == count - 1)
    def _():
        half = HD // 2

        def finish(qt, carry):
            here = pl.ds(pl.multiple_of(qt * tile, tile), tile)
            cosine_t = cost_ref[:, here] * SCALE
            sine_t = sint_ref[:, here] * SCALE
            parts = []
            for hh in range(heads):
                u1 = dqt[hh * HD : hh * HD + half, here]
                u2 = dqt[hh * HD + half : (hh + 1) * HD, here]
                parts.append(u1 * cosine_t + u2 * sine_t)
                parts.append(u2 * cosine_t - u1 * sine_t)
            dq_ref[here, :] = jnp.concatenate(parts, axis=0).T.astype(BF16)
            return carry

        lax.fori_loop(0, count, finish, 0)


def attend_back(queries, keys, keys_t, mixed, out_grad, attended, sums, low, high, meta, cosine, sine, half_tables, share, carry, tile):
    width = queries.shape[1]
    heads = width // HD
    whole = lambda shape: pl.BlockSpec(shape, lambda i, meta: (0, 0))
    rows = lambda cols: pl.BlockSpec((tile, cols), lambda i, meta: (i, 0))
    table = cosine.shape[1]
    base = functools.partial(attend_back_kernel, tile, heads, share)
    if carry is None:
        kernel = lambda *refs: base(*refs[:14], None, *refs[14:])
        extra, specs = (), []
    else:
        kernel = base
        extra, specs = (carry,), [rows(width)]
    return pl.pallas_call(
        kernel,
        grid_spec=pltpu.PrefetchScalarGridSpec(
            num_scalar_prefetch=1,
            grid=(SLOTS // tile,),
            in_specs=[
                whole((SLOTS, width)),
                rows(width),
                pl.BlockSpec((width, tile), lambda i, meta: (0, i)),
                rows(width),
                whole((SLOTS, width)),
                whole((SLOTS, width)),
                whole((heads, SLOTS)),
                whole((1, SLOTS)),
                whole((1, SLOTS)),
                rows(table),
                rows(table),
                whole((HD // 2, SLOTS)),
                whole((HD // 2, SLOTS)),
            ]
            + specs,
            out_specs=[whole((SLOTS, width)), rows(width), rows(width)],
            scratch_shapes=[
                pltpu.VMEM((width, SLOTS), F32),
                pltpu.VMEM((tile, width), F32),
                pltpu.VMEM((tile, width), F32),
                pltpu.VMEM((8, SLOTS), F32),
            ],
        ),
        out_shape=[jax.ShapeDtypeStruct((SLOTS, width), BF16)] * 3,
        compiler_params=pltpu.CompilerParams(vmem_limit_bytes=VMEM_LIMIT),
        cost_estimate=lasting(36),
        name="attend_back",
    )(meta, queries, keys, keys_t, mixed, out_grad, attended, sums, low, high, cosine, sine, *half_tables, *extra)


class Place:
    def __init__(self):
        self.size = lax.axis_size("head")
        self.half = self.size // 2
        self.data = lax.axis_size("dp")
        self.core = lax.axis_index("section")
        self.dp = lax.axis_index("dp")
        self.head = lax.axis_index("head")
        self.row = self.head // self.half
        self.seat = self.head % self.half
        self.region = (self.row + self.core) % 2

    def swap(self, x):
        return lax.ppermute(x, "section", [(0, 1), (1, 0)])

    def to_core(self, x, core):
        return lax.ppermute(x, "section", [(1 - core, core)])

    def across(self, x, core):
        size, half = self.size, self.half
        pairs = [(size + h, core * size + (h + half) % size) for h in range(size)]
        return lax.ppermute(x, ("section", "head"), pairs)

    def across_from_zero(self, x):
        size, half = self.size, self.half
        pairs = [(h, size + (h + half) % size) for h in range(size)]
        return lax.ppermute(x, ("section", "head"), pairs)

    def beside(self, x, shift):
        half = self.half
        pairs = [(h, h // half * half + (h % half + shift) % half) for h in range(self.size)]
        return lax.ppermute(x, "head", pairs)

    def around(self, x, shift):
        return lax.ppermute(x, "head", [(h, (h + shift) % self.size) for h in range(self.size)])

    def flip(self, x, bits):
        return lax.ppermute(x, "dp", [(d, d ^ bits) for d in range(self.data)])

    def by_seat(self, own, shifted):
        blocks = jnp.zeros((self.half, *own.shape), own.dtype)
        blocks = lax.dynamic_update_index_in_dim(blocks, own, self.seat, 0)
        for shift, block in enumerate(shifted, 1):
            seat = (self.seat - shift) % self.half
            blocks = lax.dynamic_update_index_in_dim(blocks, block, seat, 0)
        return blocks

    def by_region(self, own, other):
        return jnp.where(
            self.region == 0, jnp.concatenate([own, other]), jnp.concatenate([other, own])
        )

    def gather_row(self, block):
        shifted = [self.beside(block, shift) for shift in range(1, self.half)]
        own = self.by_seat(block, shifted).reshape(-1, block.shape[1])
        return self.by_region(own, self.swap(own))

    def regions(self, rows):
        pair = rows.reshape(2, rows.shape[0] // 2, *rows.shape[1:])
        own = lax.dynamic_index_in_dim(pair, self.region, 0, keepdims=False)
        other = lax.dynamic_index_in_dim(pair, 1 - self.region, 0, keepdims=False)
        return own, other

    def seat_block(self, blocks, shift):
        return lax.dynamic_index_in_dim(blocks, (self.seat + shift) % self.half, 0, keepdims=False)

    def scatter_row(self, partial, tied):
        own, other = self.regions(partial)
        summed = own + self.swap(other.astype(BF16)).astype(F32)
        summed = tied(summed.reshape(self.half, -1, partial.shape[1]))
        total = self.seat_block(summed, 0)
        for shift in range(1, self.half):
            sent = self.seat_block(summed, shift).astype(BF16)
            total = total + self.beside(sent, shift).astype(F32)
        return total

    def heads_to_slots(self, rows):
        own, other = self.regions(rows)
        pair = jnp.stack([own, self.swap(other)])
        pair = pair.reshape(2, self.half, -1, rows.shape[1]).swapaxes(0, 1)
        shifted = [
            self.beside(self.seat_block(pair, shift), shift) for shift in range(1, self.half)
        ]
        blocks = self.by_seat(self.seat_block(pair, 0), shifted)
        blocks = self.by_region(blocks[:, 0], blocks[:, 1])
        return jnp.concatenate([blocks[i] for i in range(self.size)], axis=1)

    def slots_to_heads(self, block):
        width = block.shape[1] // self.size
        cut = jnp.stack([block[:, i * width : (i + 1) * width] for i in range(self.size)])
        own, other = self.regions(cut)
        pair = jnp.stack([own, other], axis=1)
        shifted = [
            self.beside(self.seat_block(pair, shift), shift) for shift in range(1, self.half)
        ]
        rows = self.by_seat(self.seat_block(pair, 0), shifted)
        return self.by_region(
            rows[:, 0].reshape(-1, width), self.swap(rows[:, 1].reshape(-1, width))
        )

    def data_block(self, x, bits):
        return lax.dynamic_index_in_dim(x, self.dp ^ bits, 0, keepdims=False)

    def by_data(self, own, flipped):
        blocks = jnp.zeros((self.data, *own.shape), own.dtype)
        blocks = lax.dynamic_update_index_in_dim(blocks, own, self.dp, 0)
        for bits, block in enumerate(flipped, 1):
            blocks = lax.dynamic_update_index_in_dim(blocks, block, self.dp ^ bits, 0)
        return blocks

    def gather_data(self, x):
        return self.by_data(x, [self.flip(x, bits) for bits in range(1, self.data)])

    def head_block(self, x, shift):
        return lax.dynamic_index_in_dim(x, (self.head + shift) % self.size, 0, keepdims=False)

    def scatter_heads(self, x):
        total = self.head_block(x, 0).astype(F32)
        for shift in range(1, self.size):
            sent = self.head_block(x, shift).astype(BF16)
            total = total + self.around(sent, shift).astype(F32)
        return total

    def spot(self):
        return jnp.stack([self.dp, self.head]).astype(jnp.int32)

    def by_core(self, own, other, axis):
        return jnp.where(
            self.core == 0, jnp.stack([own, other], axis), jnp.stack([other, own], axis)
        )

    def gather_cores(self, x):
        return self.by_core(x, self.swap(x), 0).reshape(-1, x.shape[1])

    def scatter_cores(self, partial):
        pair = partial.reshape(2, -1, partial.shape[1])
        own = lax.dynamic_index_in_dim(pair, self.core, 0, keepdims=False)
        other = lax.dynamic_index_in_dim(pair, 1 - self.core, 0, keepdims=False)
        return own + self.swap(other.astype(BF16)).astype(F32)

    def by_row(self, own, other):
        return jnp.where(
            self.row == 0, jnp.concatenate([own, other]), jnp.concatenate([other, own])
        )

    def pick(self, zero, one):
        return jnp.where(self.core == 0, zero, one)


class Chain:
    def __init__(self, stages):
        self.stages = stages
        self.result = None
        self.flight = next(stages)

    def advance(self, arrived):
        try:
            self.flight = self.stages.send(arrived)
        except StopIteration as stop:
            self.result = stop.value

    def step(self, x):
        x, arrived = lax.optimization_barrier((x, self.flight))
        self.advance(arrived)
        return x


def lockstep(*chains):
    while active := [chain for chain in chains if chain.result is None]:
        arrived = lax.optimization_barrier([chain.flight for chain in active])
        for chain, item in zip(active, arrived):
            chain.advance(item)
    return [chain.result for chain in chains]


def after(x, *others):
    return lax.optimization_barrier((x, *others))[0]


class Cut:
    def __init__(self, place, w_gate, w_out):
        self.heads = place.size
        self.units = w_gate.shape[2] // 2
        self.outs = w_out.shape[1] // 2
        self.rows = 3 * self.units + self.outs
        self.down = (self.rows // 2 - self.units - self.outs) // 16 * 16
        self.first = self.units + self.outs + self.down
        self.second = self.rows - self.first
        self.columns = D // place.data

    def part(self, share, place):
        return lax.dynamic_slice_in_dim(share, place.dp * self.columns, self.columns, 1)

    def pieces(self):
        units, outs, down = self.units, self.outs, self.down
        return (
            ("gate", 0, units, 0, 0),
            ("out", 0, outs, 0, units),
            ("down", 0, down, 0, units + outs),
            ("down", down, units - down, 1, 0),
            ("up", 0, units, 1, units - down),
        )


def pack_weights(place, w_gate, w_up, w_down, w_out):
    kinds = (w_gate.T, w_out, w_down, w_up.T)
    halves = [item.reshape(2, -1, D) for item in kinds]

    def half(core):
        return jnp.concatenate(
            [lax.dynamic_index_in_dim(item, core, 0, keepdims=False) for item in halves]
        )

    return half(place.core), half(1 - place.core)


def share_weights(place, cut, own, sent):
    piece = place.pick(cut.part(own, place), place.to_core(cut.part(sent, place), 1))
    other = place.swap(after(sent, piece))
    return place.pick(own, other), place.pick(other, own), piece


def any_specs(count):
    return [pl.BlockSpec(memory_space=pl.ANY)] * count


def run_copies(copies):
    for copy in copies:
        copy.start()
    for copy in copies:
        copy.wait()


def assemble_kernel(cut, groups, spot, share, *refs):
    dp, head = spot[0], spot[1]
    gu, down, out, sems = refs[5 * len(groups) :]
    kinds = {"gate": gu.at[0], "up": gu.at[1], "down": down, "out": out}
    copies = []

    def add(source, kind, step, row, count, columns):
        index = lax.rem(head - step + cut.heads, cut.heads) if kind == "out" else step
        target = kinds[kind].at[index, pl.ds(row, count), columns]
        copies.append(pltpu.make_async_copy(source, target, sems.at[len(copies)]))

    for kind, row, count, part, at in cut.pieces():
        base = at + part * cut.first
        add(share.at[pl.ds(base, count), :], kind, 0, row, count, slice(None))
    for number, steps in enumerate(groups):
        ring, first_x, second_y, first_y, second_x = refs[5 * number : 5 * number + 5]
        for i, step in enumerate(steps):
            firsts = (
                ring.at[i, pl.ds(0, cut.first)], first_x.at[i], first_y.at[0, i], first_y.at[1, i],
            )
            seconds = (
                ring.at[i, pl.ds(cut.first, cut.second)], second_x.at[0, i], second_y.at[i],
                second_x.at[1, i],
            )
            for bits in range(4):
                start = pl.multiple_of((dp ^ bits) * cut.columns, cut.columns)
                for kind, row, count, part, at in cut.pieces():
                    source = (firsts, seconds)[part][bits].at[pl.ds(at, count), :]
                    add(source, kind, step, row, count, pl.ds(start, cut.columns))
    run_copies(copies)


def near_flips(place, cut, ring):
    return place.flip(ring[:, : cut.first], 1), place.flip(ring[:, cut.first :], 2)


def far_flips(place, cut, ring, first_x, second_y):
    first = jnp.stack([ring[:, : cut.first], first_x])
    second = jnp.stack([ring[:, cut.first :], second_y])
    return place.flip(first, 2), place.flip(second, 1)


def fill_kernel(cut, spot, full, gu, down, out, sems):
    head = spot[1]
    kinds = {"gate": gu.at[0], "up": gu.at[1], "down": down, "out": out}
    copies = []
    for step in range(cut.heads):
        source = lax.rem(head - step + cut.heads, cut.heads)
        for part in range(D // cut.columns):
            columns = pl.ds(part * cut.columns, cut.columns)
            for kind, row, count, late, at in cut.pieces():
                index = source if kind == "out" else step
                block = full.at[part * cut.heads + source, pl.ds(at + late * cut.first, count), :]
                target = kinds[kind].at[index, pl.ds(row, count), columns]
                copies.append(pltpu.make_async_copy(block, target, sems.at[len(copies)]))
    run_copies(copies)


def spread_at_once(place, cut, piece):
    full = yield lax.all_gather(piece, ("dp", "head"), axis=0)
    return fill(place, cut, fill_kernel, 5 * place.data * cut.heads, (full,))


def spread_in_turn(place, cut, share, piece):
    size = cut.heads
    piece = yield place.around(piece, 1)
    ring_1 = piece[None]
    piece, near_1 = yield place.around(piece, 1), near_flips(place, cut, ring_1)
    ring = [piece]
    for _ in range(3, size):
        ring.append(place.around(ring[-1], 1))
    ring, far_1 = yield ring, far_flips(place, cut, ring_1, *near_1)
    ring = jnp.stack(ring)
    near = yield near_flips(place, cut, ring)
    far = yield far_flips(place, cut, ring, *near)
    groups = [([1], (ring_1, *near_1, *far_1)), (list(range(2, size)), (ring, *near, *far))]
    return assemble(place, cut, share, groups)


def first_qkv(place, w_qkv, part):
    flipped = yield [place.flip(part, bits) for bits in range(1, place.data)]
    return place.pick(w_qkv, place.by_data(part, flipped).reshape(w_qkv.shape))


def second_qkv(place, w_qkv):
    own, other = yield place.to_core(w_qkv, 0), place.across(w_qkv, 1)
    return place.pick(own, other)


def gather_far(place, far, gain):
    normed = norm(far.astype(F32), gain).astype(BF16)
    return (yield [place.beside(normed, shift) for shift in range(1, place.half)])


def assemble(place, cut, share, groups):
    steps = [group[0] for group in groups]
    parts = [part for group in groups for part in group[1]]
    kernel = lambda cut, *refs: assemble_kernel(cut, steps, *refs)
    return fill(place, cut, kernel, 5 * (1 + 4 * (cut.heads - 1)), (share, *parts))


def fill(place, cut, kernel, copies, sources):
    shape = lambda *dims: jax.ShapeDtypeStruct(dims, BF16)
    gate_up, down, out = pl.pallas_call(
        functools.partial(kernel, cut),
        in_specs=[pl.BlockSpec(memory_space=pltpu.SMEM)] + any_specs(len(sources)),
        out_specs=[pl.BlockSpec(memory_space=pltpu.VMEM)] * 3,
        out_shape=[
            shape(2, cut.heads, cut.units, D), shape(cut.heads, cut.units, D),
            shape(cut.heads, cut.outs, D),
        ],
        scratch_shapes=[pltpu.SemaphoreType.DMA((copies,))],
        compiler_params=pltpu.CompilerParams(vmem_limit_bytes=VMEM_LIMIT),
        cost_estimate=lasting(8),
        name="assemble",
    )(place.spot(), *sources)
    out = place.by_core(out, place.swap(out), 1).reshape(-1, D)
    return gate_up[0].reshape(-1, D), gate_up[1].reshape(-1, D), down.reshape(-1, D), out


def split_kernel(cut, chunks, spot, gate, up, down, out, *refs):
    dp, head = spot[0], spot[1]
    sems = refs[-1]
    kinds = {"gate": gate, "up": up, "down": down, "out": out}
    copies = []
    for number, steps in enumerate(chunks):
        first_kept, first_sent, second_kept, second_sent = refs[4 * number : 4 * number + 4]
        firsts = (first_kept.at[0], first_sent.at[0], first_kept.at[1], first_sent.at[1])
        seconds = (second_kept.at[0], second_kept.at[1], second_sent.at[0], second_sent.at[1])
        for bits in range(4):
            start = pl.multiple_of((dp ^ bits) * cut.columns, cut.columns)
            for i, step in enumerate(steps):
                for kind, row, count, part, at in cut.pieces():
                    index = step
                    if kind == "out":
                        index = lax.rem(head - step + cut.heads, cut.heads)
                    source = kinds[kind].at[index, pl.ds(row, count), pl.ds(start, cut.columns)]
                    target = (firsts, seconds)[part][bits].at[i, pl.ds(at, count), :]
                    copies.append(pltpu.make_async_copy(source, target, sems.at[len(copies)]))
    run_copies(copies)


def split_grads(place, cut, gate, up, down, out):
    half = cut.heads // 2
    chunks = [list(range(half, cut.heads)), list(range(half))]
    shape = lambda steps, rows: jax.ShapeDtypeStruct((2, len(steps), rows, cut.columns), BF16)
    shapes = []
    for steps in chunks:
        shapes += [shape(steps, cut.first)] * 2 + [shape(steps, cut.second)] * 2
    split = pl.pallas_call(
        functools.partial(split_kernel, cut, chunks),
        in_specs=[pl.BlockSpec(memory_space=pltpu.SMEM)]
        + [pl.BlockSpec(memory_space=pltpu.VMEM)] * 4,
        out_specs=any_specs(8),
        out_shape=shapes,
        scratch_shapes=[pltpu.SemaphoreType.DMA((20 * cut.heads,))],
        compiler_params=pltpu.CompilerParams(vmem_limit_bytes=VMEM_LIMIT),
        cost_estimate=lasting(8),
        name="split",
    )(place.spot(), *(item.reshape(cut.heads, -1, D) for item in (gate, up, down, out)))
    return split[:4], split[4:]


def exchange(place, part):
    first, second = yield place.flip(part[1], 1), place.flip(part[3], 2)
    first = part[0].astype(F32) + first.astype(F32)
    second = part[2].astype(F32) + second.astype(F32)
    moved = yield place.flip(first[1].astype(BF16), 2), place.flip(second[1].astype(BF16), 1)
    kept = first[0], second[0]
    return jnp.concatenate([x + y.astype(F32) for x, y in zip(kept, moved)], axis=1)


def reduce_far(place, cut, part):
    half = cut.heads // 2
    blocks = yield from exchange(place, part)
    moved = [
        place.around(blocks[step - half].astype(BF16), -step) for step in range(half, cut.heads)
    ]
    arrived = [(yield moved[0])]
    arrived += yield moved[1:]
    return sum(item.astype(F32) for item in arrived)


def reduce_near(place, cut, part, far):
    blocks = yield from exchange(place, part)
    total = blocks[0]
    if cut.heads > 2:
        arrived = yield [
            place.around(blocks[step].astype(BF16), -step) for step in range(1, cut.heads // 2)
        ]
        total = total + sum(item.astype(F32) for item in arrived)
    total = (total + far.result).astype(BF16)
    flipped = yield [place.flip(total, bits) for bits in range(1, place.data - 1)]
    total, across = yield total, place.flip(total, place.data - 1)
    parts = place.by_data(total, [*flipped, across])
    return jnp.concatenate([parts[d] for d in range(place.data)], axis=1)


def reduce_qkv(place, grad, core, second_layer):
    grad = grad.reshape(place.data, 2, -1, grad.shape[1])
    first, second = grad[:, 0], grad[:, 1]
    sent = [
        jnp.stack([place.data_block(x, bits) for bits in pair])
        for x, pair in ((first, (1, 3)), (second, (2, 3)))
    ]
    kept = [
        jnp.stack([place.data_block(x, bits) for bits in pair])
        for x, pair in ((first, (0, 2)), (second, (0, 1)))
    ]
    arrived = yield place.flip(sent[0], 1), place.flip(sent[1], 2)
    first, second = (a.astype(F32) + b.astype(F32) for a, b in zip(kept, arrived))
    arrived = yield place.flip(first[1].astype(BF16), 2), place.flip(second[1].astype(BF16), 1)
    piece = jnp.concatenate([first[0] + arrived[0].astype(F32), second[0] + arrived[1].astype(F32)])
    piece = piece.astype(BF16)
    if core == 0:
        other = yield place.across(piece, 0)
        first = (piece.astype(F32) + other.astype(F32)).astype(BF16)
        summed = place.pick(first, second_layer())
        flipped = yield [place.flip(summed, bits) for bits in range(1, place.data)]
        return place.by_data(summed, flipped).astype(F32).reshape(D, -1)
    own, other = yield place.to_core(piece, 1), place.across(piece, 1)
    return (own.astype(F32) + other.astype(F32)).astype(BF16)


def norm(rows, gain):
    inverse = lax.rsqrt(jnp.mean(rows * rows, axis=1, keepdims=True) + EPSILON)
    return rows * inverse * gain


def norm_back(rows, gain, grad):
    inverse = lax.rsqrt(jnp.mean(rows * rows, axis=1, keepdims=True) + EPSILON)
    scaled = grad * gain
    gain_grad = jnp.sum(grad * rows * inverse, axis=0)
    rows_grad = inverse * scaled - rows * inverse**3 * jnp.mean(
        scaled * rows, axis=1, keepdims=True
    )
    return rows_grad, gain_grad


def layer_forward(place, rows, gathered, first_values, w_qkv, chain, gains, tables, later=()):
    cosine, sine, half_tables, low, high, meta, tile = tables
    if later:
        gathered = chain.step(chain.step(gathered))
    later = [Chain(begin(gathered)) for begin in later]
    queries, keys, own_values, mixed = project(gathered, w_qkv, cosine, sine, first_values)
    queries = chain.step(queries)
    attended_heads, sums = attend(queries, keys, mixed, low, high, meta, tile)
    for other in (chain, *later[1:]) if later else ():
        attended_heads = other.step(attended_heads)
    attended = place.heads_to_slots(attended_heads)
    keys_t = keys.T
    gate_w, up_w, down_w, out_w = spread = chain.result
    middle = rows + dot_nn(attended, out_w)
    ffn_normed = place.gather_cores(norm(middle, gains[1]).astype(BF16))
    gate = dot_nt(ffn_normed, gate_w)
    up = dot_nt(ffn_normed, up_w)
    activation = (jax.nn.silu(gate) * up).astype(BF16)
    result = middle + place.scatter_cores(dot_nn(activation, down_w))
    kept = (
        rows, gathered, queries, keys, keys_t, mixed, attended_heads, sums, attended, middle,
        ffn_normed, gate, up, activation,
    )
    return result, own_values, spread, kept, later


def join_halves(place, x, shifted):
    own = place.by_seat(x, shifted)
    return place.by_core(own, place.swap(own), 1).reshape(-1, x.shape[1])


def layer_backward(place, cut, grad, share, carry, w_qkv, spread, gains, kept, tables, layer, earlier, second_layer=None):
    cosine, sine, half_tables, low, high, meta, tile = tables
    gate_w, up_w, down_w, out_w = spread
    (
        rows, gathered, queries, keys, keys_t, mixed, attended_heads, sums, attended, middle,
        ffn_normed, gate, up, activation,
    ) = kept
    down_grad = place.gather_cores(grad.astype(BF16))
    act_grad = dot_nt(down_grad, down_w)
    sigma = jax.nn.sigmoid(gate)
    gate_grad = (act_grad * up * sigma * (1.0 + gate * (1.0 - sigma))).astype(BF16)
    up_grad = (act_grad * gate * sigma).astype(BF16)
    for other in earlier[0]:
        up_grad = other.step(up_grad)
    normed_grad = place.scatter_cores(dot_nn(gate_grad, gate_w) + dot_nn(up_grad, up_w))
    middle_back, grad_ffn_gain = norm_back(middle, gains[1], normed_grad)
    middle_grad = grad + middle_back
    attn_grad = middle_grad.astype(BF16)
    attended_grad = dot_nt(attn_grad, out_w).astype(BF16)
    heads_grad = place.slots_to_heads(attended_grad)
    gate_grad, up_grad, activation = after((gate_grad, up_grad, activation), attended_grad)
    out_grad = dot_tn(attended, attn_grad).reshape(place.size, 2, -1, D).swapaxes(0, 1)
    out_grad = place.scatter_cores(out_grad.reshape(-1, D))
    split = split_grads(
        place, cut, dot_tn(gate_grad, ffn_normed).astype(BF16),
        dot_tn(up_grad, ffn_normed).astype(BF16), dot_tn(activation, down_grad).astype(BF16),
        out_grad.astype(BF16),
    )
    heads_grad = after(heads_grad, *split[0], *split[1])
    for other in earlier[1]:
        heads_grad = other.step(heads_grad)
    far = Chain(reduce_far(place, cut, split[0]))
    near = Chain(reduce_near(place, cut, split[1], far))
    query_grad, key_grad, value_grad = attend_back(
        queries, keys, keys_t, mixed, heads_grad, attended_heads, sums, low, high, meta, cosine, sine, half_tables,
        share, carry, tile,
    )
    for other in (far, near, *earlier[2]):
        query_grad = other.step(query_grad)
    lin_grad = jnp.concatenate([query_grad, key_grad, value_grad], axis=1)
    partial = dot_nt(lin_grad, w_qkv)
    qkv_grad = dot_tn(gathered, after(lin_grad, partial)).astype(BF16)
    qkv_grad = Chain(reduce_qkv(place, qkv_grad, layer, second_layer))
    input_back = place.scatter_row(partial, lambda x: qkv_grad.step(far.step(x)))
    for other in (near, qkv_grad, far):
        input_back = other.step(input_back)
    rows_back, grad_attn_gain = norm_back(rows, gains[0], input_back)
    return middle_grad + rows_back, value_grad, (far, near), qkv_grad, (grad_attn_gain, grad_ffn_gain)


def local(
    hidden_in, lengths, w_query, w_key, w_value, w_out, w_gate, w_up, w_down, attn_gain, ffn_gain,
    cotangent,
):
    place = Place()
    width = w_query.shape[2]
    cut = Cut(place, w_gate, w_out)
    tile = min(512, SLOTS)

    def mine_and_sent(x):
        mine = lax.dynamic_index_in_dim(x, place.row, 0, keepdims=False)
        sent = lax.dynamic_index_in_dim(x, 1 - place.row, 0, keepdims=False)
        return mine, sent

    count = hidden_in.shape[1] // 2
    mine, sent = mine_and_sent(hidden_in)
    half_block = lambda x: lax.dynamic_slice_in_dim(x, place.core * count, count, 0)
    far = place.around(half_block(sent), place.half)
    w_qkv = jnp.concatenate([w_query[0], w_key[0], w_value[0]], axis=1)
    part = lax.dynamic_slice_in_dim(w_qkv, place.dp * cut.columns, cut.columns, 0)
    part_1 = place.across_from_zero(part)
    own_packed, sent_packed = pack_weights(place, w_gate[0], w_up[0], w_down[0], w_out[0])
    own_gains = jnp.concatenate([attn_gain, ffn_gain])
    other_gains = place.swap(own_gains)
    gains_1 = place.pick(own_gains, other_gains)
    gains_2 = place.pick(other_gains, own_gains)

    begin, last, cosine, sine = slot_tables(
        lax.dynamic_index_in_dim(lengths, place.row, 0, keepdims=False)
    )
    repeat = min(128, width) // HD
    half_tables = (cosine[:, HD // 2 :].T, sine[:, HD // 2 :].T)
    tables = (
        jnp.tile(cosine, (1, repeat)), jnp.tile(sine, (1, repeat)), half_tables,
        begin[None], last[None], tile_tables(begin, tile), tile,
    )

    near = norm(half_block(mine).astype(F32), gains_1[0]).astype(BF16)
    near_shifted = [place.beside(near, shift) for shift in range(1, place.half)]
    far, part_1, own_packed, sent_packed = lax.optimization_barrier(
        (far, part_1, own_packed, sent_packed)
    )
    share_1, share_2, piece_1 = share_weights(place, cut, own_packed, sent_packed)
    piece_2 = cut.part(share_2, place)
    chain_far = Chain(gather_far(place, far, gains_1[0]))
    chain_1 = Chain(spread_in_turn(place, cut, share_1, piece_1))
    chain_qkv = Chain(first_qkv(place, w_qkv, part_1))
    started = (chain_far, chain_qkv, chain_1)
    arrived = lax.optimization_barrier([chain.flight for chain in started])
    for chain, item in zip(started, arrived):
        chain.advance(item)
    far_shifted, w_qkv_1 = chain_far.result, chain_qkv.result
    blocks = [
        join_halves(place, near, near_shifted),
        join_halves(place, norm(far.astype(F32), gains_1[0]).astype(BF16), far_shifted),
    ]
    gathered = place.by_row(*blocks)
    rows = place.pick(mine, place.by_core(far, place.swap(far), 0).reshape(mine.shape))
    rows = rows.astype(F32)
    result_1, values_1, spread_1, kept_1, (chain_2, chain_qkv) = layer_forward(
        place, rows, gathered, None, w_qkv_1, chain_1, gains_1, tables,
        (
            lambda x: spread_at_once(place, cut, after(piece_2, x)),
            lambda x: second_qkv(place, after(w_qkv, x)),
        ),
    )
    hidden_1 = result_1.astype(BF16)
    rows = hidden_1.astype(F32)
    gathered = place.gather_row(norm(rows, gains_2[0]).astype(BF16))
    w_qkv_2 = chain_qkv.result
    result_2, _, spread_2, kept_2, _ = layer_forward(
        place, rows, gathered, values_1, w_qkv_2, chain_2, gains_2, tables
    )
    hidden_2 = result_2.astype(BF16)

    def bring(first, second):
        near = place.to_core(second.astype(BF16), 1)
        near, *far = yield near, place.across(first.astype(BF16), 0), place.across(second.astype(BF16), 1)
        return near, place.pick(*far)

    outputs = Chain(bring(hidden_1, hidden_2))
    mine, sent = mine_and_sent(cotangent)
    grad = place.pick(mine, place.across(sent.astype(BF16), 1).astype(F32))
    grad_2, carry, ffn_2, qkv_2, gain_2 = layer_backward(
        place, cut, grad, 0.5, None, w_qkv_2, spread_2, gains_2, kept_2, tables, 1,
        ((), (), (outputs,)),
    )
    grad_2 = grad_2.astype(BF16)
    far_2, near_2 = ffn_2

    def bring_one(block, core, wait=0):
        for _ in range(wait):
            block = yield block
        moved = (place.across(block.astype(BF16), core),)
        moved = yield moved if core == 0 else (*moved, place.to_core(block.astype(BF16), 1))
        return moved

    def both_rows(near, far):
        return jnp.where(place.row == 0, jnp.stack([near, far]), jnp.stack([far, near]))[None]

    grads_2 = Chain(bring_one(grad_2, 1))
    grad_1, _, (far_1, near_1), qkv_1, gain_1 = layer_backward(
        place, cut, grad_2.astype(F32), 1.0, carry, w_qkv_1, spread_1, gains_1, kept_1, tables, 0,
        ((far_2, near_2, qkv_2), (near_2, grads_2), ()), lambda: qkv_2.result,
    )

    def sum_gains(gains):
        gains = gains + (yield place.swap(gains))
        gains = gains + sum((yield [place.flip(gains, bits) for bits in range(1, place.data)]))
        return gains + sum((yield [place.around(gains, k) for k in range(1, place.size)]))

    grads_1 = Chain(bring_one(grad_1, 0, 1))
    gains = Chain(sum_gains(jnp.stack([*gain_1, *gain_2])))
    _, ffn_1, ffn_2, qkv_1, gains, grads_1 = lockstep(
        far_1, near_1, near_2, qkv_1, gains, grads_1
    )

    grads_2 = grads_2.result
    near, far = outputs.result
    layer_outputs = both_rows(place.pick(hidden_1, near), far)
    near = place.pick(grad_1, grads_2[1].astype(F32))
    input_grads = both_rows(near, place.pick(grads_1[0], grads_2[0]).astype(F32))

    own = place.pick(ffn_1, ffn_2)
    other = place.swap(place.pick(ffn_2, ffn_1))
    ffn = place.by_core(own, other, 0).astype(F32)
    units, outs = cut.units, cut.outs
    grad_gate = ffn[:, :units].reshape(-1, D).T
    grad_out = ffn[:, units : units + outs].reshape(-1, D)
    grad_down = ffn[:, units + outs : 2 * units + outs].reshape(-1, D)
    grad_up = ffn[:, 2 * units + outs :].reshape(-1, D).T
    gains = place.pick(gains[:2], gains[2:])
    return (
        layer_outputs, input_grads, *(qkv_1[None, :, i * width : (i + 1) * width] for i in range(3)), grad_out[None],
        grad_gate[None], grad_up[None], grad_down[None], gains[:1], gains[1:],
    )


def solution(mesh):
    in_specs = (
        P("dp", "head", None),
        P("dp", None),
        P("section", None, "head"),
        P("section", None, "head"),
        P("section", None, "head"),
        P("section", "head", None),
        P("section", None, "head"),
        P("section", None, "head"),
        P("section", "head", None),
        P("section", None),
        P("section", None),
        P("dp", "head", None),
    )
    out_specs = (
        P("section", "dp", "head", None),
        P("section", "dp", "head", None),
        P("section", None, "head"),
        P("section", None, "head"),
        P("section", None, "head"),
        P("section", "head", None),
        P("section", None, "head"),
        P("section", None, "head"),
        P("section", "head", None),
        P("section", None),
        P("section", None),
    )
    return jax.shard_map(local, mesh=mesh, in_specs=in_specs, out_specs=out_specs, check_vma=False)
```
